256 devices in a mesh: tm: 8 (over x, core), pair: 32 (over y, z).
Axes of the slice: x: 4, y: 4, z: 8, core: 2. Of those that a mesh axis runs over, the one named last changes fastest.
Arguments:
- coefs: bfloat16 [2048, 256, 2048], P('pair', None, 'tm'), may hold values from -0.8919053 to 0.8919053
- energies: bfloat16 [2048, 2048], P('pair', 'tm'), may hold values from 0.0195 to 16
- coulomb: bfloat16 [32, 32, 256, 256], P('pair', 'tm'), may hold values from -0.375 to 0.375
- tau_grid: float32 [3], replicated, may hold values from 0.0079 to 5.01
- freq_grid: float32 [3], replicated, may hold values from 0.2 to 5
- pairs: int32 [32, 32, 2], replicated, may hold values from -1 to 2047, as said below
Outputs:
- screened: bfloat16 [32, 32, 3, 256, 256], P('pair', 'tm')
- self_energy: float32 [2048, 2048], P('pair', 'tm')
The draws below stay inside these ranges and needn't reach their ends.
Inputs may be any that keep to these rules, and one draw needn't show every extreme that they name: Entry 0 of pairs[d,k] is a global block or -1, entry 1 a block index below 64 of device d, -1 exactly where entry 0 is -1. Padding forms the tail of each row and some row has none. No row names more than 2 blocks held by one index of pair, and some row names exactly 2.
All inputs are finite; a program needn't handle non-finite values.
Results may differ from the reference program's by a relative error of at most 0.02.
Values may be sent and summed in bfloat16 or wider, within the bound.
A program may use at most 128 MiB of HBM per device.

```python
import math
import jax
import jax.numpy as jnp
from jax import lax

A = 256
M = 2048
TAU = 3
BLK_DEV = 64
LIST = 32
SLOTS = 64
NBLK = 2048
N_TM = 8
N_PAIR = 32


def draw_coefs(key, part):
    key = jax.random.fold_in(key, 5)
    keys = jax.random.split(key, 1)
    scale = M ** (-0.25)
    values = jax.random.truncated_normal(keys[0], -6.0, 6.0, (NBLK, A, M), jnp.float32)
    return (values * scale).astype(jnp.bfloat16)


def draw_energies(key, part):
    key = jax.random.fold_in(key, 21)
    keys = jax.random.split(key, 2)
    band = jax.random.randint(keys[0], (NBLK, M), 0, 3)
    lower = jnp.where(band == 0, 0.02, jnp.where(band == 1, 0.6, 8.0)).astype(jnp.float32)
    upper = jnp.where(band == 0, 0.06, jnp.where(band == 1, 1.2, 16.0)).astype(jnp.float32)
    frac = jax.random.uniform(keys[1], (NBLK, M), jnp.float32, 0.0, 1.0)
    values = lower * jnp.exp(frac * jnp.log(upper / lower))
    values = jnp.clip(values, lower, upper)
    return values.astype(jnp.bfloat16)


def draw_tau_grid(key, part):
    key = jax.random.fold_in(key, 23)
    steps = jnp.arange(TAU, dtype=jnp.float32) / max(TAU - 1, 1)
    base = 0.01 * jnp.exp(steps * jnp.log(400.0))
    jitter = jnp.exp(jax.random.uniform(key, (TAU,), jnp.float32, jnp.log(0.8), jnp.log(1.25)))
    return (base * jitter).astype(jnp.float32)


def draw_coulomb(key, part):
    key = jax.random.fold_in(key, 9)
    scale = A ** (-0.5)
    values = jax.random.truncated_normal(key, -6.0, 6.0, (N_PAIR, LIST, A, A), jnp.float32)
    return (values * scale).astype(jnp.bfloat16)


def draw_pairs(key, part):
    capacity = SLOTS // N_PAIR
    token_count = N_PAIR * capacity
    keys = jax.random.split(jax.random.fold_in(key, 17), 6)
    tokens = jnp.arange(token_count, dtype=jnp.int32) // capacity
    heavy = jax.random.randint(keys[0], (N_PAIR,), 0, N_PAIR)
    spread = jnp.arange(token_count, dtype=jnp.int32)
    scores = jax.random.randint(keys[1], (N_PAIR, token_count), 0, 1 << 20) * token_count + spread[None, :]
    scores = jnp.where(tokens[None, :] == heavy[:, None], spread[None, :] - token_count, scores)
    order = jnp.argsort(scores, axis=1, stable=True)
    chosen = tokens[order][:, :LIST]
    shuffle_keys = jax.random.randint(keys[2], (N_PAIR, LIST), 0, 1 << 20) * LIST + jnp.arange(LIST, dtype=jnp.int32)[None, :]
    perm = jnp.argsort(shuffle_keys, axis=1, stable=True)
    chosen = jnp.take_along_axis(chosen, perm, axis=1)
    counts = jax.random.randint(keys[3], (N_PAIR,), LIST * 5 // 8, LIST + 1)
    full_row = jax.random.randint(keys[4], (), 0, N_PAIR)
    counts = jnp.where(jnp.arange(N_PAIR) == full_row, LIST, counts)
    alive = jnp.arange(LIST)[None, :] < counts[:, None]
    picks = jax.random.randint(keys[5], (N_PAIR, LIST, 2), 0, BLK_DEV)
    remote = jnp.where(alive, chosen * BLK_DEV + picks[:, :, 0], -1)
    local = jnp.where(alive, picks[:, :, 1], -1)
    return jnp.stack([remote, local], axis=2).astype(jnp.int32)


def setup_inputs(seed: int = 0) -> dict:
    splits = jax.random.split(jax.random.key(seed), 7)
    coefs = draw_coefs(jax.random.fold_in(splits[6], 71), 0)
    energies = draw_energies(jax.random.fold_in(splits[6], 71), 0)
    coulomb = draw_coulomb(jax.random.fold_in(splits[6], 71), 0)
    tau_grid = draw_tau_grid(jax.random.fold_in(splits[6], 71), 0)
    freq_grid = jnp.clip(jnp.exp(jax.random.uniform(splits[4], (TAU,), jnp.float32, math.log(0.2), math.log(5.0))), 0.2, 5.0)
    pairs = draw_pairs(jax.random.fold_in(splits[6], 71), 0)
    return dict(coefs=coefs, energies=energies, coulomb=coulomb, tau_grid=tau_grid, freq_grid=freq_grid, pairs=pairs)


def dress(coef_block, expo, tvalue):
    decay = jnp.exp(-tvalue * expo.astype(jnp.float32))
    return (coef_block.astype(jnp.float32) * decay[:, None, :]).astype(jnp.bfloat16)

def reference(coefs, energies, coulomb, tau_grid, freq_grid, pairs):
    nblocks = coefs.shape[0]
    slice_len = M // N_TM
    cosine = jnp.cos(freq_grid[:, None] * tau_grid[None, :])
    hi = lax.Precision.HIGHEST

    def one_row(device):
        row = pairs[device]
        remote = row[:, 0]
        local = row[:, 1]
        alive = remote >= 0
        keep = alive.astype(jnp.bfloat16)
        remote_idx = jnp.where(alive, remote, 0).astype(jnp.int32)
        local_idx = (device * BLK_DEV + jnp.where(alive, local, 0)).astype(jnp.int32)
        coef_g = coefs[remote_idx] * keep[:, None, None]
        coef_a = coefs[local_idx] * keep[:, None, None]
        ener_g = energies[remote_idx]
        ener_a = energies[local_idx]
        dressed_a = []
        dressed_g = []
        chi_list = []
        for tpoint in range(TAU):
            xa = dress(coef_a, ener_a, tau_grid[tpoint])
            yg = dress(coef_g, ener_g, tau_grid[tpoint])
            dressed_a.append(xa)
            dressed_g.append(yg)
            xs = xa.astype(jnp.float32).reshape(LIST, A, N_TM, slice_len)
            ys = yg.astype(jnp.float32).reshape(LIST, A, N_TM, slice_len)
            part = jnp.einsum('kpsm,kqsm->kspq', xs, ys).astype(jnp.bfloat16)
            part = lax.optimization_barrier(part)
            chi_list.append(lax.optimization_barrier(jnp.sum(part.astype(jnp.float32), axis=1)))
        chi = jnp.stack(chi_list, axis=1)
        chiw = jnp.einsum('wt,ktpq->kwpq', cosine, chi, precision=hi).astype(jnp.bfloat16)
        tile = coulomb[device].astype(jnp.float32)
        prod = jnp.einsum('kwpq,kqr->kwpr', chiw.astype(jnp.float32), tile)
        prod_b = prod.astype(jnp.bfloat16).astype(jnp.float32)
        wfreq = prod + jnp.einsum('kwpq,kwqr->kwpr', prod_b, prod_b) / math.sqrt(A)
        wtime = (jnp.einsum('wt,kwpq->ktpq', cosine, wfreq, precision=hi) / TAU).astype(jnp.bfloat16)
        total = jnp.zeros((LIST, M), jnp.float32)
        for tpoint in range(TAU):
            wy = jnp.einsum('kpq,kqm->kpm', wtime[:, tpoint].astype(jnp.float32), dressed_g[tpoint].astype(jnp.float32))
            total = total + lax.optimization_barrier(jnp.sum(dressed_a[tpoint].astype(jnp.float32) * wy, axis=1))
        return (wtime, total / TAU)
    screened, contrib = lax.map(one_row, jnp.arange(N_PAIR, dtype=jnp.int32))
    remote_all = pairs[:, :, 0].reshape(-1)
    seg_ids = jnp.where(remote_all >= 0, remote_all, nblocks).astype(jnp.int32)
    summed = jax.ops.segment_sum(contrib.reshape(-1, M), seg_ids, num_segments=nblocks + 1)
    return (screened, summed[:nblocks])
```

```python
import functools
import math

import jax
import jax.numpy as jnp
from jax import lax
from jax.experimental import pallas as pl
from jax.experimental.pallas import tpu as pltpu
from jax.sharding import PartitionSpec as P

CAP = 2
CHUNKS = 4
MESH = pl.DeviceIdType.MESH


def greet(n_tm, n_pair, my_tm, my_pair):
    barrier = pltpu.get_barrier_semaphore()

    def pair_peer(i, c):
        other = lax.rem(my_pair + i, n_pair)
        pl.semaphore_signal(barrier, inc=1, device_id=(my_tm, other), device_id_type=MESH)
        return c

    def tm_peer(i, c):
        other = lax.rem(my_tm + i, n_tm)
        pl.semaphore_signal(barrier, inc=1, device_id=(other, my_pair), device_id_type=MESH)
        return c

    lax.fori_loop(1, n_pair, pair_peer, 0)
    lax.fori_loop(1, n_tm, tm_peer, 0)
    pl.semaphore_wait(barrier, n_pair + n_tm - 2)


def wait_bytes(ref, sem):
    pltpu.make_async_copy(ref, ref, sem).wait()


def gather_kernel(
    n_tm, n_pair, own, rows,
    slot_ref, local_ref, pick_ref, coef_ref, ener_ref,
    a_out, g_out, e_out,
    *scratch,
):
    my_tm, my_pair = lax.axis_index("tm"), lax.axis_index("pair")
    sends, recvs = scratch[:CHUNKS], scratch[CHUNKS : 2 * CHUNKS]
    (e_send, e_recv, a_send, g_send, x_ener,
     pair_send, pair_recv, a_sems, g_sems, e_sems, own_sems) = scratch[2 * CHUNKS :]
    peers, others = n_pair - 1, n_tm - 1
    step = rows // CHUNKS
    greet(n_tm, n_pair, my_tm, my_pair)

    def pair_copy(i, c):
        target = lax.rem(my_pair + i + 1, n_pair)
        return pltpu.make_async_remote_copy(
            src_ref=sends[c].at[pl.ds(CAP * i, CAP)],
            dst_ref=recvs[c].at[pl.ds(CAP * i, CAP)],
            send_sem=pair_send.at[c], recv_sem=pair_recv.at[c],
            device_id=(my_tm, target), device_id_type=MESH,
        )

    def ener_copy(i):
        target = lax.rem(my_pair + i + 1, n_pair)
        return pltpu.make_async_remote_copy(
            src_ref=e_send.at[i], dst_ref=e_recv.at[i],
            send_sem=pair_send.at[CHUNKS], recv_sem=pair_recv.at[CHUNKS],
            device_id=(my_tm, target), device_id_type=MESH,
        )

    row_id = lax.broadcasted_iota(jnp.int32, (16, ener_ref.shape[2]), 0)

    def stage_a(u):
        owner = lax.rem(my_tm + u + 1, n_tm)
        for e in range(own):
            a_send[u, e] = coef_ref[local_ref[owner * own + e]]
        return owner

    def send_pair(c):
        def one(i, carry):
            for j in range(CAP):
                sends[c][CAP * i + j] = coef_ref[pick_ref[CAP * i + j], pl.ds(c * step, step), :]
            pair_copy(i, c).start()
            return carry

        lax.fori_loop(0, peers, one, 0)
        for j in range(CAP):
            recvs[c][CAP * peers + j] = coef_ref[pick_ref[CAP * peers + j], pl.ds(c * step, step), :]

    def stage_ener(i):
        tile = jnp.zeros(row_id.shape, jnp.float32)
        for j in range(CAP):
            tile = jnp.where(row_id == j, ener_ref[pick_ref[CAP * i + j]].astype(jnp.float32), tile)
        return tile.astype(jnp.bfloat16)

    def send_ener(i, carry):
        e_send[i] = stage_ener(i)
        ener_copy(i).start()
        return carry

    def a_one(u, carry):
        owner = stage_a(u)
        pltpu.make_async_remote_copy(
            src_ref=a_send.at[u], dst_ref=a_out.at[my_tm],
            send_sem=a_sems.at[0], recv_sem=a_sems.at[1],
            device_id=(owner, my_pair), device_id_type=MESH,
        ).start()
        return carry

    send_pair(0)
    lax.fori_loop(0, others, a_one, 0)
    stage_a(others)
    own_a = pltpu.make_async_copy(a_send.at[others], a_out.at[my_tm], own_sems.at[0])
    own_a.start()
    lax.fori_loop(0, peers, send_ener, 0)
    e_recv[peers] = stage_ener(peers)
    for c in range(1, CHUNKS):
        send_pair(c)

    owned_g = []
    for c in range(CHUNKS):
        wait_bytes(recvs[c].at[pl.ds(0, CAP * peers)], pair_recv.at[c])

        def stage_g(u):
            owner = lax.rem(my_tm + u + 1, n_tm)
            for e in range(own):
                g_send[c, u, e] = recvs[c][slot_ref[owner * own + e]]
            return owner

        def g_one(u, carry):
            owner = stage_g(u)
            pltpu.make_async_remote_copy(
                src_ref=g_send.at[c, u], dst_ref=g_out.at[c, my_tm],
                send_sem=g_sems.at[0, c], recv_sem=g_sems.at[1, c],
                device_id=(owner, my_pair), device_id_type=MESH,
            ).start()
            return carry

        lax.fori_loop(0, others, g_one, 0)
        stage_g(others)
        copy = pltpu.make_async_copy(g_send.at[c, others], g_out.at[c, my_tm], own_sems.at[1 + c])
        copy.start()
        owned_g.append(copy)
        if c == 0:
            wait_bytes(e_recv.at[pl.ds(0, peers)], pair_recv.at[CHUNKS])

            def stage_x(u):
                owner = lax.rem(my_tm + u + 1, n_tm)
                tile = jnp.zeros(row_id.shape, jnp.float32)
                for e in range(own):
                    slot = slot_ref[owner * own + e]
                    held = e_recv[slot // CAP].astype(jnp.float32)
                    picked = jnp.sum(jnp.where(row_id == lax.rem(slot, CAP), held, 0.0), axis=0, keepdims=True)
                    tile = jnp.where(row_id == e, picked, tile)
                    mine = ener_ref[local_ref[owner * own + e]].astype(jnp.float32)
                    tile = jnp.where(row_id == own + e, mine, tile)
                x_ener[u] = tile.astype(jnp.bfloat16)
                return owner

            def x_one(u, carry):
                owner = stage_x(u)
                pltpu.make_async_remote_copy(
                    src_ref=x_ener.at[u], dst_ref=e_out.at[my_tm],
                    send_sem=e_sems.at[0], recv_sem=e_sems.at[1],
                    device_id=(owner, my_pair), device_id_type=MESH,
                ).start()
                return carry

            lax.fori_loop(0, others, x_one, 0)
            stage_x(others)
            own_e = pltpu.make_async_copy(x_ener.at[others], e_out.at[my_tm], own_sems.at[1 + CHUNKS])
            own_e.start()

    for c in range(CHUNKS):
        wait_bytes(sends[c].at[pl.ds(0, CAP * peers)], pair_send.at[c])
    wait_bytes(e_send.at[pl.ds(0, peers)], pair_send.at[CHUNKS])
    for side in range(2):
        wait_bytes(a_send.at[pl.ds(0, others)], a_sems.at[side])
        wait_bytes(x_ener.at[pl.ds(0, others)], e_sems.at[side])
        for c in range(CHUNKS):
            wait_bytes(g_send.at[c, pl.ds(0, others)], g_sems.at[side, c])
    own_a.wait()
    own_e.wait()
    for copy in owned_g:
        copy.wait()


def entry_kernel(own, n_time, a_ref, g_ref, e_ref, tile_ref, cos_ref, tau_ref, live_ref, w_ref, c_ref, x_ref, y_ref):
    e = pl.program_id(0)
    slices, _, size, width = a_ref.shape
    live = live_ref[e]
    row_id = lax.broadcasted_iota(jnp.int32, (16, width), 0)
    chi = [jnp.zeros((size, size), jnp.float32) for _ in range(n_time)]
    for m in range(slices):
        ener = e_ref[m].astype(jnp.float32)
        eg = jnp.sum(jnp.where(row_id == e, ener, 0.0), axis=0, keepdims=True)
        ea = jnp.sum(jnp.where(row_id == own + e, ener, 0.0), axis=0, keepdims=True)
        a = a_ref[m, 0].astype(jnp.float32)
        g = g_ref[:, m, 0].reshape(size, width).astype(jnp.float32)
        for t in range(n_time):
            x = (a * jnp.exp(-tau_ref[t] * ea)).astype(jnp.bfloat16)
            y = (g * jnp.exp(-tau_ref[t] * eg)).astype(jnp.bfloat16)
            x_ref[t, m] = x
            y_ref[t, m] = y
            chi[t] = chi[t] + lax.dot_general(
                x, y, (((1,), (1,)), ((), ())), preferred_element_type=jnp.float32
            )
    chi = [c * live for c in chi]
    wfreq = []
    for w in range(n_time):
        chiw = sum(cos_ref[w, t] * chi[t] for t in range(n_time)).astype(jnp.bfloat16)
        prod = jnp.dot(chiw, tile_ref[0], preferred_element_type=jnp.float32)
        prod_b = prod.astype(jnp.bfloat16)
        wfreq.append(
            prod + jnp.dot(prod_b, prod_b, preferred_element_type=jnp.float32) * (1.0 / math.sqrt(size))
        )
    screened = []
    for t in range(n_time):
        wt = (sum(cos_ref[w, t] * wfreq[w] for w in range(n_time)) * (1.0 / n_time)).astype(jnp.bfloat16)
        w_ref[0, t] = wt
        screened.append(wt)
    for m in range(slices):
        total = jnp.zeros((1, width), jnp.float32)
        for t in range(n_time):
            wy = jnp.dot(screened[t], y_ref[t, m], preferred_element_type=jnp.float32)
            total = total + jnp.sum(x_ref[t, m].astype(jnp.float32) * wy, axis=0, keepdims=True)
        c_ref[0, pl.ds(m, 1), :] = total * (1.0 / n_time)


def return_kernel(
    n_tm, n_pair, own,
    back_ref, keep_ref, contrib_ref, owning_ref,
    out_ref,
    c_send, c_recv, p_send, p_recv, tm_sems, pair_sems,
):
    my_tm, my_pair = lax.axis_index("tm"), lax.axis_index("pair")
    peers, others = n_pair - 1, n_tm - 1
    width = out_ref.shape[1]
    c_send[...] = jnp.zeros_like(c_send)
    p_send[...] = jnp.zeros_like(p_send)
    greet(n_tm, n_pair, my_tm, my_pair)

    def stage_c(u):
        owner = lax.rem(my_tm + u + 1, n_tm)
        for e in range(own):
            c_send[u, pl.ds(e, 1), :] = contrib_ref[e, pl.ds(owner, 1), :]
        return owner

    def tm_one(u, carry):
        owner = stage_c(u)
        pltpu.make_async_remote_copy(
            src_ref=c_send.at[u], dst_ref=c_recv.at[u],
            send_sem=tm_sems.at[0], recv_sem=tm_sems.at[1],
            device_id=(owner, my_pair), device_id_type=MESH,
        ).start()
        return carry

    lax.fori_loop(0, others, tm_one, 0)
    stage_c(others)
    wait_bytes(c_recv.at[pl.ds(0, others)], tm_sems.at[1])
    c_recv[others] = c_send[others]

    def stage_p(i):
        for j in range(CAP):
            at = back_ref[CAP * i + j]
            keep = keep_ref[CAP * i + j]
            p_send[i, pl.ds(j, 1), :] = c_recv[at // own, pl.ds(lax.rem(at, own), 1), :] * keep

    def pair_one(i, carry):
        stage_p(i)
        target = lax.rem(my_pair + n_pair - 1 - i, n_pair)
        pltpu.make_async_remote_copy(
            src_ref=p_send.at[i], dst_ref=p_recv.at[i],
            send_sem=pair_sems.at[0], recv_sem=pair_sems.at[1],
            device_id=(my_tm, target), device_id_type=MESH,
        ).start()
        return carry

    lax.fori_loop(0, peers, pair_one, 0)
    stage_p(peers)
    wait_bytes(p_recv.at[pl.ds(0, peers)], pair_sems.at[1])
    p_recv[peers] = p_send[peers]
    incoming = p_recv[...].reshape(n_pair * 8, width)
    out_ref[...] = jnp.dot(
        owning_ref[...], incoming, precision=lax.Precision.HIGHEST, preferred_element_type=jnp.float32
    )
    wait_bytes(c_send.at[pl.ds(0, others)], tm_sems.at[0])
    wait_bytes(p_send.at[pl.ds(0, peers)], pair_sems.at[0])


def body(n_tm, n_pair, coefs, energies, coulomb, tau_grid, freq_grid, pairs):
    blocks, size, width = coefs.shape
    n_time = tau_grid.shape[0]
    listed = pairs.shape[1]
    own = listed // n_tm
    my_tm, my_pair = lax.axis_index("tm"), lax.axis_index("pair")
    remote, local = pairs[:, :, 0], pairs[:, :, 1]
    live = remote >= 0
    source = jnp.where(live, remote // blocks, -1)
    held = remote % blocks
    pos = jnp.arange(listed, dtype=jnp.int32)
    before = (source[:, :, None] == source[:, None, :]) & (pos[None, :] < pos[:, None])[None]
    rank = jnp.sum(before.astype(jnp.int32), axis=2)
    slots = jnp.arange(CAP, dtype=jnp.int32)
    hit = (source == my_pair)[:, None, :] & (rank[:, None, :] == slots[None, :, None])
    pick = jnp.sum(jnp.where(hit, held[:, None, :], 0), axis=2)
    used = jnp.sum(hit.astype(jnp.int32), axis=2)
    turn = lambda v: lax.dynamic_slice_in_dim(jnp.concatenate([v, v]), my_pair + 1, n_pair)
    pick, used = turn(pick), turn(used)
    row = lambda v: lax.dynamic_index_in_dim(v, my_pair, 0, keepdims=False)
    my_live, my_source, my_rank = row(live), row(source), row(rank)
    my_local = jnp.where(my_live, row(local), 0)
    offset = (my_pair - my_source + n_pair - 1) % n_pair
    slot = jnp.where(my_live, offset * CAP + my_rank, 0)
    lane = jnp.arange(n_pair * CAP, dtype=jnp.int32)
    match = (slot[None, :] == lane[:, None]) & my_live[None, :]
    back = jnp.sum(jnp.where(match, pos[None, :], 0), axis=1)
    back_keep = jnp.sum(match.astype(jnp.float32), axis=1)
    back = ((my_tm - back // own + n_tm - 1) % n_tm) * own + back % own
    tall = jnp.arange(8, dtype=jnp.int32)
    pick8 = jnp.pad(jnp.where(used > 0, pick, -1), ((0, 0), (0, 8 - CAP)), constant_values=-1)
    owning = (jnp.arange(blocks, dtype=jnp.int32)[:, None] == pick8.reshape(1, -1)).astype(jnp.float32)
    my_owned = lax.dynamic_slice_in_dim(my_live, my_tm * own, own).astype(jnp.float32)
    cosine = jnp.cos(freq_grid[:, None] * tau_grid[None, :])
    ener16 = jnp.broadcast_to(energies[:, None, :], (blocks, 16, width))

    smem = pl.BlockSpec(memory_space=pltpu.SMEM)
    vmem = pl.BlockSpec(memory_space=pltpu.VMEM)
    hbm = pl.BlockSpec(memory_space=pl.ANY)
    step = size // CHUNKS
    bf16 = jnp.bfloat16
    DMA = pltpu.SemaphoreType.DMA
    a_all, g_all, e_all = pl.pallas_call(
        functools.partial(gather_kernel, n_tm, n_pair, own, size),
        out_shape=(
            jax.ShapeDtypeStruct((n_tm, own, size, width), bf16),
            jax.ShapeDtypeStruct((CHUNKS, n_tm, own, step, width), bf16),
            jax.ShapeDtypeStruct((n_tm, 16, width), bf16),
        ),
        in_specs=[smem] * 3 + [vmem] * 2,
        out_specs=(hbm, hbm, hbm),
        scratch_shapes=[pltpu.VMEM((CAP * n_pair, step, width), bf16)] * (2 * CHUNKS)
        + [
            pltpu.VMEM((n_pair, 16, width), bf16),
            pltpu.VMEM((n_pair, 16, width), bf16),
            pltpu.VMEM((n_tm, own, size, width), bf16),
            pltpu.VMEM((CHUNKS, n_tm, own, step, width), bf16),
            pltpu.VMEM((n_tm, 16, width), bf16),
            DMA((CHUNKS + 1,)),
            DMA((CHUNKS + 1,)),
            DMA((2,)),
            DMA((2, CHUNKS)),
            DMA((2,)),
            DMA((2 + CHUNKS,)),
        ],
        compiler_params=pltpu.CompilerParams(
            collective_id=0, has_side_effects=True, vmem_limit_bytes=56 * 1024 * 1024
        ),
    )(slot, my_local, pick.reshape(-1), coefs, ener16)

    screened, contrib = pl.pallas_call(
        functools.partial(entry_kernel, own, n_time),
        grid=(own,),
        out_shape=(
            jax.ShapeDtypeStruct((own, n_time, size, size), bf16),
            jax.ShapeDtypeStruct((own, n_tm, width), jnp.float32),
        ),
        in_specs=[
            pl.BlockSpec((n_tm, 1, size, width), lambda e: (0, e, 0, 0)),
            pl.BlockSpec((CHUNKS, n_tm, 1, step, width), lambda e: (0, 0, e, 0, 0)),
            pl.BlockSpec((n_tm, 16, width), lambda e: (0, 0, 0)),
            pl.BlockSpec((1, size, size), lambda e: (e, 0, 0)),
            smem, smem, smem,
        ],
        out_specs=(
            pl.BlockSpec((1, n_time, size, size), lambda e: (e, 0, 0, 0)),
            pl.BlockSpec((1, n_tm, width), lambda e: (e, 0, 0)),
        ),
        scratch_shapes=[pltpu.VMEM((n_time, n_tm, size, width), bf16)] * 2,
        compiler_params=pltpu.CompilerParams(vmem_limit_bytes=48 * 1024 * 1024),
    )(a_all, g_all, e_all, coulomb[0], cosine, tau_grid, my_owned)

    self_energy = pl.pallas_call(
        functools.partial(return_kernel, n_tm, n_pair, own),
        out_shape=jax.ShapeDtypeStruct((blocks, width), jnp.float32),
        in_specs=[smem, smem, vmem, vmem],
        out_specs=vmem,
        scratch_shapes=[
            pltpu.VMEM((n_tm, 8, width), jnp.float32),
            pltpu.VMEM((n_tm, 8, width), jnp.float32),
            pltpu.VMEM((n_pair, 8, width), jnp.float32),
            pltpu.VMEM((n_pair, 8, width), jnp.float32),
            DMA((2,)),
            DMA((2,)),
        ],
        compiler_params=pltpu.CompilerParams(collective_id=1, has_side_effects=True),
    )(back, back_keep, contrib, owning)
    return (screened[None], self_energy)


def solution(mesh):
    return jax.shard_map(
        functools.partial(body, mesh.shape["tm"], mesh.shape["pair"]),
        mesh=mesh,
        in_specs=(
            P("pair", None, "tm"),
            P("pair", "tm"),
            P("pair", "tm", None, None),
            P(),
            P(),
            P(),
        ),
        out_specs=(P("pair", "tm", None, None, None), P("pair", "tm")),
        check_vma=False,
    )
```

```python
import functools
import math

import jax
import jax.numpy as jnp
from jax import lax
from jax.experimental import pallas as pl
from jax.experimental.pallas import tpu as pltpu
from jax.sharding import PartitionSpec as P

CAP = 2
CHUNKS = 4
FAST_CHUNKS = 8
Y_CAP = 15
Z_CAPS = (11, 11, 10, 9)
N_Y = 4
POOLS = 3
MESH = pl.DeviceIdType.MESH


def greet(n_tm, n_pair, my_tm, my_pair):
    barrier = pltpu.get_barrier_semaphore()

    def pair_peer(i, c):
        other = lax.rem(my_pair + i, n_pair)
        pl.semaphore_signal(barrier, inc=1, device_id=(my_tm, other), device_id_type=MESH)
        return c

    def tm_peer(i, c):
        other = lax.rem(my_tm + i, n_tm)
        pl.semaphore_signal(barrier, inc=1, device_id=(other, my_pair), device_id_type=MESH)
        return c

    lax.fori_loop(1, n_pair, pair_peer, 0)
    lax.fori_loop(1, n_tm, tm_peer, 0)
    pl.semaphore_wait(barrier, n_pair + n_tm - 2)


def wait_bytes(ref, sem):
    pltpu.make_async_copy(ref, ref, sem).wait()


def gather_kernel(
    n_tm, n_pair, own, rows,
    slot_ref, local_ref, pick_ref, coef_ref, ener_ref,
    a_out, g_out, e_out,
    *scratch,
):
    my_tm, my_pair = lax.axis_index("tm"), lax.axis_index("pair")
    sends, recvs = scratch[:CHUNKS], scratch[CHUNKS : 2 * CHUNKS]
    (e_send, e_recv, a_send, g_send, x_ener,
     pair_send, pair_recv, a_sems, g_sems, e_sems, own_sems) = scratch[2 * CHUNKS :]
    peers, others = n_pair - 1, n_tm - 1
    step = rows // CHUNKS
    greet(n_tm, n_pair, my_tm, my_pair)

    def pair_copy(i, c):
        target = lax.rem(my_pair + i + 1, n_pair)
        return pltpu.make_async_remote_copy(
            src_ref=sends[c].at[pl.ds(CAP * i, CAP)],
            dst_ref=recvs[c].at[pl.ds(CAP * i, CAP)],
            send_sem=pair_send.at[c], recv_sem=pair_recv.at[c],
            device_id=(my_tm, target), device_id_type=MESH,
        )

    def ener_copy(i):
        target = lax.rem(my_pair + i + 1, n_pair)
        return pltpu.make_async_remote_copy(
            src_ref=e_send.at[i], dst_ref=e_recv.at[i],
            send_sem=pair_send.at[CHUNKS], recv_sem=pair_recv.at[CHUNKS],
            device_id=(my_tm, target), device_id_type=MESH,
        )

    row_id = lax.broadcasted_iota(jnp.int32, (16, ener_ref.shape[2]), 0)

    def stage_a(u):
        owner = lax.rem(my_tm + u + 1, n_tm)
        for e in range(own):
            a_send[u, e] = coef_ref[local_ref[owner * own + e]]
        return owner

    def send_pair(c):
        def one(i, carry):
            for j in range(CAP):
                sends[c][CAP * i + j] = coef_ref[pick_ref[CAP * i + j], pl.ds(c * step, step), :]
            pair_copy(i, c).start()
            return carry

        lax.fori_loop(0, peers, one, 0)
        for j in range(CAP):
            recvs[c][CAP * peers + j] = coef_ref[pick_ref[CAP * peers + j], pl.ds(c * step, step), :]

    def stage_ener(i):
        tile = jnp.zeros(row_id.shape, jnp.float32)
        for j in range(CAP):
            tile = jnp.where(row_id == j, ener_ref[pick_ref[CAP * i + j]].astype(jnp.float32), tile)
        return tile.astype(jnp.bfloat16)

    def send_ener(i, carry):
        e_send[i] = stage_ener(i)
        ener_copy(i).start()
        return carry

    def a_one(u, carry):
        owner = stage_a(u)
        pltpu.make_async_remote_copy(
            src_ref=a_send.at[u], dst_ref=a_out.at[my_tm],
            send_sem=a_sems.at[0], recv_sem=a_sems.at[1],
            device_id=(owner, my_pair), device_id_type=MESH,
        ).start()
        return carry

    send_pair(0)
    lax.fori_loop(0, others, a_one, 0)
    stage_a(others)
    own_a = pltpu.make_async_copy(a_send.at[others], a_out.at[my_tm], own_sems.at[0])
    own_a.start()
    lax.fori_loop(0, peers, send_ener, 0)
    e_recv[peers] = stage_ener(peers)
    for c in range(1, CHUNKS):
        send_pair(c)

    owned_g = []
    for c in range(CHUNKS):
        wait_bytes(recvs[c].at[pl.ds(0, CAP * peers)], pair_recv.at[c])

        def stage_g(u):
            owner = lax.rem(my_tm + u + 1, n_tm)
            for e in range(own):
                g_send[c, u, e] = recvs[c][slot_ref[owner * own + e]]
            return owner

        def g_one(u, carry):
            owner = stage_g(u)
            pltpu.make_async_remote_copy(
                src_ref=g_send.at[c, u], dst_ref=g_out.at[my_tm, :, pl.ds(c * step, step)],
                send_sem=g_sems.at[0, c], recv_sem=g_sems.at[1, c],
                device_id=(owner, my_pair), device_id_type=MESH,
            ).start()
            return carry

        lax.fori_loop(0, others, g_one, 0)
        stage_g(others)
        copy = pltpu.make_async_copy(g_send.at[c, others], g_out.at[my_tm, :, pl.ds(c * step, step)], own_sems.at[1 + c])
        copy.start()
        owned_g.append(copy)
        if c == 0:
            wait_bytes(e_recv.at[pl.ds(0, peers)], pair_recv.at[CHUNKS])

            def stage_x(u):
                owner = lax.rem(my_tm + u + 1, n_tm)
                tile = jnp.zeros(row_id.shape, jnp.float32)
                for e in range(own):
                    slot = slot_ref[owner * own + e]
                    held = e_recv[slot // CAP].astype(jnp.float32)
                    picked = jnp.sum(jnp.where(row_id == lax.rem(slot, CAP), held, 0.0), axis=0, keepdims=True)
                    tile = jnp.where(row_id == e, picked, tile)
                    mine = ener_ref[local_ref[owner * own + e]].astype(jnp.float32)
                    tile = jnp.where(row_id == own + e, mine, tile)
                x_ener[u] = tile.astype(jnp.bfloat16)
                return owner

            def x_one(u, carry):
                owner = stage_x(u)
                pltpu.make_async_remote_copy(
                    src_ref=x_ener.at[u], dst_ref=e_out.at[my_tm],
                    send_sem=e_sems.at[0], recv_sem=e_sems.at[1],
                    device_id=(owner, my_pair), device_id_type=MESH,
                ).start()
                return carry

            lax.fori_loop(0, others, x_one, 0)
            stage_x(others)
            own_e = pltpu.make_async_copy(x_ener.at[others], e_out.at[my_tm], own_sems.at[1 + CHUNKS])
            own_e.start()

    for c in range(CHUNKS):
        wait_bytes(sends[c].at[pl.ds(0, CAP * peers)], pair_send.at[c])
    wait_bytes(e_send.at[pl.ds(0, peers)], pair_send.at[CHUNKS])
    for side in range(2):
        wait_bytes(a_send.at[pl.ds(0, others)], a_sems.at[side])
        wait_bytes(x_ener.at[pl.ds(0, others)], e_sems.at[side])
        for c in range(CHUNKS):
            wait_bytes(g_send.at[c, pl.ds(0, others)], g_sems.at[side, c])
    own_a.wait()
    own_e.wait()
    for copy in owned_g:
        copy.wait()


def fast_kernel(
    n_tm, n_pair, own, rows,
    final_ref, slot_ref, local_ref, pick_ref, y_ref, z_ref, coef_ref, ener_ref,
    a_out, g_out, e_out,
    y_send, y_recv, z_send, z_recv, e_send, e_recv, x_send, x_ener, *rest,
):
    pools = rest[:POOLS]
    (y_ssem, y_rsem, z_ssem, z_rsem, pair_send, pair_recv, a_sems, g_sems, e_sems, own_sems) = rest[POOLS:]
    my_tm, my_pair = lax.axis_index("tm"), lax.axis_index("pair")
    peers, others = n_pair - 1, n_tm - 1
    n_z = n_pair // N_Y
    my_y, my_z = my_pair // n_z, lax.rem(my_pair, n_z)
    step = rows // FAST_CHUNKS
    blocks = coef_ref.shape[0]
    y_slots = (N_Y - 1) * Y_CAP
    ahead = (my_y * n_z + lax.rem(my_z + 1, n_z), my_y * n_z + lax.rem(my_z + n_z - 1, n_z))
    firsts = [sum(Z_CAPS[:r]) for r in range(len(Z_CAPS) + 1)]
    greet(n_tm, n_pair, my_tm, my_pair)
    row_id = lax.broadcasted_iota(jnp.int32, (16, ener_ref.shape[2]), 0)

    def ener_copy(i):
        target = lax.rem(my_pair + i + 1, n_pair)
        return pltpu.make_async_remote_copy(
            src_ref=e_send.at[i], dst_ref=e_recv.at[i],
            send_sem=pair_send, recv_sem=pair_recv,
            device_id=(my_tm, target), device_id_type=MESH,
        )

    def stage_ener(i):
        tile = jnp.zeros(row_id.shape, jnp.float32)
        for j in range(CAP):
            tile = jnp.where(row_id == j, ener_ref[pick_ref[CAP * i + j]].astype(jnp.float32), tile)
        return tile.astype(jnp.bfloat16)

    def send_ener(i, carry):
        e_send[i] = stage_ener(i)
        ener_copy(i).start()
        return carry

    def send_y(c):
        for i in range(N_Y - 1):
            def one(j, carry):
                y_send[c, i, j] = coef_ref[y_ref[i * Y_CAP + j], pl.ds(c * step, step), :]
                return carry

            lax.fori_loop(0, Y_CAP, one, 0)
            target = lax.rem(my_y + i + 1, N_Y) * n_z + my_z
            pltpu.make_async_remote_copy(
                src_ref=y_send.at[c, i], dst_ref=y_recv.at[c, i],
                send_sem=y_ssem, recv_sem=y_rsem.at[c],
                device_id=(my_tm, target), device_id_type=MESH,
            ).start()

    def fill(c):
        pool = pools[c % POOLS]
        pool[pl.ds(0, blocks)] = coef_ref[:, pl.ds(c * step, step), :]
        wait_bytes(y_recv.at[c], y_rsem.at[c])
        for i in range(N_Y - 1):
            pool[pl.ds(blocks + i * Y_CAP, Y_CAP)] = y_recv[c, i]

    def span(c, r, way):
        return (c, way, pl.ds(firsts[r], Z_CAPS[r]))

    def send_z(c, r):
        pool = pools[c % POOLS]
        for way in range(2):
            base = (2 * r + way) * Z_CAPS[0]

            def one(j, carry):
                z_send[c, way, firsts[r] + j] = pool[z_ref[base + j]]
                return carry

            lax.fori_loop(0, Z_CAPS[r], one, 0)
            pltpu.make_async_remote_copy(
                src_ref=z_send.at[span(c, r, way)], dst_ref=z_recv.at[span(c, r, way)],
                send_sem=z_ssem, recv_sem=z_rsem.at[c, r, way],
                device_id=(my_tm, ahead[way]), device_id_type=MESH,
            ).start()

    def take_z(c, r):
        pool = pools[c % POOLS]
        for way in range(2):
            wait_bytes(z_recv.at[span(c, r, way)], z_rsem.at[c, r, way])
            at = blocks + y_slots + way * firsts[-1] + firsts[r]
            pool[pl.ds(at, Z_CAPS[r])] = z_recv[span(c, r, way)]

    def stage_a(u):
        owner = lax.rem(my_tm + u + 1, n_tm)
        for e in range(own):
            x_send[u, e] = coef_ref[local_ref[owner * own + e]]
        return owner

    def a_one(u, carry):
        owner = stage_a(u)
        pltpu.make_async_remote_copy(
            src_ref=x_send.at[u], dst_ref=a_out.at[my_tm],
            send_sem=a_sems.at[0], recv_sem=a_sems.at[1],
            device_id=(owner, my_pair), device_id_type=MESH,
        ).start()
        return carry

    def send_x(c):
        pool = pools[c % POOLS]
        part = pl.ds(c * step, step)

        def stage_g(u):
            owner = lax.rem(my_tm + u + 1, n_tm)
            for e in range(own):
                x_send[u, e, part] = pool[final_ref[owner * own + e]]
            return owner

        def g_one(u, carry):
            owner = stage_g(u)
            pltpu.make_async_remote_copy(
                src_ref=x_send.at[u, :, part], dst_ref=g_out.at[my_tm, :, part],
                send_sem=g_sems.at[0, c], recv_sem=g_sems.at[1, c],
                device_id=(owner, my_pair), device_id_type=MESH,
            ).start()
            return carry

        lax.fori_loop(0, others, g_one, 0)
        stage_g(others)
        pltpu.make_async_copy(x_send.at[others, :, part], g_out.at[my_tm, :, part], own_sems.at[1 + c]).start()

    def send_x_ener():
        wait_bytes(e_recv.at[pl.ds(0, peers)], pair_recv)

        def stage_x(u):
            owner = lax.rem(my_tm + u + 1, n_tm)
            tile = jnp.zeros(row_id.shape, jnp.float32)
            for e in range(own):
                slot = slot_ref[owner * own + e]
                held = e_recv[slot // CAP].astype(jnp.float32)
                picked = jnp.sum(jnp.where(row_id == lax.rem(slot, CAP), held, 0.0), axis=0, keepdims=True)
                tile = jnp.where(row_id == e, picked, tile)
                mine = ener_ref[local_ref[owner * own + e]].astype(jnp.float32)
                tile = jnp.where(row_id == own + e, mine, tile)
            x_ener[u] = tile.astype(jnp.bfloat16)
            return owner

        def x_one(u, carry):
            owner = stage_x(u)
            pltpu.make_async_remote_copy(
                src_ref=x_ener.at[u], dst_ref=e_out.at[my_tm],
                send_sem=e_sems.at[0], recv_sem=e_sems.at[1],
                device_id=(owner, my_pair), device_id_type=MESH,
            ).start()
            return carry

        lax.fori_loop(0, others, x_one, 0)
        stage_x(others)
        pltpu.make_async_copy(x_ener.at[others], e_out.at[my_tm], own_sems.at[1 + FAST_CHUNKS]).start()

    send_y(0)
    lax.fori_loop(0, peers, send_ener, 0)
    e_recv[peers] = stage_ener(peers)
    send_y(1)
    lax.fori_loop(0, others, a_one, 0)
    stage_a(others)
    own_a = pltpu.make_async_copy(x_send.at[others], a_out.at[my_tm], own_sems.at[0])
    own_a.start()
    last = len(Z_CAPS) - 1
    fill(0)
    send_z(0, 0)
    fill(1)
    send_z(1, 0)
    for first in range(0, FAST_CHUNKS, 2):
        second = first + 1
        more = first + 2 < FAST_CHUNKS
        if more:
            send_y(first + 2)
        for r in range(last):
            take_z(first, r)
            send_z(first, r + 1)
            take_z(second, r)
            send_z(second, r + 1)
            if more and r == 0:
                send_y(first + 3)
        if more:
            fill(first + 2)
            send_z(first + 2, 0)
        take_z(first, last)
        if first == 0:
            own_a.wait()
            wait_bytes(x_send.at[pl.ds(0, others)], a_sems.at[0])
        send_x(first)
        if more:
            fill(first + 3)
            send_z(first + 3, 0)
        take_z(second, last)
        send_x(second)
        if first == 0:
            send_x_ener()

    wait_bytes(y_send, y_ssem)
    wait_bytes(z_send, z_ssem)
    wait_bytes(e_send.at[pl.ds(0, peers)], pair_send)
    wait_bytes(x_send.at[pl.ds(0, others)], a_sems.at[1])
    for side in range(2):
        wait_bytes(x_ener.at[pl.ds(0, others)], e_sems.at[side])
        for c in range(FAST_CHUNKS):
            wait_bytes(x_send.at[pl.ds(0, others), :, pl.ds(c * step, step)], g_sems.at[side, c])
    for c in range(FAST_CHUNKS):
        part = pl.ds(c * step, step)
        pltpu.make_async_copy(x_send.at[others, :, part], g_out.at[my_tm, :, part], own_sems.at[1 + c]).wait()
    pltpu.make_async_copy(x_ener.at[others], e_out.at[my_tm], own_sems.at[1 + FAST_CHUNKS]).wait()


def list_fits(n_pair, live, source):
    n_z = n_pair // N_Y
    ids = jnp.arange(n_pair, dtype=jnp.int32)
    count = jnp.sum((source[:, :, None] == ids).astype(jnp.int32), axis=1)
    by_y = jnp.sum(count.reshape(N_Y, n_z, N_Y, n_z), axis=1)
    far = jnp.arange(N_Y)[:, None, None] != jnp.arange(N_Y)[None, :, None]
    fits = jnp.all(jnp.where(far, by_y, 0) <= Y_CAP)
    at = jnp.sum(count.reshape(N_Y, n_z, N_Y, n_z), axis=2)
    half = n_z // 2
    y_id, z_id = jnp.arange(N_Y)[:, None], jnp.arange(n_z)[None, :]
    zd_id, zs_id = jnp.arange(n_z)[:, None], jnp.arange(n_z)[None, :]
    delta = (zd_id - zs_id) % n_z
    for way in range(2):
        queue = [None]
        for far_by in range(1, half + 1):
            gap = far_by if way == 0 else n_z - far_by
            n = jnp.sum(jnp.where(delta[None] == gap, at, 0), axis=1)
            if far_by == half:
                even = (y_id + z_id) % 2 == 0
                n = (n + jnp.where(even, 1 - way, way)) // 2
            queue.append(n)
        for cap in Z_CAPS:
            left = jnp.full((N_Y, n_z), cap, jnp.int32)
            moved = [None] * (half + 1)
            for far_by in range(half, 0, -1):
                moved[far_by] = jnp.minimum(queue[far_by], left)
                left = left - moved[far_by]
            for far_by in range(1, half + 1):
                queue[far_by] = queue[far_by] - moved[far_by]
                if far_by < half:
                    queue[far_by] = queue[far_by] + jnp.roll(moved[far_by + 1], 1 - 2 * way, axis=1)
        fits = fits & (sum(jnp.sum(q) for q in queue[1:]) == 0)
    return fits


def routes(n_pair, blocks, my_pair, live, source, held, rank):
    listed = live.shape[1]
    n_z = n_pair // N_Y
    my_y, my_z = my_pair // n_z, my_pair % n_z
    rows = jnp.arange(n_pair, dtype=jnp.int32)
    mine = source == my_pair
    per_row = jnp.sum(mine.astype(jnp.int32), axis=1)
    same = (rows[:, None] // n_z == rows[None, :] // n_z) & (rows[None, :] < rows[:, None])
    first = jnp.sum(jnp.where(same, per_row[None, :], 0), axis=1)
    place = jnp.where(mine, first[:, None] + rank, -1).reshape(N_Y, 1, n_z * listed)
    want = jnp.arange(Y_CAP, dtype=jnp.int32)[None, :, None]
    y_tab = jnp.sum(jnp.where(place == want, held.reshape(N_Y, 1, n_z * listed), 0), axis=2)
    y_tab = lax.dynamic_slice_in_dim(jnp.concatenate([y_tab, y_tab]), my_y + 1, N_Y - 1)

    ring = lambda v: lax.dynamic_slice_in_dim(v, my_y * n_z, n_z).reshape(n_z * listed)
    src, hold, alive = ring(source), ring(held), ring(live)
    n = n_z * listed
    ids = jnp.arange(n, dtype=jnp.int32)
    zd = ids // listed
    ys, zs = src // n_z, src % n_z
    earlier = ids[None, :] < ids[:, None]
    y_rank = jnp.sum(((src[:, None] == src[None, :]) & earlier).astype(jnp.int32), axis=1)
    z_key = jnp.where(alive, zs, -1)
    z_rank = jnp.sum(
        ((z_key[:, None] == z_key[None, :]) & (zd[:, None] == zd[None, :]) & earlier).astype(jnp.int32), axis=1
    )
    step_y = (my_y - ys) % N_Y
    loc = jnp.where(step_y == 0, hold, blocks + (step_y - 1) * Y_CAP + y_rank)
    loc = jnp.where(alive, loc, 0)
    delta = (zd - zs) % n_z
    half = n_z // 2
    plus = (delta < half) | ((delta == half) & ((z_rank + zs + my_y) % 2 == 0))
    way = jnp.where(plus, 0, 1)
    rem = jnp.where(alive, jnp.where(plus, delta, n_z - delta), 0)
    pos = zs
    total = sum(Z_CAPS)
    tables, begun = [], 0
    slots = jnp.arange(Z_CAPS[0], dtype=jnp.int32)
    for cap in Z_CAPS:
        active = rem > 0
        group = jnp.where(active, pos * 2 + way, -1)
        key = rem * n - ids
        ahead = (group[:, None] == group[None, :]) & (key[None, :] > key[:, None])
        order = jnp.sum(ahead.astype(jnp.int32), axis=1)
        moved = active & (order < cap)
        for w in range(2):
            here = jnp.where(moved & (group == my_z * 2 + w), order, -1)
            tables.append(jnp.sum(jnp.where(here[None, :] == slots[:, None], loc[None, :], 0), axis=1))
        to = blocks + (N_Y - 1) * Y_CAP + way * total + begun + order
        loc = jnp.where(moved, to, loc)
        pos = jnp.where(moved, (pos + jnp.where(plus, 1, n_z - 1)) % n_z, pos)
        rem = rem - moved.astype(jnp.int32)
        begun += cap
    final = lax.dynamic_slice_in_dim(loc, my_z * listed, listed)
    return y_tab.reshape(-1), jnp.concatenate(tables), final


def entry_kernel(own, n_time, a_ref, g_ref, e_ref, tile_ref, cos_ref, tau_ref, live_ref, w_ref, c_ref, x_ref, y_ref):
    e = pl.program_id(0)
    slices, _, size, width = a_ref.shape
    live = live_ref[e]
    row_id = lax.broadcasted_iota(jnp.int32, (16, width), 0)
    chi = [jnp.zeros((size, size), jnp.float32) for _ in range(n_time)]
    for m in range(slices):
        ener = e_ref[m].astype(jnp.float32)
        eg = jnp.sum(jnp.where(row_id == e, ener, 0.0), axis=0, keepdims=True)
        ea = jnp.sum(jnp.where(row_id == own + e, ener, 0.0), axis=0, keepdims=True)
        a = a_ref[m, 0].astype(jnp.float32)
        g = g_ref[m, 0].astype(jnp.float32)
        for t in range(n_time):
            x = (a * jnp.exp(-tau_ref[t] * ea)).astype(jnp.bfloat16)
            y = (g * jnp.exp(-tau_ref[t] * eg)).astype(jnp.bfloat16)
            x_ref[t, m] = x
            y_ref[t, m] = y
            chi[t] = chi[t] + lax.dot_general(
                x, y, (((1,), (1,)), ((), ())), preferred_element_type=jnp.float32
            )
    chi = [c * live for c in chi]
    wfreq = []
    for w in range(n_time):
        chiw = sum(cos_ref[w, t] * chi[t] for t in range(n_time)).astype(jnp.bfloat16)
        prod = jnp.dot(chiw, tile_ref[0], preferred_element_type=jnp.float32)
        prod_b = prod.astype(jnp.bfloat16)
        wfreq.append(
            prod + jnp.dot(prod_b, prod_b, preferred_element_type=jnp.float32) * (1.0 / math.sqrt(size))
        )
    screened = []
    for t in range(n_time):
        wt = (sum(cos_ref[w, t] * wfreq[w] for w in range(n_time)) * (1.0 / n_time)).astype(jnp.bfloat16)
        w_ref[0, t] = wt
        screened.append(wt)
    for m in range(slices):
        total = jnp.zeros((1, width), jnp.float32)
        for t in range(n_time):
            wy = jnp.dot(screened[t], y_ref[t, m], preferred_element_type=jnp.float32)
            total = total + jnp.sum(x_ref[t, m].astype(jnp.float32) * wy, axis=0, keepdims=True)
        c_ref[0, pl.ds(m, 1), :] = total * (1.0 / n_time)


def return_kernel(
    n_tm, n_pair, own,
    back_ref, keep_ref, contrib_ref, owning_ref,
    out_ref,
    c_send, c_recv, p_send, p_recv, tm_sems, pair_sems,
):
    my_tm, my_pair = lax.axis_index("tm"), lax.axis_index("pair")
    peers, others = n_pair - 1, n_tm - 1
    width = out_ref.shape[1]
    c_send[...] = jnp.zeros_like(c_send)
    p_send[...] = jnp.zeros_like(p_send)
    greet(n_tm, n_pair, my_tm, my_pair)

    def stage_c(u):
        owner = lax.rem(my_tm + u + 1, n_tm)
        for e in range(own):
            c_send[u, pl.ds(e, 1), :] = contrib_ref[e, pl.ds(owner, 1), :]
        return owner

    def tm_one(u, carry):
        owner = stage_c(u)
        pltpu.make_async_remote_copy(
            src_ref=c_send.at[u], dst_ref=c_recv.at[u],
            send_sem=tm_sems.at[0], recv_sem=tm_sems.at[1],
            device_id=(owner, my_pair), device_id_type=MESH,
        ).start()
        return carry

    lax.fori_loop(0, others, tm_one, 0)
    stage_c(others)
    wait_bytes(c_recv.at[pl.ds(0, others)], tm_sems.at[1])
    c_recv[others] = c_send[others]

    def stage_p(i):
        for j in range(CAP):
            at = back_ref[CAP * i + j]
            keep = keep_ref[CAP * i + j]
            p_send[i, pl.ds(j, 1), :] = c_recv[at // own, pl.ds(lax.rem(at, own), 1), :] * keep

    def pair_one(i, carry):
        stage_p(i)
        target = lax.rem(my_pair + n_pair - 1 - i, n_pair)
        pltpu.make_async_remote_copy(
            src_ref=p_send.at[i], dst_ref=p_recv.at[i],
            send_sem=pair_sems.at[0], recv_sem=pair_sems.at[1],
            device_id=(my_tm, target), device_id_type=MESH,
        ).start()
        return carry

    lax.fori_loop(0, peers, pair_one, 0)
    stage_p(peers)
    wait_bytes(p_recv.at[pl.ds(0, peers)], pair_sems.at[1])
    p_recv[peers] = p_send[peers]
    incoming = p_recv[...].reshape(n_pair * 8, width)
    out_ref[...] = jnp.dot(
        owning_ref[...], incoming, precision=lax.Precision.HIGHEST, preferred_element_type=jnp.float32
    )
    wait_bytes(c_send.at[pl.ds(0, others)], tm_sems.at[0])
    wait_bytes(p_send.at[pl.ds(0, peers)], pair_sems.at[0])


def body(n_tm, n_pair, coefs, energies, coulomb, tau_grid, freq_grid, pairs):
    blocks, size, width = coefs.shape
    n_time = tau_grid.shape[0]
    listed = pairs.shape[1]
    own = listed // n_tm
    my_tm, my_pair = lax.axis_index("tm"), lax.axis_index("pair")
    remote, local = pairs[:, :, 0], pairs[:, :, 1]
    live = remote >= 0
    source = jnp.where(live, remote // blocks, -1)
    held = remote % blocks
    pos = jnp.arange(listed, dtype=jnp.int32)
    before = (source[:, :, None] == source[:, None, :]) & (pos[None, :] < pos[:, None])[None]
    rank = jnp.sum(before.astype(jnp.int32), axis=2)
    slots = jnp.arange(CAP, dtype=jnp.int32)
    hit = (source == my_pair)[:, None, :] & (rank[:, None, :] == slots[None, :, None])
    pick = jnp.sum(jnp.where(hit, held[:, None, :], 0), axis=2)
    used = jnp.sum(hit.astype(jnp.int32), axis=2)
    turn = lambda v: lax.dynamic_slice_in_dim(jnp.concatenate([v, v]), my_pair + 1, n_pair)
    pick, used = turn(pick), turn(used)
    row = lambda v: lax.dynamic_index_in_dim(v, my_pair, 0, keepdims=False)
    my_live, my_source, my_rank = row(live), row(source), row(rank)
    my_local = jnp.where(my_live, row(local), 0)
    offset = (my_pair - my_source + n_pair - 1) % n_pair
    slot = jnp.where(my_live, offset * CAP + my_rank, 0)
    lane = jnp.arange(n_pair * CAP, dtype=jnp.int32)
    match = (slot[None, :] == lane[:, None]) & my_live[None, :]
    back = jnp.sum(jnp.where(match, pos[None, :], 0), axis=1)
    back_keep = jnp.sum(match.astype(jnp.float32), axis=1)
    back = ((my_tm - back // own + n_tm - 1) % n_tm) * own + back % own
    tall = jnp.arange(8, dtype=jnp.int32)
    pick8 = jnp.pad(jnp.where(used > 0, pick, -1), ((0, 0), (0, 8 - CAP)), constant_values=-1)
    owning = (jnp.arange(blocks, dtype=jnp.int32)[:, None] == pick8.reshape(1, -1)).astype(jnp.float32)
    my_owned = lax.dynamic_slice_in_dim(my_live, my_tm * own, own).astype(jnp.float32)
    cosine = jnp.cos(freq_grid[:, None] * tau_grid[None, :])
    ener16 = jnp.broadcast_to(energies[:, None, :], (blocks, 16, width))

    smem = pl.BlockSpec(memory_space=pltpu.SMEM)
    vmem = pl.BlockSpec(memory_space=pltpu.VMEM)
    hbm = pl.BlockSpec(memory_space=pl.ANY)
    bf16 = jnp.bfloat16
    DMA = pltpu.SemaphoreType.DMA
    step = size // CHUNKS
    thin = size // FAST_CHUNKS
    gathered = (
        jax.ShapeDtypeStruct((n_tm, own, size, width), bf16),
        jax.ShapeDtypeStruct((n_tm, own, size, width), bf16),
        jax.ShapeDtypeStruct((n_tm, 16, width), bf16),
    )
    fits = list_fits(n_pair, live, source)
    y_tab, z_tab, final = routes(n_pair, blocks, my_pair, live, source, held, rank)
    pick_flat = pick.reshape(-1)

    def pooled(slot, my_local, pick_flat, y_tab, z_tab, final, coefs, ener16):
        total = sum(Z_CAPS)
        depth = blocks + (N_Y - 1) * Y_CAP + 2 * total
        return pl.pallas_call(
            functools.partial(fast_kernel, n_tm, n_pair, own, size),
            out_shape=gathered,
            in_specs=[smem] * 6 + [vmem] * 2,
            out_specs=(hbm, hbm, hbm),
            scratch_shapes=[pltpu.VMEM((FAST_CHUNKS, N_Y - 1, Y_CAP, thin, width), bf16)] * 2
            + [pltpu.VMEM((FAST_CHUNKS, 2, total, thin, width), bf16)] * 2
            + [
                pltpu.VMEM((n_pair, 16, width), bf16),
                pltpu.VMEM((n_pair, 16, width), bf16),
                pltpu.VMEM((n_tm, own, size, width), bf16),
                pltpu.VMEM((n_tm, 16, width), bf16),
            ]
            + [pltpu.VMEM((depth, thin, width), bf16)] * POOLS
            + [
                DMA,
                DMA((FAST_CHUNKS,)),
                DMA,
                DMA((FAST_CHUNKS, len(Z_CAPS), 2)),
                DMA,
                DMA,
                DMA((2,)),
                DMA((2, FAST_CHUNKS)),
                DMA((2,)),
                DMA((2 + FAST_CHUNKS,)),
            ],
            compiler_params=pltpu.CompilerParams(
                collective_id=2, has_side_effects=True, vmem_limit_bytes=62 * 1024 * 1024
            ),
        )(final, slot, my_local, pick_flat, y_tab, z_tab, coefs, ener16)

    def direct(slot, my_local, pick_flat, y_tab, z_tab, final, coefs, ener16):
        return pl.pallas_call(
            functools.partial(gather_kernel, n_tm, n_pair, own, size),
            out_shape=gathered,
            in_specs=[smem] * 3 + [vmem] * 2,
            out_specs=(hbm, hbm, hbm),
            scratch_shapes=[pltpu.VMEM((CAP * n_pair, step, width), bf16)] * (2 * CHUNKS)
            + [
                pltpu.VMEM((n_pair, 16, width), bf16),
                pltpu.VMEM((n_pair, 16, width), bf16),
                pltpu.VMEM((n_tm, own, size, width), bf16),
                pltpu.VMEM((CHUNKS, n_tm, own, step, width), bf16),
                pltpu.VMEM((n_tm, 16, width), bf16),
                DMA((CHUNKS + 1,)),
                DMA((CHUNKS + 1,)),
                DMA((2,)),
                DMA((2, CHUNKS)),
                DMA((2,)),
                DMA((2 + CHUNKS,)),
            ],
            compiler_params=pltpu.CompilerParams(
                collective_id=0, has_side_effects=True, vmem_limit_bytes=56 * 1024 * 1024
            ),
        )(slot, my_local, pick_flat, coefs, ener16)

    a_all, g_all, e_all = lax.cond(
        fits, pooled, direct, slot, my_local, pick_flat, y_tab, z_tab, final, coefs, ener16
    )

    screened, contrib = pl.pallas_call(
        functools.partial(entry_kernel, own, n_time),
        grid=(own,),
        out_shape=(
            jax.ShapeDtypeStruct((own, n_time, size, size), bf16),
            jax.ShapeDtypeStruct((own, n_tm, width), jnp.float32),
        ),
        in_specs=[
            pl.BlockSpec((n_tm, 1, size, width), lambda e: (0, e, 0, 0)),
            pl.BlockSpec((n_tm, 1, size, width), lambda e: (0, e, 0, 0)),
            pl.BlockSpec((n_tm, 16, width), lambda e: (0, 0, 0)),
            pl.BlockSpec((1, size, size), lambda e: (e, 0, 0)),
            smem, smem, smem,
        ],
        out_specs=(
            pl.BlockSpec((1, n_time, size, size), lambda e: (e, 0, 0, 0)),
            pl.BlockSpec((1, n_tm, width), lambda e: (e, 0, 0)),
        ),
        scratch_shapes=[pltpu.VMEM((n_time, n_tm, size, width), bf16)] * 2,
        compiler_params=pltpu.CompilerParams(vmem_limit_bytes=48 * 1024 * 1024),
    )(a_all, g_all, e_all, coulomb[0], cosine, tau_grid, my_owned)

    self_energy = pl.pallas_call(
        functools.partial(return_kernel, n_tm, n_pair, own),
        out_shape=jax.ShapeDtypeStruct((blocks, width), jnp.float32),
        in_specs=[smem, smem, vmem, vmem],
        out_specs=vmem,
        scratch_shapes=[
            pltpu.VMEM((n_tm, 8, width), jnp.float32),
            pltpu.VMEM((n_tm, 8, width), jnp.float32),
            pltpu.VMEM((n_pair, 8, width), jnp.float32),
            pltpu.VMEM((n_pair, 8, width), jnp.float32),
            DMA((2,)),
            DMA((2,)),
        ],
        compiler_params=pltpu.CompilerParams(collective_id=1, has_side_effects=True),
    )(back, back_keep, contrib, owning)
    return (screened[None], self_energy)


def solution(mesh):
    return jax.shard_map(
        functools.partial(body, mesh.shape["tm"], mesh.shape["pair"]),
        mesh=mesh,
        in_specs=(
            P("pair", None, "tm"),
            P("pair", "tm"),
            P("pair", "tm", None, None),
            P(),
            P(),
            P(),
        ),
        out_specs=(P("pair", "tm", None, None, None), P("pair", "tm")),
        check_vma=False,
    )
```

```python
import functools
import math

import jax
import jax.numpy as jnp
from jax import lax
from jax.experimental import pallas as pl
from jax.experimental.pallas import tpu as pltpu
from jax.sharding import PartitionSpec as P

CAP = 2
CHUNKS = 4
PARTS = (16, 16, 32, 32, 32, 32, 32, 32, 16, 16)
FAST_CHUNKS = len(PARTS)
Y_CAP = 15
Z_CAPS = (10, 10, 10, 9)
LINE = 128
N_Y = 4
POOLS = 3
MESH = pl.DeviceIdType.MESH


def greet(n_tm, n_pair, my_tm, my_pair):
    barrier = pltpu.get_barrier_semaphore()

    def pair_peer(i, c):
        other = lax.rem(my_pair + i, n_pair)
        pl.semaphore_signal(barrier, inc=1, device_id=(my_tm, other), device_id_type=MESH)
        return c

    def tm_peer(i, c):
        other = lax.rem(my_tm + i, n_tm)
        pl.semaphore_signal(barrier, inc=1, device_id=(other, my_pair), device_id_type=MESH)
        return c

    lax.fori_loop(1, n_pair, pair_peer, 0)
    lax.fori_loop(1, n_tm, tm_peer, 0)
    pl.semaphore_wait(barrier, n_pair + n_tm - 2)


class View:
    def __init__(self, ref, at):
        self.ref, self.at = ref, at

    def __getitem__(self, i):
        return self.ref[self.at + i]


def views(table, listed, n_pair):
    sizes = (listed, listed, CAP * n_pair, listed, (N_Y - 1) * Y_CAP)
    at = [sum(sizes[:i]) for i in range(len(sizes) + 1)]
    return [View(table, i) for i in at]


def wait_bytes(ref, sem):
    pltpu.make_async_copy(ref, ref, sem).wait()


def gather_kernel(
    n_tm, n_pair, own, rows,
    table_ref, coef_ref, ener_ref,
    a_out, g_out, e_out,
    *scratch,
):
    slot_ref, local_ref, pick_ref = views(table_ref, n_tm * own, n_pair)[:3]
    my_tm, my_pair = lax.axis_index("tm"), lax.axis_index("pair")
    sends, recvs = scratch[:CHUNKS], scratch[CHUNKS : 2 * CHUNKS]
    (e_send, e_recv, a_send, g_send, x_ener,
     pair_send, pair_recv, a_sems, g_sems, e_sems, own_sems) = scratch[2 * CHUNKS :]
    peers, others = n_pair - 1, n_tm - 1
    step = rows // CHUNKS
    greet(n_tm, n_pair, my_tm, my_pair)

    def pair_copy(i, c):
        target = lax.rem(my_pair + i + 1, n_pair)
        return pltpu.make_async_remote_copy(
            src_ref=sends[c].at[pl.ds(CAP * i, CAP)],
            dst_ref=recvs[c].at[pl.ds(CAP * i, CAP)],
            send_sem=pair_send.at[c], recv_sem=pair_recv.at[c],
            device_id=(my_tm, target), device_id_type=MESH,
        )

    def ener_copy(i):
        target = lax.rem(my_pair + i + 1, n_pair)
        return pltpu.make_async_remote_copy(
            src_ref=e_send.at[pl.ds(CAP * i, CAP)], dst_ref=e_recv.at[pl.ds(CAP * i, CAP)],
            send_sem=pair_send.at[CHUNKS], recv_sem=pair_recv.at[CHUNKS],
            device_id=(my_tm, target), device_id_type=MESH,
        )


    def stage_a(u):
        owner = lax.rem(my_tm + u + 1, n_tm)
        for e in range(own):
            a_send[u, e] = coef_ref[local_ref[owner * own + e]]
        return owner

    def send_pair(c):
        def one(i, carry):
            for j in range(CAP):
                sends[c][CAP * i + j] = coef_ref[pick_ref[CAP * i + j], pl.ds(c * step, step), :]
            pair_copy(i, c).start()
            return carry

        lax.fori_loop(0, peers, one, 0)
        for j in range(CAP):
            recvs[c][CAP * peers + j] = coef_ref[pick_ref[CAP * peers + j], pl.ds(c * step, step), :]

    def send_ener(i, carry):
        for j in range(CAP):
            e_send[CAP * i + j] = ener_ref[pick_ref[CAP * i + j]]
        ener_copy(i).start()
        return carry

    def keep_ener():
        for j in range(CAP * peers, CAP * n_pair):
            e_recv[j] = ener_ref[pick_ref[j]]

    def a_one(u, carry):
        owner = stage_a(u)
        pltpu.make_async_remote_copy(
            src_ref=a_send.at[u], dst_ref=a_out.at[my_tm],
            send_sem=a_sems.at[0], recv_sem=a_sems.at[1],
            device_id=(owner, my_pair), device_id_type=MESH,
        ).start()
        return carry

    send_pair(0)
    lax.fori_loop(0, others, a_one, 0)
    stage_a(others)
    own_a = pltpu.make_async_copy(a_send.at[others], a_out.at[my_tm], own_sems.at[0])
    own_a.start()
    lax.fori_loop(0, peers, send_ener, 0)
    keep_ener()
    for c in range(1, CHUNKS):
        send_pair(c)

    owned_g = []
    for c in range(CHUNKS):
        wait_bytes(recvs[c].at[pl.ds(0, CAP * peers)], pair_recv.at[c])

        def stage_g(u):
            owner = lax.rem(my_tm + u + 1, n_tm)
            for e in range(own):
                g_send[c, u, e] = recvs[c][slot_ref[owner * own + e]]
            return owner

        def g_one(u, carry):
            owner = stage_g(u)
            pltpu.make_async_remote_copy(
                src_ref=g_send.at[c, u], dst_ref=g_out.at[my_tm, :, pl.ds(c * step, step)],
                send_sem=g_sems.at[0, c], recv_sem=g_sems.at[1, c],
                device_id=(owner, my_pair), device_id_type=MESH,
            ).start()
            return carry

        lax.fori_loop(0, others, g_one, 0)
        stage_g(others)
        copy = pltpu.make_async_copy(g_send.at[c, others], g_out.at[my_tm, :, pl.ds(c * step, step)], own_sems.at[1 + c])
        copy.start()
        owned_g.append(copy)
        if c == 0:
            wait_bytes(e_recv.at[pl.ds(0, CAP * peers)], pair_recv.at[CHUNKS])

            def stage_x(u):
                owner = lax.rem(my_tm + u + 1, n_tm)
                for e in range(own):
                    x_ener[u, e] = e_recv[slot_ref[owner * own + e]]
                    x_ener[u, own + e] = ener_ref[local_ref[owner * own + e]]
                return owner

            def x_one(u, carry):
                owner = stage_x(u)
                pltpu.make_async_remote_copy(
                    src_ref=x_ener.at[u], dst_ref=e_out.at[my_tm],
                    send_sem=e_sems.at[0], recv_sem=e_sems.at[1],
                    device_id=(owner, my_pair), device_id_type=MESH,
                ).start()
                return carry

            lax.fori_loop(0, others, x_one, 0)
            stage_x(others)
            own_e = pltpu.make_async_copy(x_ener.at[others], e_out.at[my_tm], own_sems.at[1 + CHUNKS])
            own_e.start()

    for c in range(CHUNKS):
        wait_bytes(sends[c].at[pl.ds(0, CAP * peers)], pair_send.at[c])
    wait_bytes(e_send.at[pl.ds(0, CAP * peers)], pair_send.at[CHUNKS])
    for side in range(2):
        wait_bytes(a_send.at[pl.ds(0, others)], a_sems.at[side])
        wait_bytes(x_ener.at[pl.ds(0, others)], e_sems.at[side])
        for c in range(CHUNKS):
            wait_bytes(g_send.at[c, pl.ds(0, others)], g_sems.at[side, c])
    own_a.wait()
    own_e.wait()
    for copy in owned_g:
        copy.wait()


def fast_kernel(
    n_tm, n_pair, own, rows,
    table_ref, coef_ref, ener_ref,
    a_out, g_out, e_out,
    y_send, y_recv, z_send, z_recv, e_send, e_recv, x_send, x_ener, *rest,
):
    slot_ref, local_ref, pick_ref, final_ref, y_ref, z_ref = views(table_ref, n_tm * own, n_pair)
    pools = rest[:POOLS]
    (y_ssem, y_rsem, z_ssem, z_rsem, pair_send, pair_recv, a_sems, g_sems, e_sems, own_sems) = rest[POOLS:]
    my_tm, my_pair = lax.axis_index("tm"), lax.axis_index("pair")
    peers, others = n_pair - 1, n_tm - 1
    n_z = n_pair // N_Y
    my_y, my_z = my_pair // n_z, lax.rem(my_pair, n_z)
    assert sum(PARTS) == rows
    spans = [pl.ds(sum(PARTS[:c]), PARTS[c]) for c in range(FAST_CHUNKS)]
    blocks = coef_ref.shape[0]
    y_slots = (N_Y - 1) * Y_CAP
    ahead = (my_y * n_z + lax.rem(my_z + 1, n_z), my_y * n_z + lax.rem(my_z + n_z - 1, n_z))
    firsts = [sum(Z_CAPS[:r]) for r in range(len(Z_CAPS) + 1)]
    greet(n_tm, n_pair, my_tm, my_pair)

    def ener_copy(i):
        target = lax.rem(my_pair + i + 1, n_pair)
        return pltpu.make_async_remote_copy(
            src_ref=e_send.at[pl.ds(CAP * i, CAP)], dst_ref=e_recv.at[pl.ds(CAP * i, CAP)],
            send_sem=pair_send, recv_sem=pair_recv,
            device_id=(my_tm, target), device_id_type=MESH,
        )

    def send_ener(i, carry):
        for j in range(CAP):
            e_send[CAP * i + j] = ener_ref[pick_ref[CAP * i + j]]
        ener_copy(i).start()
        return carry

    def keep_ener():
        for j in range(CAP * peers, CAP * n_pair):
            e_recv[j] = ener_ref[pick_ref[j]]

    def send_y(c):
        for i in range(N_Y - 1):
            def one(j, carry):
                y_send[i, j, spans[c]] = coef_ref[y_ref[i * Y_CAP + j], spans[c], :]
                return carry

            lax.fori_loop(0, Y_CAP, one, 0)
            target = lax.rem(my_y + i + 1, N_Y) * n_z + my_z
            pltpu.make_async_remote_copy(
                src_ref=y_send.at[i, :, spans[c]], dst_ref=y_recv.at[i, :, spans[c]],
                send_sem=y_ssem, recv_sem=y_rsem.at[c],
                device_id=(my_tm, target), device_id_type=MESH,
            ).start()

    def fill(c):
        pool = pools[c % POOLS]
        held = pl.ds(0, PARTS[c])
        pool[pl.ds(0, blocks), held] = coef_ref[:, spans[c], :]
        wait_bytes(y_recv.at[:, :, spans[c]], y_rsem.at[c])
        for i in range(N_Y - 1):
            pool[pl.ds(blocks + i * Y_CAP, Y_CAP), held] = y_recv[i, :, spans[c]]

    def span(c, r, way):
        return (way, pl.ds(firsts[r], Z_CAPS[r]), spans[c])

    def send_z(c, r):
        pool = pools[c % POOLS]
        for way in range(2):
            base = (2 * r + way) * Z_CAPS[0]

            def one(j, carry):
                z_send[way, firsts[r] + j, spans[c]] = pool[z_ref[base + j], pl.ds(0, PARTS[c])]
                return carry

            lax.fori_loop(0, Z_CAPS[r], one, 0)
            pltpu.make_async_remote_copy(
                src_ref=z_send.at[span(c, r, way)], dst_ref=z_recv.at[span(c, r, way)],
                send_sem=z_ssem, recv_sem=z_rsem.at[c, r, way],
                device_id=(my_tm, ahead[way]), device_id_type=MESH,
            ).start()

    def take_z(c, r):
        pool = pools[c % POOLS]
        for way in range(2):
            wait_bytes(z_recv.at[span(c, r, way)], z_rsem.at[c, r, way])
            at = blocks + y_slots + way * firsts[-1] + firsts[r]
            pool[pl.ds(at, Z_CAPS[r]), pl.ds(0, PARTS[c])] = z_recv[span(c, r, way)]

    def stage_a(u):
        owner = lax.rem(my_tm + u + 1, n_tm)
        for e in range(own):
            x_send[u, e] = coef_ref[local_ref[owner * own + e]]
        return owner

    def a_one(u, carry):
        owner = stage_a(u)
        pltpu.make_async_remote_copy(
            src_ref=x_send.at[u], dst_ref=a_out.at[my_tm],
            send_sem=a_sems.at[0], recv_sem=a_sems.at[1],
            device_id=(owner, my_pair), device_id_type=MESH,
        ).start()
        return carry

    def send_x(c):
        pool = pools[c % POOLS]
        part = spans[c]

        def stage_g(u):
            owner = lax.rem(my_tm + u + 1, n_tm)
            for e in range(own):
                x_send[u, e, part] = pool[final_ref[owner * own + e], pl.ds(0, PARTS[c])]
            return owner

        def g_one(u, carry):
            owner = stage_g(u)
            pltpu.make_async_remote_copy(
                src_ref=x_send.at[u, :, part], dst_ref=g_out.at[my_tm, :, part],
                send_sem=g_sems.at[0, c], recv_sem=g_sems.at[1, c],
                device_id=(owner, my_pair), device_id_type=MESH,
            ).start()
            return carry

        lax.fori_loop(0, others, g_one, 0)
        stage_g(others)
        pltpu.make_async_copy(x_send.at[others, :, part], g_out.at[my_tm, :, part], own_sems.at[1 + c]).start()

    def send_x_ener():
        wait_bytes(e_recv.at[pl.ds(0, CAP * peers)], pair_recv)

        def stage_x(u):
            owner = lax.rem(my_tm + u + 1, n_tm)
            for e in range(own):
                x_ener[u, e] = e_recv[slot_ref[owner * own + e]]
                x_ener[u, own + e] = ener_ref[local_ref[owner * own + e]]
            return owner

        def x_one(u, carry):
            owner = stage_x(u)
            pltpu.make_async_remote_copy(
                src_ref=x_ener.at[u], dst_ref=e_out.at[my_tm],
                send_sem=e_sems.at[0], recv_sem=e_sems.at[1],
                device_id=(owner, my_pair), device_id_type=MESH,
            ).start()
            return carry

        lax.fori_loop(0, others, x_one, 0)
        stage_x(others)
        pltpu.make_async_copy(x_ener.at[others], e_out.at[my_tm], own_sems.at[1 + FAST_CHUNKS]).start()

    send_y(0)
    lax.fori_loop(0, peers, send_ener, 0)
    keep_ener()
    send_y(1)
    lax.fori_loop(0, others, a_one, 0)
    stage_a(others)
    own_a = pltpu.make_async_copy(x_send.at[others], a_out.at[my_tm], own_sems.at[0])
    own_a.start()
    last = len(Z_CAPS) - 1
    fill(0)
    send_z(0, 0)
    fill(1)
    send_z(1, 0)
    for first in range(0, FAST_CHUNKS, 2):
        second = first + 1
        more = first + 2 < FAST_CHUNKS
        if more:
            send_y(first + 2)
        for r in range(last):
            take_z(first, r)
            send_z(first, r + 1)
            take_z(second, r)
            send_z(second, r + 1)
            if more and r == 0:
                send_y(first + 3)
        if more:
            fill(first + 2)
            send_z(first + 2, 0)
        take_z(first, last)
        if first == 0:
            own_a.wait()
            wait_bytes(x_send.at[pl.ds(0, others)], a_sems.at[0])
        send_x(first)
        if more:
            fill(first + 3)
            send_z(first + 3, 0)
        take_z(second, last)
        send_x(second)
        if first == 0:
            send_x_ener()

    wait_bytes(y_send, y_ssem)
    wait_bytes(z_send, z_ssem)
    wait_bytes(e_send.at[pl.ds(0, CAP * peers)], pair_send)
    wait_bytes(x_send.at[pl.ds(0, others)], a_sems.at[1])
    for side in range(2):
        wait_bytes(x_ener.at[pl.ds(0, others)], e_sems.at[side])
        for c in range(FAST_CHUNKS):
            wait_bytes(x_send.at[pl.ds(0, others), :, spans[c]], g_sems.at[side, c])
    for c in range(FAST_CHUNKS):
        part = spans[c]
        pltpu.make_async_copy(x_send.at[others, :, part], g_out.at[my_tm, :, part], own_sems.at[1 + c]).wait()
    pltpu.make_async_copy(x_ener.at[others], e_out.at[my_tm], own_sems.at[1 + FAST_CHUNKS]).wait()


def routes(n_pair, blocks, my_pair, live, source, held, rank):
    listed = live.shape[1]
    n_z = n_pair // N_Y
    n = n_z * listed
    my_y, my_z = my_pair // n_z, my_pair % n_z
    rows = jnp.arange(n_pair, dtype=jnp.int32)
    mine = source == my_pair
    per_row = jnp.sum(mine.astype(jnp.int32), axis=1)
    same = (rows[:, None] // n_z == rows[None, :] // n_z) & (rows[None, :] < rows[:, None])
    first = jnp.sum(jnp.where(same, per_row[None, :], 0), axis=1)
    place = jnp.where(mine, first[:, None] + rank, -1).reshape(N_Y, 1, n)
    want = jnp.arange(Y_CAP, dtype=jnp.int32)[None, :, None]
    y_tab = jnp.sum(jnp.where(place == want, held.reshape(N_Y, 1, n), 0), axis=2)
    y_tab = lax.dynamic_slice_in_dim(jnp.concatenate([y_tab, y_tab]), my_y + 1, N_Y - 1)
    ring_source = source.reshape(N_Y, n)
    count = jnp.sum((ring_source[:, None, :] == rows[None, :, None]).astype(jnp.int32), axis=2)
    leg = jnp.where(rows[None, :] // n_z == jnp.arange(N_Y)[:, None], 0, count)

    pos_in = jnp.arange(listed, dtype=jnp.int32)
    z_key = jnp.where(live, source % n_z, -1)
    z_same = (z_key[:, :, None] == z_key[:, None, :]) & (pos_in[None, :] < pos_in[:, None])[None]
    z_rank = jnp.sum(z_same.astype(jnp.int32), axis=2).reshape(N_Y, n)
    ids = jnp.arange(n, dtype=jnp.int32)
    zd = ids // listed
    zs = ring_source % n_z
    delta = (zd[None, :] - zs) % n_z
    half = n_z // 2
    plus = (delta < half) | ((delta == half) & ((z_rank + zs + jnp.arange(N_Y)[:, None]) % 2 == 0))
    way = jnp.where(plus, 0, 1)
    rem = jnp.where(live.reshape(N_Y, n), jnp.where(plus, delta, n_z - delta), 0)
    pos = zs

    ring = lambda v: lax.dynamic_index_in_dim(v, my_y, 0, keepdims=False)
    src, my_way = ring(ring_source), ring(way)
    earlier = ids[None, :] < ids[:, None]
    y_rank = jnp.sum(((src[:, None] == src[None, :]) & earlier).astype(jnp.int32), axis=1)
    step_y = (my_y - src // n_z) % N_Y
    loc = jnp.where(step_y == 0, ring(held.reshape(N_Y, n)), blocks + (step_y - 1) * Y_CAP + y_rank)
    loc = jnp.where(src >= 0, loc, 0)
    total = sum(Z_CAPS)
    tables, begun = [], 0
    slots = jnp.arange(Z_CAPS[0], dtype=jnp.int32)
    for cap in Z_CAPS:
        group = jnp.where(rem > 0, pos * 2 + way, -1)
        key = rem * n - ids[None, :]
        ahead = (group[:, :, None] == group[:, None, :]) & (key[:, None, :] > key[:, :, None])
        order = jnp.sum(ahead.astype(jnp.int32), axis=2)
        moved = (rem > 0) & (order < cap)
        my_order, my_moved, my_group = ring(order), ring(moved), ring(group)
        for w in range(2):
            here = jnp.where(my_moved & (my_group == my_z * 2 + w), my_order, -1)
            tables.append(jnp.sum(jnp.where(here[None, :] == slots[:, None], loc[None, :], 0), axis=1))
        loc = jnp.where(my_moved, blocks + (N_Y - 1) * Y_CAP + my_way * total + begun + my_order, loc)
        pos = jnp.where(moved, (pos + jnp.where(plus, 1, n_z - 1)) % n_z, pos)
        rem = rem - moved.astype(jnp.int32)
        begun += cap
    final = lax.dynamic_slice_in_dim(loc, my_z * listed, listed)
    fits = jnp.maximum(jnp.max(rem), jnp.max(leg - Y_CAP)) <= 0
    return fits, y_tab.reshape(-1), jnp.concatenate(tables), final


def entry_kernel(own, n_time, a_ref, g_ref, e_ref, tile_ref, cos_ref, tau_ref, live_ref, w_ref, c_ref, x_ref, y_ref):
    e = pl.program_id(0)
    slices, _, size, width = a_ref.shape
    live = live_ref[e]
    lines = lambda v: jnp.concatenate([v[i : i + 1] for i in range(v.shape[0])], axis=1)
    chi = [jnp.zeros((size, size), jnp.float32) for _ in range(n_time)]
    for m in range(slices):
        eg = lines(e_ref[m, e])
        ea = lines(e_ref[m, own + e])
        a = a_ref[m, 0].astype(jnp.float32)
        g = g_ref[m, 0].astype(jnp.float32)
        for t in range(n_time):
            x = (a * jnp.exp(-tau_ref[t] * ea)).astype(jnp.bfloat16)
            y = (g * jnp.exp(-tau_ref[t] * eg)).astype(jnp.bfloat16)
            x_ref[t, m] = x
            y_ref[t, m] = y
            chi[t] = chi[t] + lax.dot_general(
                x, y, (((1,), (1,)), ((), ())), preferred_element_type=jnp.float32
            )
    chi = [c * live for c in chi]
    wfreq = []
    for w in range(n_time):
        chiw = sum(cos_ref[w, t] * chi[t] for t in range(n_time)).astype(jnp.bfloat16)
        prod = jnp.dot(chiw, tile_ref[0], preferred_element_type=jnp.float32)
        prod_b = prod.astype(jnp.bfloat16)
        wfreq.append(
            prod + jnp.dot(prod_b, prod_b, preferred_element_type=jnp.float32) * (1.0 / math.sqrt(size))
        )
    screened = []
    for t in range(n_time):
        wt = (sum(cos_ref[w, t] * wfreq[w] for w in range(n_time)) * (1.0 / n_time)).astype(jnp.bfloat16)
        w_ref[0, t] = wt
        screened.append(wt)
    for m in range(slices):
        total = jnp.zeros((1, width), jnp.float32)
        for t in range(n_time):
            wy = jnp.dot(screened[t], y_ref[t, m], preferred_element_type=jnp.float32)
            total = total + jnp.sum(x_ref[t, m].astype(jnp.float32) * wy, axis=0, keepdims=True)
        c_ref[0, pl.ds(m, 1), :] = total * (1.0 / n_time)


def return_kernel(
    n_tm, n_pair, own,
    back_ref, contrib_ref, owning_ref,
    out_ref,
    c_send, c_recv, p_send, p_recv, tm_sems, pair_sems,
):
    my_tm, my_pair = lax.axis_index("tm"), lax.axis_index("pair")
    peers, others = n_pair - 1, n_tm - 1
    width = out_ref.shape[1]
    c_send[...] = jnp.zeros_like(c_send)
    greet(n_tm, n_pair, my_tm, my_pair)

    def stage_c(u):
        owner = lax.rem(my_tm + u + 1, n_tm)
        for e in range(own):
            c_send[u, pl.ds(e, 1), :] = contrib_ref[e, pl.ds(owner, 1), :]
        return owner

    def tm_one(u, carry):
        owner = stage_c(u)
        pltpu.make_async_remote_copy(
            src_ref=c_send.at[u], dst_ref=c_recv.at[u],
            send_sem=tm_sems.at[0], recv_sem=tm_sems.at[1],
            device_id=(owner, my_pair), device_id_type=MESH,
        ).start()
        return carry

    lax.fori_loop(0, others, tm_one, 0)
    stage_c(others)
    wait_bytes(c_recv.at[pl.ds(0, others)], tm_sems.at[1])
    c_recv[others] = c_send[others]

    def stage_p(i):
        for j in range(CAP):
            at = back_ref[CAP * i + j]
            keep = jnp.where(at >= 0, 1.0, 0.0)
            at = jnp.maximum(at, 0)
            line = c_recv[at // own, pl.ds(lax.rem(at, own), 1), :] * keep
            for h in range(width // LINE):
                p_send[CAP * i + j, pl.ds(h, 1), :] = line[:, h * LINE : (h + 1) * LINE]

    def pair_one(i, carry):
        stage_p(i)
        target = lax.rem(my_pair + n_pair - 1 - i, n_pair)
        pltpu.make_async_remote_copy(
            src_ref=p_send.at[pl.ds(CAP * i, CAP)], dst_ref=p_recv.at[pl.ds(CAP * i, CAP)],
            send_sem=pair_sems.at[0], recv_sem=pair_sems.at[1],
            device_id=(my_tm, target), device_id_type=MESH,
        ).start()
        return carry

    lax.fori_loop(0, peers, pair_one, 0)
    stage_p(peers)
    wait_bytes(p_recv.at[pl.ds(0, CAP * peers)], pair_sems.at[1])
    for j in range(CAP * peers, CAP * n_pair):
        p_recv[j] = p_send[j]
    for h in range(width // LINE):
        out_ref[:, pl.ds(h * LINE, LINE)] = jnp.dot(
            owning_ref[...], p_recv[:, h, :], precision=lax.Precision.HIGHEST, preferred_element_type=jnp.float32
        )
    wait_bytes(c_send.at[pl.ds(0, others)], tm_sems.at[0])
    wait_bytes(p_send.at[pl.ds(0, CAP * peers)], pair_sems.at[0])


def body(n_tm, n_pair, coefs, energies, coulomb, tau_grid, freq_grid, pairs):
    blocks, size, width = coefs.shape
    n_time = tau_grid.shape[0]
    listed = pairs.shape[1]
    own = listed // n_tm
    my_tm, my_pair = lax.axis_index("tm"), lax.axis_index("pair")
    remote, local = pairs[:, :, 0], pairs[:, :, 1]
    live = remote >= 0
    source = jnp.where(live, remote // blocks, -1)
    held = remote % blocks
    pos = jnp.arange(listed, dtype=jnp.int32)
    before = (source[:, :, None] == source[:, None, :]) & (pos[None, :] < pos[:, None])[None]
    rank = jnp.sum(before.astype(jnp.int32), axis=2)
    slots = jnp.arange(CAP, dtype=jnp.int32)
    hit = (source == my_pair)[:, None, :] & (rank[:, None, :] == slots[None, :, None])
    pick = jnp.sum(jnp.where(hit, held[:, None, :], 0), axis=2)
    used = jnp.sum(hit.astype(jnp.int32), axis=2)
    turn = lambda v: lax.dynamic_slice_in_dim(jnp.concatenate([v, v]), my_pair + 1, n_pair)
    pick, used = turn(pick), turn(used)
    row = lambda v: lax.dynamic_index_in_dim(v, my_pair, 0, keepdims=False)
    my_live, my_source, my_rank = row(live), row(source), row(rank)
    my_local = jnp.where(my_live, row(local), 0)
    offset = (my_pair - my_source + n_pair - 1) % n_pair
    slot = jnp.where(my_live, offset * CAP + my_rank, 0)
    lane = jnp.arange(n_pair * CAP, dtype=jnp.int32)
    match = (slot[None, :] == lane[:, None]) & my_live[None, :]
    back = jnp.sum(jnp.where(match, pos[None, :], 0), axis=1)
    back = ((my_tm - back // own + n_tm - 1) % n_tm) * own + back % own
    back = jnp.where(jnp.any(match, axis=1), back, -1)
    given = jnp.where(used > 0, pick, -1).reshape(1, -1)
    owning = (jnp.arange(blocks, dtype=jnp.int32)[:, None] == given).astype(jnp.float32)
    my_owned = lax.dynamic_slice_in_dim(my_live, my_tm * own, own).astype(jnp.float32)
    cosine = jnp.cos(freq_grid[:, None] * tau_grid[None, :])
    lined = energies.astype(jnp.float32).reshape(blocks, width // LINE, LINE)

    smem = pl.BlockSpec(memory_space=pltpu.SMEM)
    vmem = pl.BlockSpec(memory_space=pltpu.VMEM)
    hbm = pl.BlockSpec(memory_space=pl.ANY)
    bf16 = jnp.bfloat16
    DMA = pltpu.SemaphoreType.DMA
    step = size // CHUNKS
    thin = size // FAST_CHUNKS
    gathered = (
        jax.ShapeDtypeStruct((n_tm, own, size, width), bf16),
        jax.ShapeDtypeStruct((n_tm, own, size, width), bf16),
        jax.ShapeDtypeStruct((n_tm, 2 * own, width // LINE, LINE), jnp.float32),
    )
    fits, y_tab, z_tab, final = routes(n_pair, blocks, my_pair, live, source, held, rank)
    table = jnp.concatenate([slot, my_local, pick.reshape(-1), final, y_tab, z_tab]).astype(jnp.int32)

    def pooled(table, coefs, lined):
        total = sum(Z_CAPS)
        depth = blocks + (N_Y - 1) * Y_CAP + 2 * total
        return pl.pallas_call(
            functools.partial(fast_kernel, n_tm, n_pair, own, size),
            out_shape=gathered,
            in_specs=[smem] + [vmem] * 2,
            out_specs=(hbm, hbm, hbm),
            scratch_shapes=[pltpu.VMEM((N_Y - 1, Y_CAP, size, width), bf16)] * 2
            + [pltpu.VMEM((2, total, size, width), bf16)] * 2
            + [
                pltpu.VMEM((CAP * n_pair, width // LINE, LINE), jnp.float32),
                pltpu.VMEM((CAP * n_pair, width // LINE, LINE), jnp.float32),
                pltpu.VMEM((n_tm, own, size, width), bf16),
                pltpu.VMEM((n_tm, 2 * own, width // LINE, LINE), jnp.float32),
            ]
            + [pltpu.VMEM((depth, max(PARTS), width), bf16)] * POOLS
            + [
                DMA,
                DMA((FAST_CHUNKS,)),
                DMA,
                DMA((FAST_CHUNKS, len(Z_CAPS), 2)),
                DMA,
                DMA,
                DMA((2,)),
                DMA((2, FAST_CHUNKS)),
                DMA((2,)),
                DMA((2 + FAST_CHUNKS,)),
            ],
            compiler_params=pltpu.CompilerParams(
                collective_id=2, has_side_effects=True, vmem_limit_bytes=62 * 1024 * 1024
            ),
        )(table, coefs, lined)

    def direct(table, coefs, lined):
        return pl.pallas_call(
            functools.partial(gather_kernel, n_tm, n_pair, own, size),
            out_shape=gathered,
            in_specs=[smem] + [vmem] * 2,
            out_specs=(hbm, hbm, hbm),
            scratch_shapes=[pltpu.VMEM((CAP * n_pair, step, width), bf16)] * (2 * CHUNKS)
            + [
                pltpu.VMEM((CAP * n_pair, width // LINE, LINE), jnp.float32),
                pltpu.VMEM((CAP * n_pair, width // LINE, LINE), jnp.float32),
                pltpu.VMEM((n_tm, own, size, width), bf16),
                pltpu.VMEM((CHUNKS, n_tm, own, step, width), bf16),
                pltpu.VMEM((n_tm, 2 * own, width // LINE, LINE), jnp.float32),
                DMA((CHUNKS + 1,)),
                DMA((CHUNKS + 1,)),
                DMA((2,)),
                DMA((2, CHUNKS)),
                DMA((2,)),
                DMA((2 + CHUNKS,)),
            ],
            compiler_params=pltpu.CompilerParams(
                collective_id=0, has_side_effects=True, vmem_limit_bytes=56 * 1024 * 1024
            ),
        )(table, coefs, lined)

    a_all, g_all, e_all = lax.cond(
        fits, pooled, direct, table, coefs, lined
    )

    screened, contrib = pl.pallas_call(
        functools.partial(entry_kernel, own, n_time),
        grid=(own,),
        out_shape=(
            jax.ShapeDtypeStruct((own, n_time, size, size), bf16),
            jax.ShapeDtypeStruct((own, n_tm, width), jnp.float32),
        ),
        in_specs=[
            pl.BlockSpec((n_tm, 1, size, width), lambda e: (0, e, 0, 0)),
            pl.BlockSpec((n_tm, 1, size, width), lambda e: (0, e, 0, 0)),
            pl.BlockSpec((n_tm, 2 * own, width // LINE, LINE), lambda e: (0, 0, 0, 0)),
            pl.BlockSpec((1, size, size), lambda e: (e, 0, 0)),
            smem, smem, smem,
        ],
        out_specs=(
            pl.BlockSpec((1, n_time, size, size), lambda e: (e, 0, 0, 0)),
            pl.BlockSpec((1, n_tm, width), lambda e: (e, 0, 0)),
        ),
        scratch_shapes=[pltpu.VMEM((n_time, n_tm, size, width), bf16)] * 2,
        compiler_params=pltpu.CompilerParams(vmem_limit_bytes=48 * 1024 * 1024),
    )(a_all, g_all, e_all, coulomb[0], cosine, tau_grid, my_owned)

    self_energy = pl.pallas_call(
        functools.partial(return_kernel, n_tm, n_pair, own),
        out_shape=jax.ShapeDtypeStruct((blocks, width), jnp.float32),
        in_specs=[smem, vmem, vmem],
        out_specs=vmem,
        scratch_shapes=[
            pltpu.VMEM((n_tm, 8, width), jnp.float32),
            pltpu.VMEM((n_tm, 8, width), jnp.float32),
            pltpu.VMEM((CAP * n_pair, width // LINE, LINE), jnp.float32),
            pltpu.VMEM((CAP * n_pair, width // LINE, LINE), jnp.float32),
            DMA((2,)),
            DMA((2,)),
        ],
        compiler_params=pltpu.CompilerParams(collective_id=1, has_side_effects=True),
    )(back, contrib, owning)
    return (screened[None], self_energy)


def solution(mesh):
    return jax.shard_map(
        functools.partial(body, mesh.shape["tm"], mesh.shape["pair"]),
        mesh=mesh,
        in_specs=(
            P("pair", None, "tm"),
            P("pair", "tm"),
            P("pair", "tm", None, None),
            P(),
            P(),
            P(),
        ),
        out_specs=(P("pair", "tm", None, None, None), P("pair", "tm")),
        check_vma=False,
    )
```

```python
import functools
import math

import jax
import jax.numpy as jnp
import numpy as np
from jax import lax
from jax.experimental import pallas as pl
from jax.experimental.pallas import tpu as pltpu
from jax.sharding import PartitionSpec as P

CAP = 2
CHUNKS = 4
PARTS = (16, 16, 32, 32, 32, 32, 32, 32, 16, 16)
FAST_CHUNKS = len(PARTS)
Y_CAP = 15
Z_CAPS = (10, 10, 9, 8)
LINE = 128
N_Y = 4
POOLS = 3
MESH = pl.DeviceIdType.MESH


def greet(n_tm, n_pair, my_tm, my_pair):
    barrier = pltpu.get_barrier_semaphore()

    def pair_peer(i, c):
        other = lax.rem(my_pair + i, n_pair)
        pl.semaphore_signal(barrier, inc=1, device_id=(my_tm, other), device_id_type=MESH)
        return c

    def tm_peer(i, c):
        other = lax.rem(my_tm + i, n_tm)
        pl.semaphore_signal(barrier, inc=1, device_id=(other, my_pair), device_id_type=MESH)
        return c

    lax.fori_loop(1, n_pair, pair_peer, 0)
    lax.fori_loop(1, n_tm, tm_peer, 0)
    pl.semaphore_wait(barrier, n_pair + n_tm - 2)


class View:
    def __init__(self, ref, at):
        self.ref, self.at = ref, at

    def __getitem__(self, i):
        return self.ref[self.at + i]


def views(table, listed, n_pair):
    sizes = (listed, listed, CAP * n_pair, listed, (N_Y - 1) * Y_CAP)
    at = [sum(sizes[:i]) for i in range(len(sizes) + 1)]
    return [View(table, i) for i in at]


def wait_bytes(ref, sem):
    pltpu.make_async_copy(ref, ref, sem).wait()


def gather_kernel(
    n_tm, n_pair, own, rows,
    table_ref, coef_ref, ener_ref,
    a_out, g_out, e_out,
    *scratch,
):
    slot_ref, local_ref, pick_ref = views(table_ref, n_tm * own, n_pair)[:3]
    my_tm, my_pair = lax.axis_index("tm"), lax.axis_index("pair")
    sends, recvs = scratch[:CHUNKS], scratch[CHUNKS : 2 * CHUNKS]
    (e_send, e_recv, a_send, g_send, x_ener,
     pair_send, pair_recv, a_sems, g_sems, e_sems, own_sems) = scratch[2 * CHUNKS :]
    peers, others = n_pair - 1, n_tm - 1
    step = rows // CHUNKS
    greet(n_tm, n_pair, my_tm, my_pair)

    def pair_copy(i, c):
        target = lax.rem(my_pair + i + 1, n_pair)
        return pltpu.make_async_remote_copy(
            src_ref=sends[c].at[pl.ds(CAP * i, CAP)],
            dst_ref=recvs[c].at[pl.ds(CAP * i, CAP)],
            send_sem=pair_send.at[c], recv_sem=pair_recv.at[c],
            device_id=(my_tm, target), device_id_type=MESH,
        )

    def ener_copy(i):
        target = lax.rem(my_pair + i + 1, n_pair)
        return pltpu.make_async_remote_copy(
            src_ref=e_send.at[pl.ds(CAP * i, CAP)], dst_ref=e_recv.at[pl.ds(CAP * i, CAP)],
            send_sem=pair_send.at[CHUNKS], recv_sem=pair_recv.at[CHUNKS],
            device_id=(my_tm, target), device_id_type=MESH,
        )


    def stage_a(u):
        owner = lax.rem(my_tm + u + 1, n_tm)
        for e in range(own):
            a_send[u, e] = coef_ref[local_ref[owner * own + e]]
        return owner

    def send_pair(c):
        def one(i, carry):
            for j in range(CAP):
                sends[c][CAP * i + j] = coef_ref[pick_ref[CAP * i + j], pl.ds(c * step, step), :]
            pair_copy(i, c).start()
            return carry

        lax.fori_loop(0, peers, one, 0)
        for j in range(CAP):
            recvs[c][CAP * peers + j] = coef_ref[pick_ref[CAP * peers + j], pl.ds(c * step, step), :]

    def send_ener(i, carry):
        for j in range(CAP):
            e_send[CAP * i + j] = ener_ref[pick_ref[CAP * i + j]]
        ener_copy(i).start()
        return carry

    def keep_ener():
        for j in range(CAP * peers, CAP * n_pair):
            e_recv[j] = ener_ref[pick_ref[j]]

    def a_one(u, carry):
        owner = stage_a(u)
        pltpu.make_async_remote_copy(
            src_ref=a_send.at[u], dst_ref=a_out.at[my_tm],
            send_sem=a_sems.at[0], recv_sem=a_sems.at[1],
            device_id=(owner, my_pair), device_id_type=MESH,
        ).start()
        return carry

    send_pair(0)
    lax.fori_loop(0, others, a_one, 0)
    stage_a(others)
    own_a = pltpu.make_async_copy(a_send.at[others], a_out.at[my_tm], own_sems.at[0])
    own_a.start()
    lax.fori_loop(0, peers, send_ener, 0)
    keep_ener()
    for c in range(1, CHUNKS):
        send_pair(c)

    owned_g = []
    for c in range(CHUNKS):
        wait_bytes(recvs[c].at[pl.ds(0, CAP * peers)], pair_recv.at[c])

        def stage_g(u):
            owner = lax.rem(my_tm + u + 1, n_tm)
            for e in range(own):
                g_send[c, u, e] = recvs[c][slot_ref[owner * own + e]]
            return owner

        def g_one(u, carry):
            owner = stage_g(u)
            pltpu.make_async_remote_copy(
                src_ref=g_send.at[c, u], dst_ref=g_out.at[my_tm, :, pl.ds(c * step, step)],
                send_sem=g_sems.at[0, c], recv_sem=g_sems.at[1, c],
                device_id=(owner, my_pair), device_id_type=MESH,
            ).start()
            return carry

        lax.fori_loop(0, others, g_one, 0)
        stage_g(others)
        copy = pltpu.make_async_copy(g_send.at[c, others], g_out.at[my_tm, :, pl.ds(c * step, step)], own_sems.at[1 + c])
        copy.start()
        owned_g.append(copy)
        if c == 0:
            wait_bytes(e_recv.at[pl.ds(0, CAP * peers)], pair_recv.at[CHUNKS])

            def stage_x(u):
                owner = lax.rem(my_tm + u + 1, n_tm)
                for e in range(own):
                    x_ener[u, e] = e_recv[slot_ref[owner * own + e]]
                    x_ener[u, own + e] = ener_ref[local_ref[owner * own + e]]
                return owner

            def x_one(u, carry):
                owner = stage_x(u)
                pltpu.make_async_remote_copy(
                    src_ref=x_ener.at[u], dst_ref=e_out.at[my_tm],
                    send_sem=e_sems.at[0], recv_sem=e_sems.at[1],
                    device_id=(owner, my_pair), device_id_type=MESH,
                ).start()
                return carry

            lax.fori_loop(0, others, x_one, 0)
            stage_x(others)
            own_e = pltpu.make_async_copy(x_ener.at[others], e_out.at[my_tm], own_sems.at[1 + CHUNKS])
            own_e.start()

    for c in range(CHUNKS):
        wait_bytes(sends[c].at[pl.ds(0, CAP * peers)], pair_send.at[c])
    wait_bytes(e_send.at[pl.ds(0, CAP * peers)], pair_send.at[CHUNKS])
    for side in range(2):
        wait_bytes(a_send.at[pl.ds(0, others)], a_sems.at[side])
        wait_bytes(x_ener.at[pl.ds(0, others)], e_sems.at[side])
        for c in range(CHUNKS):
            wait_bytes(g_send.at[c, pl.ds(0, others)], g_sems.at[side, c])
    own_a.wait()
    own_e.wait()
    for copy in owned_g:
        copy.wait()


def fast_kernel(
    n_tm, n_pair, own, rows,
    table_ref, coef_ref, ener_ref,
    a_out, g_out, e_out,
    y_send, y_recv, z_send, z_recv, e_send, e_recv, a_send, x_send, x_ener, *rest,
):
    slot_ref, local_ref, pick_ref, final_ref, y_ref, z_ref = views(table_ref, n_tm * own, n_pair)
    pools = rest[:POOLS]
    (y_ssem, y_rsem, z_ssem, z_rsem, pair_send, pair_recv, a_sems, g_sems, e_sems, own_sems) = rest[POOLS:]
    my_tm, my_pair = lax.axis_index("tm"), lax.axis_index("pair")
    peers, others = n_pair - 1, n_tm - 1
    n_z = n_pair // N_Y
    my_y, my_z = my_pair // n_z, lax.rem(my_pair, n_z)
    assert sum(PARTS) == rows
    begin = [sum(PARTS[:c]) for c in range(FAST_CHUNKS)]
    spans = [pl.ds(begin[c], PARTS[c]) for c in range(FAST_CHUNKS)]
    y_rows = [pl.ds(Y_CAP * begin[c], Y_CAP * PARTS[c]) for c in range(FAST_CHUNKS)]
    blocks, _, width = coef_ref.shape
    y_slots = (N_Y - 1) * Y_CAP
    ahead = (my_y * n_z + lax.rem(my_z + 1, n_z), my_y * n_z + lax.rem(my_z + n_z - 1, n_z))
    firsts = [sum(Z_CAPS[:r]) for r in range(len(Z_CAPS) + 1)]
    greet(n_tm, n_pair, my_tm, my_pair)

    def ener_copy(i):
        target = lax.rem(my_pair + i + 1, n_pair)
        return pltpu.make_async_remote_copy(
            src_ref=e_send.at[pl.ds(CAP * i, CAP)], dst_ref=e_recv.at[pl.ds(CAP * i, CAP)],
            send_sem=pair_send, recv_sem=pair_recv,
            device_id=(my_tm, target), device_id_type=MESH,
        )

    def send_ener(i, carry):
        for j in range(CAP):
            e_send[CAP * i + j] = ener_ref[pick_ref[CAP * i + j]]
        ener_copy(i).start()
        return carry

    def keep_ener():
        for j in range(CAP * peers, CAP * n_pair):
            e_recv[j] = ener_ref[pick_ref[j]]

    def send_y(c):
        for i in range(N_Y - 1):
            def one(j, carry):
                y_send[i, pl.ds(pl.multiple_of(Y_CAP * begin[c] + j * PARTS[c], 16), PARTS[c]), :] = coef_ref[y_ref[i * Y_CAP + j], spans[c], :]
                return carry

            lax.fori_loop(0, Y_CAP, one, 0)
            target = lax.rem(my_y + i + 1, N_Y) * n_z + my_z
            pltpu.make_async_remote_copy(
                src_ref=y_send.at[i, y_rows[c]], dst_ref=y_recv.at[i, y_rows[c]],
                send_sem=y_ssem, recv_sem=y_rsem.at[c],
                device_id=(my_tm, target), device_id_type=MESH,
            ).start()

    def fill(c):
        pool = pools[c % POOLS]
        held = pl.ds(0, PARTS[c])
        pool[pl.ds(0, blocks), held] = coef_ref[:, spans[c], :]
        wait_bytes(y_recv.at[:, y_rows[c]], y_rsem.at[c])
        for i in range(N_Y - 1):
            pool[pl.ds(blocks + i * Y_CAP, Y_CAP), held] = y_recv[i, y_rows[c]].reshape(Y_CAP, PARTS[c], width)

    def span(c, r, way):
        return (way, pl.ds(firsts[-1] * begin[c] + firsts[r] * PARTS[c], Z_CAPS[r] * PARTS[c]))

    def send_z(c, r):
        pool = pools[c % POOLS]
        for way in range(2):
            base = (2 * r + way) * Z_CAPS[0]

            def one(j, carry):
                at = firsts[-1] * begin[c] + (firsts[r] + j) * PARTS[c]
                z_send[way, pl.ds(pl.multiple_of(at, 16), PARTS[c]), :] = pool[z_ref[base + j], pl.ds(0, PARTS[c])]
                return carry

            lax.fori_loop(0, Z_CAPS[r], one, 0)
            pltpu.make_async_remote_copy(
                src_ref=z_send.at[span(c, r, way)], dst_ref=z_recv.at[span(c, r, way)],
                send_sem=z_ssem, recv_sem=z_rsem.at[c, r, way],
                device_id=(my_tm, ahead[way]), device_id_type=MESH,
            ).start()

    def take_z(c, r):
        pool = pools[c % POOLS]
        for way in range(2):
            wait_bytes(z_recv.at[span(c, r, way)], z_rsem.at[c, r, way])
            at = blocks + y_slots + way * firsts[-1] + firsts[r]
            pool[pl.ds(at, Z_CAPS[r]), pl.ds(0, PARTS[c])] = z_recv[span(c, r, way)].reshape(Z_CAPS[r], PARTS[c], width)

    def stage_a(u):
        owner = lax.rem(my_tm + u + 1, n_tm)
        for e in range(own):
            a_send[u, e] = coef_ref[local_ref[owner * own + e]]
        return owner

    def a_one(u, carry):
        owner = stage_a(u)
        pltpu.make_async_remote_copy(
            src_ref=a_send.at[u], dst_ref=a_out.at[my_tm],
            send_sem=a_sems.at[0], recv_sem=a_sems.at[1],
            device_id=(owner, my_pair), device_id_type=MESH,
        ).start()
        return carry

    def send_x(c):
        pool = pools[c % POOLS]
        part = spans[c]

        def stage_g(u):
            owner = lax.rem(my_tm + u + 1, n_tm)
            for e in range(own):
                x_send[u, e, part] = pool[final_ref[owner * own + e], pl.ds(0, PARTS[c])]
            return owner

        def g_one(u, carry):
            owner = stage_g(u)
            pltpu.make_async_remote_copy(
                src_ref=x_send.at[u, :, part], dst_ref=g_out.at[my_tm, :, part],
                send_sem=g_sems.at[0, c], recv_sem=g_sems.at[1, c],
                device_id=(owner, my_pair), device_id_type=MESH,
            ).start()
            return carry

        lax.fori_loop(0, others, g_one, 0)
        stage_g(others)
        pltpu.make_async_copy(x_send.at[others, :, part], g_out.at[my_tm, :, part], own_sems.at[1 + c]).start()

    def send_x_ener():
        wait_bytes(e_recv.at[pl.ds(0, CAP * peers)], pair_recv)

        def stage_x(u):
            owner = lax.rem(my_tm + u + 1, n_tm)
            for e in range(own):
                x_ener[u, e] = e_recv[slot_ref[owner * own + e]]
                x_ener[u, own + e] = ener_ref[local_ref[owner * own + e]]
            return owner

        def x_one(u, carry):
            owner = stage_x(u)
            pltpu.make_async_remote_copy(
                src_ref=x_ener.at[u], dst_ref=e_out.at[my_tm],
                send_sem=e_sems.at[0], recv_sem=e_sems.at[1],
                device_id=(owner, my_pair), device_id_type=MESH,
            ).start()
            return carry

        lax.fori_loop(0, others, x_one, 0)
        stage_x(others)
        pltpu.make_async_copy(x_ener.at[others], e_out.at[my_tm], own_sems.at[1 + FAST_CHUNKS]).start()

    def own_a():
        stage_a(others)
        pltpu.make_async_copy(a_send.at[others], a_out.at[my_tm], own_sems.at[0]).start()

    tasks = [functools.partial(lax.fori_loop, u, u + 1, a_one, 0) for u in range(others)]
    tasks.append(own_a)
    few = 4
    for i in range(0, peers, few):
        tasks.append(functools.partial(lax.fori_loop, i, min(i + few, peers), send_ener, 0))
    tasks.append(keep_ener)

    def spare():
        if tasks:
            tasks.pop(0)()

    last = len(Z_CAPS) - 1
    sent_ener = False
    send_y(0)
    send_y(1)
    fill(0)
    send_z(0, 0)
    send_y(2)
    fill(1)
    send_z(1, 0)
    send_y(3)
    spare()
    for first in range(0, FAST_CHUNKS, 2):
        second = first + 1
        more = first + 2 < FAST_CHUNKS
        for r in range(last):
            take_z(first, r)
            send_z(first, r + 1)
            spare()
            take_z(second, r)
            send_z(second, r + 1)
            spare()
            if first + 4 + r < FAST_CHUNKS and r < 2:
                send_y(first + 4 + r)
        if more:
            fill(first + 2)
            send_z(first + 2, 0)
        take_z(first, last)
        send_x(first)
        if more:
            fill(first + 3)
            send_z(first + 3, 0)
        take_z(second, last)
        send_x(second)
        if not tasks and not sent_ener:
            sent_ener = True
            send_x_ener()
    assert sent_ener

    wait_bytes(y_send, y_ssem)
    wait_bytes(z_send, z_ssem)
    wait_bytes(e_send.at[pl.ds(0, CAP * peers)], pair_send)
    pltpu.make_async_copy(a_send.at[others], a_out.at[my_tm], own_sems.at[0]).wait()
    for side in range(2):
        wait_bytes(a_send.at[pl.ds(0, others)], a_sems.at[side])
        wait_bytes(x_ener.at[pl.ds(0, others)], e_sems.at[side])
        for c in range(FAST_CHUNKS):
            wait_bytes(x_send.at[pl.ds(0, others), :, spans[c]], g_sems.at[side, c])
    for c in range(FAST_CHUNKS):
        part = spans[c]
        pltpu.make_async_copy(x_send.at[others, :, part], g_out.at[my_tm, :, part], own_sems.at[1 + c]).wait()
    pltpu.make_async_copy(x_ener.at[others], e_out.at[my_tm], own_sems.at[1 + FAST_CHUNKS]).wait()


def half_way(n_z, z_key):
    half = n_z // 2
    node = np.arange(n_z)
    gap = (node[:, None] - node[None, :]) % n_z
    count = jnp.sum((z_key[:, None, :] == node[None, :, None]).astype(jnp.int32), axis=2)
    count = count.reshape(N_Y, 1, n_z * n_z)
    busy = []
    for way in range(2):
        trip = gap if way == 0 else (-gap) % n_z
        hops = gap.T if way == 0 else (-gap.T) % n_z
        passes = (trip[None] < half) & (hops.T[:, None, :] < trip[None])
        load = jnp.sum(jnp.where(passes.reshape(1, n_z, n_z * n_z), count, 0), axis=2)
        near = (hops if way == 0 else hops) < half
        busy.append(jnp.max(jnp.where(near[None], load[:, None, :], 0), axis=2))
    opposite = (gap == half).reshape(n_z, n_z)
    there = jnp.sum(jnp.where(opposite[None], count.reshape(N_Y, n_z, n_z), 0), axis=1)
    even = ((np.arange(N_Y)[:, None] + node[None, :]) % 2 == 0).astype(np.int32)
    return jnp.clip((there * 32 + 8 * (busy[1] - busy[0]) + 32 * even) // 64, 0, there)


def routes(n_pair, blocks, my_pair, live, source, held, rank):
    listed = live.shape[1]
    n_z = n_pair // N_Y
    n = n_z * listed
    my_y, my_z = my_pair // n_z, my_pair % n_z
    rows = jnp.arange(n_pair, dtype=jnp.int32)
    mine = source == my_pair
    per_row = jnp.sum(mine.astype(jnp.int32), axis=1)
    same = (rows[:, None] // n_z == rows[None, :] // n_z) & (rows[None, :] < rows[:, None])
    first = jnp.sum(jnp.where(same, per_row[None, :], 0), axis=1)
    place = jnp.where(mine, first[:, None] + rank, -1).reshape(N_Y, 1, n)
    want = jnp.arange(Y_CAP, dtype=jnp.int32)[None, :, None]
    y_tab = jnp.sum(jnp.where(place == want, held.reshape(N_Y, 1, n), 0), axis=2)
    y_tab = lax.dynamic_slice_in_dim(jnp.concatenate([y_tab, y_tab]), my_y + 1, N_Y - 1)
    ring_source = source.reshape(N_Y, n)
    ids = jnp.arange(n, dtype=jnp.int32)
    earlier = ids[None, :] < ids[:, None]
    y_same = (ring_source[:, :, None] == ring_source[:, None, :]) & earlier[None]
    y_rank = jnp.sum(y_same.astype(jnp.int32), axis=2)
    off_ring = live.reshape(N_Y, n) & (ring_source // n_z != jnp.arange(N_Y)[:, None])
    y_over = jnp.where(off_ring, y_rank, 0) - (Y_CAP - 1)

    pos_in = jnp.arange(listed, dtype=jnp.int32)
    z_key = jnp.where(live, source % n_z, -1)
    z_same = (z_key[:, :, None] == z_key[:, None, :]) & (pos_in[None, :] < pos_in[:, None])[None]
    z_rank = jnp.sum(z_same.astype(jnp.int32), axis=2).reshape(N_Y, n)
    zd = ids // listed
    zs = ring_source % n_z
    delta = (zd[None, :] - zs) % n_z
    half = n_z // 2
    share = half_way(n_z, z_key)
    mine_share = jnp.sum(jnp.where(zs[:, :, None] == jnp.arange(n_z)[None, None, :], share[:, None, :], 0), axis=2)
    plus = (delta < half) | ((delta == half) & (z_rank < mine_share))
    way = jnp.where(plus, 0, 1)
    rem = jnp.where(live.reshape(N_Y, n), jnp.where(plus, delta, n_z - delta), 0)
    pos = zs

    ring = lambda v: lax.dynamic_index_in_dim(v, my_y, 0, keepdims=False)
    src, my_way = ring(ring_source), ring(way)
    step_y = (my_y - src // n_z) % N_Y
    loc = jnp.where(step_y == 0, ring(held.reshape(N_Y, n)), blocks + (step_y - 1) * Y_CAP + ring(y_rank))
    loc = jnp.where(src >= 0, loc, 0)
    total = sum(Z_CAPS)
    tables, begun = [], 0
    slots = jnp.arange(Z_CAPS[0], dtype=jnp.int32)
    for cap in Z_CAPS:
        group = jnp.where(rem > 0, pos * 2 + way, -1)
        key = rem * n - ids[None, :]
        ahead = (group[:, :, None] == group[:, None, :]) & (key[:, None, :] > key[:, :, None])
        order = jnp.sum(ahead.astype(jnp.int32), axis=2)
        moved = (rem > 0) & (order < cap)
        my_order, my_moved, my_group = ring(order), ring(moved), ring(group)
        for w in range(2):
            here = jnp.where(my_moved & (my_group == my_z * 2 + w), my_order, -1)
            tables.append(jnp.sum(jnp.where(here[None, :] == slots[:, None], loc[None, :], 0), axis=1))
        loc = jnp.where(my_moved, blocks + (N_Y - 1) * Y_CAP + my_way * total + begun + my_order, loc)
        pos = jnp.where(moved, (pos + jnp.where(plus, 1, n_z - 1)) % n_z, pos)
        rem = rem - moved.astype(jnp.int32)
        begun += cap
    final = lax.dynamic_slice_in_dim(loc, my_z * listed, listed)
    fits = jnp.maximum(jnp.max(rem), jnp.max(y_over)) <= 0
    return fits, y_tab.reshape(-1), jnp.concatenate(tables), final


def entry_kernel(own, n_time, a_ref, g_ref, e_ref, tile_ref, cos_ref, tau_ref, live_ref, w_ref, c_ref, x_ref, y_ref, s_ref):
    e = pl.program_id(0)
    slices, _, size, width = a_ref.shape
    live = live_ref[e]
    lines = lambda v: jnp.concatenate([v[i : i + 1] for i in range(v.shape[0])], axis=1)
    for m in range(slices):
        span = pl.ds(m * width, width)
        x_ref[:, span] = a_ref[m, 0]
        rate = lines(e_ref[m, e] + e_ref[m, own + e])
        g = g_ref[m, 0].astype(jnp.float32)
        for t in range(n_time):
            decay = jnp.exp(-tau_ref[t] * rate)
            s_ref[pl.ds(t, 1), span] = decay
            y_ref[t, :, span] = (g * decay).astype(jnp.bfloat16)
    chi = []
    for t in range(n_time):
        chi.append(live * lax.dot_general(
            x_ref[...], y_ref[t], (((1,), (1,)), ((), ())), preferred_element_type=jnp.float32
        ))
    wfreq = []
    for w in range(n_time):
        chiw = sum(cos_ref[w, t] * chi[t] for t in range(n_time)).astype(jnp.bfloat16)
        prod = jnp.dot(chiw, tile_ref[0], preferred_element_type=jnp.float32)
        prod_b = prod.astype(jnp.bfloat16)
        wfreq.append(
            prod + jnp.dot(prod_b, prod_b, preferred_element_type=jnp.float32) * (1.0 / math.sqrt(size))
        )
    for t in range(n_time):
        w_ref[0, t] = (sum(cos_ref[w, t] * wfreq[w] for w in range(n_time)) * (1.0 / n_time)).astype(jnp.bfloat16)
    screened = w_ref[0].reshape(n_time * size, size)
    for m in range(slices):
        span = pl.ds(m * width, width)
        wy = jnp.dot(screened, g_ref[m, 0], preferred_element_type=jnp.float32)
        a = a_ref[m, 0].astype(jnp.float32)
        total = jnp.zeros((1, width), jnp.float32)
        for t in range(n_time):
            part = jnp.sum(a * wy[t * size : (t + 1) * size], axis=0, keepdims=True)
            total = total + s_ref[pl.ds(t, 1), span] * part
        c_ref[0, pl.ds(m, 1), :] = total * (1.0 / n_time)


def return_kernel(
    n_tm, n_pair, own,
    back_ref, contrib_ref, owning_ref,
    out_ref,
    c_send, c_recv, p_send, p_recv, tm_sems, pair_sems,
):
    my_tm, my_pair = lax.axis_index("tm"), lax.axis_index("pair")
    peers, others = n_pair - 1, n_tm - 1
    width = out_ref.shape[1]
    c_send[...] = jnp.zeros_like(c_send)
    greet(n_tm, n_pair, my_tm, my_pair)

    def stage_c(u):
        owner = lax.rem(my_tm + u + 1, n_tm)
        for e in range(own):
            c_send[u, pl.ds(e, 1), :] = contrib_ref[e, pl.ds(owner, 1), :]
        return owner

    def tm_one(u, carry):
        owner = stage_c(u)
        pltpu.make_async_remote_copy(
            src_ref=c_send.at[u], dst_ref=c_recv.at[u],
            send_sem=tm_sems.at[0], recv_sem=tm_sems.at[1],
            device_id=(owner, my_pair), device_id_type=MESH,
        ).start()
        return carry

    lax.fori_loop(0, others, tm_one, 0)
    stage_c(others)
    wait_bytes(c_recv.at[pl.ds(0, others)], tm_sems.at[1])
    c_recv[others] = c_send[others]

    def stage_p(i):
        for j in range(CAP):
            at = back_ref[CAP * i + j]
            keep = jnp.where(at >= 0, 1.0, 0.0)
            at = jnp.maximum(at, 0)
            line = c_recv[at // own, pl.ds(lax.rem(at, own), 1), :] * keep
            for h in range(width // LINE):
                p_send[CAP * i + j, pl.ds(h, 1), :] = line[:, h * LINE : (h + 1) * LINE]

    def pair_one(i, carry):
        stage_p(i)
        target = lax.rem(my_pair + n_pair - 1 - i, n_pair)
        pltpu.make_async_remote_copy(
            src_ref=p_send.at[pl.ds(CAP * i, CAP)], dst_ref=p_recv.at[pl.ds(CAP * i, CAP)],
            send_sem=pair_sems.at[0], recv_sem=pair_sems.at[1],
            device_id=(my_tm, target), device_id_type=MESH,
        ).start()
        return carry

    lax.fori_loop(0, peers, pair_one, 0)
    stage_p(peers)
    wait_bytes(p_recv.at[pl.ds(0, CAP * peers)], pair_sems.at[1])
    for j in range(CAP * peers, CAP * n_pair):
        p_recv[j] = p_send[j]
    for h in range(width // LINE):
        out_ref[:, pl.ds(h * LINE, LINE)] = jnp.dot(
            owning_ref[...], p_recv[:, h, :], precision=lax.Precision.HIGHEST, preferred_element_type=jnp.float32
        )
    wait_bytes(c_send.at[pl.ds(0, others)], tm_sems.at[0])
    wait_bytes(p_send.at[pl.ds(0, CAP * peers)], pair_sems.at[0])


def body(n_tm, n_pair, coefs, energies, coulomb, tau_grid, freq_grid, pairs):
    blocks, size, width = coefs.shape
    n_time = tau_grid.shape[0]
    listed = pairs.shape[1]
    own = listed // n_tm
    my_tm, my_pair = lax.axis_index("tm"), lax.axis_index("pair")
    remote, local = pairs[:, :, 0], pairs[:, :, 1]
    live = remote >= 0
    source = jnp.where(live, remote // blocks, -1)
    held = remote % blocks
    pos = jnp.arange(listed, dtype=jnp.int32)
    before = (source[:, :, None] == source[:, None, :]) & (pos[None, :] < pos[:, None])[None]
    rank = jnp.sum(before.astype(jnp.int32), axis=2)
    slots = jnp.arange(CAP, dtype=jnp.int32)
    hit = (source == my_pair)[:, None, :] & (rank[:, None, :] == slots[None, :, None])
    pick = jnp.sum(jnp.where(hit, held[:, None, :], 0), axis=2)
    used = jnp.sum(hit.astype(jnp.int32), axis=2)
    turn = lambda v: lax.dynamic_slice_in_dim(jnp.concatenate([v, v]), my_pair + 1, n_pair)
    pick, used = turn(pick), turn(used)
    row = lambda v: lax.dynamic_index_in_dim(v, my_pair, 0, keepdims=False)
    my_live, my_source, my_rank = row(live), row(source), row(rank)
    my_local = jnp.where(my_live, row(local), 0)
    offset = (my_pair - my_source + n_pair - 1) % n_pair
    slot = jnp.where(my_live, offset * CAP + my_rank, 0)
    lane = jnp.arange(n_pair * CAP, dtype=jnp.int32)
    match = (slot[None, :] == lane[:, None]) & my_live[None, :]
    back = jnp.sum(jnp.where(match, pos[None, :], 0), axis=1)
    back = ((my_tm - back // own + n_tm - 1) % n_tm) * own + back % own
    back = jnp.where(jnp.any(match, axis=1), back, -1)
    given = jnp.where(used > 0, pick, -1).reshape(1, -1)
    owning = (jnp.arange(blocks, dtype=jnp.int32)[:, None] == given).astype(jnp.float32)
    my_owned = lax.dynamic_slice_in_dim(my_live, my_tm * own, own).astype(jnp.float32)
    cosine = jnp.cos(freq_grid[:, None] * tau_grid[None, :])
    lined = energies.astype(jnp.float32).reshape(blocks, width // LINE, LINE)

    smem = pl.BlockSpec(memory_space=pltpu.SMEM)
    vmem = pl.BlockSpec(memory_space=pltpu.VMEM)
    hbm = pl.BlockSpec(memory_space=pl.ANY)
    bf16 = jnp.bfloat16
    DMA = pltpu.SemaphoreType.DMA
    step = size // CHUNKS
    thin = size // FAST_CHUNKS
    gathered = (
        jax.ShapeDtypeStruct((n_tm, own, size, width), bf16),
        jax.ShapeDtypeStruct((n_tm, own, size, width), bf16),
        jax.ShapeDtypeStruct((n_tm, 2 * own, width // LINE, LINE), jnp.float32),
    )
    fits, y_tab, z_tab, final = routes(n_pair, blocks, my_pair, live, source, held, rank)
    table = jnp.concatenate([slot, my_local, pick.reshape(-1), final, y_tab, z_tab]).astype(jnp.int32)

    def pooled(table, coefs, lined):
        total = sum(Z_CAPS)
        depth = blocks + (N_Y - 1) * Y_CAP + 2 * total
        return pl.pallas_call(
            functools.partial(fast_kernel, n_tm, n_pair, own, size),
            out_shape=gathered,
            in_specs=[smem] + [vmem] * 2,
            out_specs=(hbm, hbm, hbm),
            scratch_shapes=[pltpu.VMEM((N_Y - 1, Y_CAP * size, width), bf16)] * 2
            + [pltpu.VMEM((2, total * size, width), bf16)] * 2
            + [
                pltpu.VMEM((CAP * n_pair, width // LINE, LINE), jnp.float32),
                pltpu.VMEM((CAP * n_pair, width // LINE, LINE), jnp.float32),
                pltpu.VMEM((n_tm, own, size, width), bf16),
                pltpu.VMEM((n_tm, own, size, width), bf16),
                pltpu.VMEM((n_tm, 2 * own, width // LINE, LINE), jnp.float32),
            ]
            + [pltpu.VMEM((depth, max(PARTS), width), bf16)] * POOLS
            + [
                DMA,
                DMA((FAST_CHUNKS,)),
                DMA,
                DMA((FAST_CHUNKS, len(Z_CAPS), 2)),
                DMA,
                DMA,
                DMA((2,)),
                DMA((2, FAST_CHUNKS)),
                DMA((2,)),
                DMA((2 + FAST_CHUNKS,)),
            ],
            compiler_params=pltpu.CompilerParams(
                collective_id=2, has_side_effects=True, vmem_limit_bytes=62 * 1024 * 1024
            ),
        )(table, coefs, lined)

    def direct(table, coefs, lined):
        return pl.pallas_call(
            functools.partial(gather_kernel, n_tm, n_pair, own, size),
            out_shape=gathered,
            in_specs=[smem] + [vmem] * 2,
            out_specs=(hbm, hbm, hbm),
            scratch_shapes=[pltpu.VMEM((CAP * n_pair, step, width), bf16)] * (2 * CHUNKS)
            + [
                pltpu.VMEM((CAP * n_pair, width // LINE, LINE), jnp.float32),
                pltpu.VMEM((CAP * n_pair, width // LINE, LINE), jnp.float32),
                pltpu.VMEM((n_tm, own, size, width), bf16),
                pltpu.VMEM((CHUNKS, n_tm, own, step, width), bf16),
                pltpu.VMEM((n_tm, 2 * own, width // LINE, LINE), jnp.float32),
                DMA((CHUNKS + 1,)),
                DMA((CHUNKS + 1,)),
                DMA((2,)),
                DMA((2, CHUNKS)),
                DMA((2,)),
                DMA((2 + CHUNKS,)),
            ],
            compiler_params=pltpu.CompilerParams(
                collective_id=0, has_side_effects=True, vmem_limit_bytes=56 * 1024 * 1024
            ),
        )(table, coefs, lined)

    a_all, g_all, e_all = lax.cond(
        fits, pooled, direct, table, coefs, lined
    )

    screened, contrib = pl.pallas_call(
        functools.partial(entry_kernel, own, n_time),
        grid=(own,),
        out_shape=(
            jax.ShapeDtypeStruct((own, n_time, size, size), bf16),
            jax.ShapeDtypeStruct((own, n_tm, width), jnp.float32),
        ),
        in_specs=[
            pl.BlockSpec((n_tm, 1, size, width), lambda e: (0, e, 0, 0)),
            pl.BlockSpec((n_tm, 1, size, width), lambda e: (0, e, 0, 0)),
            pl.BlockSpec((n_tm, 2 * own, width // LINE, LINE), lambda e: (0, 0, 0, 0)),
            pl.BlockSpec((1, size, size), lambda e: (e, 0, 0)),
            smem, smem, smem,
        ],
        out_specs=(
            pl.BlockSpec((1, n_time, size, size), lambda e: (e, 0, 0, 0)),
            pl.BlockSpec((1, n_tm, width), lambda e: (e, 0, 0)),
        ),
        scratch_shapes=[
            pltpu.VMEM((size, n_tm * width), bf16),
            pltpu.VMEM((n_time, size, n_tm * width), bf16),
            pltpu.VMEM((8, n_tm * width), jnp.float32),
        ],
        compiler_params=pltpu.CompilerParams(vmem_limit_bytes=48 * 1024 * 1024),
    )(a_all, g_all, e_all, coulomb[0], cosine, tau_grid, my_owned)

    self_energy = pl.pallas_call(
        functools.partial(return_kernel, n_tm, n_pair, own),
        out_shape=jax.ShapeDtypeStruct((blocks, width), jnp.float32),
        in_specs=[smem, vmem, vmem],
        out_specs=vmem,
        scratch_shapes=[
            pltpu.VMEM((n_tm, 8, width), jnp.float32),
            pltpu.VMEM((n_tm, 8, width), jnp.float32),
            pltpu.VMEM((CAP * n_pair, width // LINE, LINE), jnp.float32),
            pltpu.VMEM((CAP * n_pair, width // LINE, LINE), jnp.float32),
            DMA((2,)),
            DMA((2,)),
        ],
        compiler_params=pltpu.CompilerParams(collective_id=1, has_side_effects=True),
    )(back, contrib, owning)
    return (screened[None], self_energy)


def solution(mesh):
    return jax.shard_map(
        functools.partial(body, mesh.shape["tm"], mesh.shape["pair"]),
        mesh=mesh,
        in_specs=(
            P("pair", None, "tm"),
            P("pair", "tm"),
            P("pair", "tm", None, None),
            P(),
            P(),
            P(),
        ),
        out_specs=(P("pair", "tm", None, None, None), P("pair", "tm")),
        check_vma=False,
    )
```

```python
import functools
import math

import jax
import jax.numpy as jnp
import numpy as np
from jax import lax
from jax.experimental import pallas as pl
from jax.experimental.pallas import tpu as pltpu
from jax.sharding import PartitionSpec as P

CAP = 2
CHUNKS = 4
PARTS = (16, 16, 32, 32, 32, 32, 32, 32, 16, 16)
FAST_CHUNKS = len(PARTS)
Y_CAP = 15
Z_CAPS = (10, 10, 9, 8)
LINE = 128
N_Y = 4
POOLS = 3
MESH = pl.DeviceIdType.MESH


def greet(n_tm, n_pair, my_tm, my_pair):
    barrier = pltpu.get_barrier_semaphore()

    def pair_peer(i, c):
        other = lax.rem(my_pair + i, n_pair)
        pl.semaphore_signal(barrier, inc=1, device_id=(my_tm, other), device_id_type=MESH)
        return c

    def tm_peer(i, c):
        other = lax.rem(my_tm + i, n_tm)
        pl.semaphore_signal(barrier, inc=1, device_id=(other, my_pair), device_id_type=MESH)
        return c

    lax.fori_loop(1, n_pair, pair_peer, 0)
    lax.fori_loop(1, n_tm, tm_peer, 0)
    pl.semaphore_wait(barrier, n_pair + n_tm - 2)


class View:
    def __init__(self, ref, at):
        self.ref, self.at = ref, at

    def __getitem__(self, i):
        return self.ref[self.at + i]


def views(table, listed, n_pair):
    sizes = (listed, listed, CAP * n_pair, listed, (N_Y - 1) * Y_CAP)
    at = [sum(sizes[:i]) for i in range(len(sizes) + 1)]
    return [View(table, i) for i in at]


def wait_bytes(ref, sem):
    pltpu.make_async_copy(ref, ref, sem).wait()


def gather_kernel(
    n_tm, n_pair, own, rows,
    table_ref, coef_ref, ener_ref,
    a_out, g_out, e_out,
    *scratch,
):
    slot_ref, local_ref, pick_ref = views(table_ref, n_tm * own, n_pair)[:3]
    my_tm, my_pair = lax.axis_index("tm"), lax.axis_index("pair")
    sends, recvs = scratch[:CHUNKS], scratch[CHUNKS : 2 * CHUNKS]
    (e_send, e_recv, a_send, g_send, x_ener,
     pair_send, pair_recv, a_sems, g_sems, e_sems, own_sems) = scratch[2 * CHUNKS :]
    peers, others = n_pair - 1, n_tm - 1
    step = rows // CHUNKS
    greet(n_tm, n_pair, my_tm, my_pair)

    def pair_copy(i, c):
        target = lax.rem(my_pair + i + 1, n_pair)
        return pltpu.make_async_remote_copy(
            src_ref=sends[c].at[pl.ds(CAP * i, CAP)],
            dst_ref=recvs[c].at[pl.ds(CAP * i, CAP)],
            send_sem=pair_send.at[c], recv_sem=pair_recv.at[c],
            device_id=(my_tm, target), device_id_type=MESH,
        )

    def ener_copy(i):
        target = lax.rem(my_pair + i + 1, n_pair)
        return pltpu.make_async_remote_copy(
            src_ref=e_send.at[pl.ds(CAP * i, CAP)], dst_ref=e_recv.at[pl.ds(CAP * i, CAP)],
            send_sem=pair_send.at[CHUNKS], recv_sem=pair_recv.at[CHUNKS],
            device_id=(my_tm, target), device_id_type=MESH,
        )


    def stage_a(u):
        owner = lax.rem(my_tm + u + 1, n_tm)
        for e in range(own):
            a_send[u, e] = coef_ref[local_ref[owner * own + e]]
        return owner

    def send_pair(c):
        def one(i, carry):
            for j in range(CAP):
                sends[c][CAP * i + j] = coef_ref[pick_ref[CAP * i + j], pl.ds(c * step, step), :]
            pair_copy(i, c).start()
            return carry

        lax.fori_loop(0, peers, one, 0)
        for j in range(CAP):
            recvs[c][CAP * peers + j] = coef_ref[pick_ref[CAP * peers + j], pl.ds(c * step, step), :]

    def send_ener(i, carry):
        for j in range(CAP):
            e_send[CAP * i + j] = ener_ref[pick_ref[CAP * i + j]]
        ener_copy(i).start()
        return carry

    def keep_ener():
        for j in range(CAP * peers, CAP * n_pair):
            e_recv[j] = ener_ref[pick_ref[j]]

    def a_one(u, carry):
        owner = stage_a(u)
        pltpu.make_async_remote_copy(
            src_ref=a_send.at[u], dst_ref=a_out.at[my_tm],
            send_sem=a_sems.at[0], recv_sem=a_sems.at[1],
            device_id=(owner, my_pair), device_id_type=MESH,
        ).start()
        return carry

    send_pair(0)
    lax.fori_loop(0, others, a_one, 0)
    stage_a(others)
    own_a = pltpu.make_async_copy(a_send.at[others], a_out.at[my_tm], own_sems.at[0])
    own_a.start()
    lax.fori_loop(0, peers, send_ener, 0)
    keep_ener()
    for c in range(1, CHUNKS):
        send_pair(c)

    owned_g = []
    for c in range(CHUNKS):
        wait_bytes(recvs[c].at[pl.ds(0, CAP * peers)], pair_recv.at[c])

        def stage_g(u):
            owner = lax.rem(my_tm + u + 1, n_tm)
            for e in range(own):
                g_send[c, u, e] = recvs[c][slot_ref[owner * own + e]]
            return owner

        def g_one(u, carry):
            owner = stage_g(u)
            pltpu.make_async_remote_copy(
                src_ref=g_send.at[c, u], dst_ref=g_out.at[my_tm, :, pl.ds(c * step, step)],
                send_sem=g_sems.at[0, c], recv_sem=g_sems.at[1, c],
                device_id=(owner, my_pair), device_id_type=MESH,
            ).start()
            return carry

        lax.fori_loop(0, others, g_one, 0)
        stage_g(others)
        copy = pltpu.make_async_copy(g_send.at[c, others], g_out.at[my_tm, :, pl.ds(c * step, step)], own_sems.at[1 + c])
        copy.start()
        owned_g.append(copy)
        if c == 0:
            wait_bytes(e_recv.at[pl.ds(0, CAP * peers)], pair_recv.at[CHUNKS])

            def stage_x(u):
                owner = lax.rem(my_tm + u + 1, n_tm)
                for e in range(own):
                    x_ener[u, e] = e_recv[slot_ref[owner * own + e]]
                    x_ener[u, own + e] = ener_ref[local_ref[owner * own + e]]
                return owner

            def x_one(u, carry):
                owner = stage_x(u)
                pltpu.make_async_remote_copy(
                    src_ref=x_ener.at[u], dst_ref=e_out.at[my_tm],
                    send_sem=e_sems.at[0], recv_sem=e_sems.at[1],
                    device_id=(owner, my_pair), device_id_type=MESH,
                ).start()
                return carry

            lax.fori_loop(0, others, x_one, 0)
            stage_x(others)
            own_e = pltpu.make_async_copy(x_ener.at[others], e_out.at[my_tm], own_sems.at[1 + CHUNKS])
            own_e.start()

    for c in range(CHUNKS):
        wait_bytes(sends[c].at[pl.ds(0, CAP * peers)], pair_send.at[c])
    wait_bytes(e_send.at[pl.ds(0, CAP * peers)], pair_send.at[CHUNKS])
    for side in range(2):
        wait_bytes(a_send.at[pl.ds(0, others)], a_sems.at[side])
        wait_bytes(x_ener.at[pl.ds(0, others)], e_sems.at[side])
        for c in range(CHUNKS):
            wait_bytes(g_send.at[c, pl.ds(0, others)], g_sems.at[side, c])
    own_a.wait()
    own_e.wait()
    for copy in owned_g:
        copy.wait()


def fast_kernel(
    n_tm, n_pair, own, rows,
    table_ref, coef_hbm, ener_ref,
    a_out, g_out, e_out,
    coef_ref, y_send, y_recv, z_send, z_recv, e_send, e_recv, a_send, x_send, x_ener, *rest,
):
    slot_ref, local_ref, pick_ref, final_ref, y_ref, z_ref = views(table_ref, n_tm * own, n_pair)
    pools = rest[:POOLS]
    (y_ssem, y_rsem, z_ssem, z_rsem, pair_send, pair_recv, a_sems, g_sems, e_sems, own_sems) = rest[POOLS:]
    my_tm, my_pair = lax.axis_index("tm"), lax.axis_index("pair")
    peers, others = n_pair - 1, n_tm - 1
    n_z = n_pair // N_Y
    my_y, my_z = my_pair // n_z, lax.rem(my_pair, n_z)
    assert sum(PARTS) == rows
    begin = [sum(PARTS[:c]) for c in range(FAST_CHUNKS)]
    spans = [pl.ds(begin[c], PARTS[c]) for c in range(FAST_CHUNKS)]
    y_rows = [pl.ds(Y_CAP * begin[c], Y_CAP * PARTS[c]) for c in range(FAST_CHUNKS)]
    blocks, _, width = coef_ref.shape
    y_slots = (N_Y - 1) * Y_CAP
    ahead = (my_y * n_z + lax.rem(my_z + 1, n_z), my_y * n_z + lax.rem(my_z + n_z - 1, n_z))
    firsts = [sum(Z_CAPS[:r]) for r in range(len(Z_CAPS) + 1)]
    load = pltpu.make_async_copy(coef_hbm, coef_ref, own_sems.at[2 + FAST_CHUNKS])
    load.start()
    greet(n_tm, n_pair, my_tm, my_pair)
    load.wait()

    def ener_copy(i):
        target = lax.rem(my_pair + i + 1, n_pair)
        return pltpu.make_async_remote_copy(
            src_ref=e_send.at[pl.ds(CAP * i, CAP)], dst_ref=e_recv.at[pl.ds(CAP * i, CAP)],
            send_sem=pair_send, recv_sem=pair_recv,
            device_id=(my_tm, target), device_id_type=MESH,
        )

    def send_ener(i, carry):
        for j in range(CAP):
            e_send[CAP * i + j] = ener_ref[pick_ref[CAP * i + j]]
        ener_copy(i).start()
        return carry

    def keep_ener():
        for j in range(CAP * peers, CAP * n_pair):
            e_recv[j] = ener_ref[pick_ref[j]]

    def send_y(c):
        for i in range(N_Y - 1):
            def one(j, carry):
                y_send[i, pl.ds(pl.multiple_of(Y_CAP * begin[c] + j * PARTS[c], 16), PARTS[c]), :] = coef_ref[y_ref[i * Y_CAP + j], spans[c], :]
                return carry

            lax.fori_loop(0, Y_CAP, one, 0)
            target = lax.rem(my_y + i + 1, N_Y) * n_z + my_z
            pltpu.make_async_remote_copy(
                src_ref=y_send.at[i, y_rows[c]], dst_ref=y_recv.at[i, y_rows[c]],
                send_sem=y_ssem, recv_sem=y_rsem.at[c],
                device_id=(my_tm, target), device_id_type=MESH,
            ).start()

    def fill(c):
        pool = pools[c % POOLS]
        held = pl.ds(0, PARTS[c])
        pool[pl.ds(0, blocks), held] = coef_ref[:, spans[c], :]
        wait_bytes(y_recv.at[:, y_rows[c]], y_rsem.at[c])
        for i in range(N_Y - 1):
            pool[pl.ds(blocks + i * Y_CAP, Y_CAP), held] = y_recv[i, y_rows[c]].reshape(Y_CAP, PARTS[c], width)

    def span(c, r, way):
        return (way, pl.ds(firsts[-1] * begin[c] + firsts[r] * PARTS[c], Z_CAPS[r] * PARTS[c]))

    def send_z(c, r):
        pool = pools[c % POOLS]
        for way in range(2):
            base = (2 * r + way) * Z_CAPS[0]

            def one(j, carry):
                at = firsts[-1] * begin[c] + (firsts[r] + j) * PARTS[c]
                z_send[way, pl.ds(pl.multiple_of(at, 16), PARTS[c]), :] = pool[z_ref[base + j], pl.ds(0, PARTS[c])]
                return carry

            lax.fori_loop(0, Z_CAPS[r], one, 0)
            pltpu.make_async_remote_copy(
                src_ref=z_send.at[span(c, r, way)], dst_ref=z_recv.at[span(c, r, way)],
                send_sem=z_ssem, recv_sem=z_rsem.at[c, r, way],
                device_id=(my_tm, ahead[way]), device_id_type=MESH,
            ).start()

    def take_z(c, r):
        pool = pools[c % POOLS]
        for way in range(2):
            wait_bytes(z_recv.at[span(c, r, way)], z_rsem.at[c, r, way])
            at = blocks + y_slots + way * firsts[-1] + firsts[r]
            pool[pl.ds(at, Z_CAPS[r]), pl.ds(0, PARTS[c])] = z_recv[span(c, r, way)].reshape(Z_CAPS[r], PARTS[c], width)

    def stage_a(u):
        owner = lax.rem(my_tm + u + 1, n_tm)
        for e in range(own):
            a_send[u, e] = coef_ref[local_ref[owner * own + e]]
        return owner

    def a_one(u, carry):
        owner = stage_a(u)
        pltpu.make_async_remote_copy(
            src_ref=a_send.at[u], dst_ref=a_out.at[my_tm],
            send_sem=a_sems.at[0], recv_sem=a_sems.at[1],
            device_id=(owner, my_pair), device_id_type=MESH,
        ).start()
        return carry

    def send_x(c):
        pool = pools[c % POOLS]
        part = spans[c]

        def stage_g(u):
            owner = lax.rem(my_tm + u + 1, n_tm)
            for e in range(own):
                x_send[u, e, part] = pool[final_ref[owner * own + e], pl.ds(0, PARTS[c])]
            return owner

        def g_one(u, carry):
            owner = stage_g(u)
            pltpu.make_async_remote_copy(
                src_ref=x_send.at[u, :, part], dst_ref=g_out.at[my_tm, :, part],
                send_sem=g_sems.at[0, c], recv_sem=g_sems.at[1, c],
                device_id=(owner, my_pair), device_id_type=MESH,
            ).start()
            return carry

        lax.fori_loop(0, others, g_one, 0)
        stage_g(others)
        pltpu.make_async_copy(x_send.at[others, :, part], g_out.at[my_tm, :, part], own_sems.at[1 + c]).start()

    def send_x_ener():
        wait_bytes(e_recv.at[pl.ds(0, CAP * peers)], pair_recv)

        def stage_x(u):
            owner = lax.rem(my_tm + u + 1, n_tm)
            for e in range(own):
                x_ener[u, e] = e_recv[slot_ref[owner * own + e]]
                x_ener[u, own + e] = ener_ref[local_ref[owner * own + e]]
            return owner

        def x_one(u, carry):
            owner = stage_x(u)
            pltpu.make_async_remote_copy(
                src_ref=x_ener.at[u], dst_ref=e_out.at[my_tm],
                send_sem=e_sems.at[0], recv_sem=e_sems.at[1],
                device_id=(owner, my_pair), device_id_type=MESH,
            ).start()
            return carry

        lax.fori_loop(0, others, x_one, 0)
        stage_x(others)
        pltpu.make_async_copy(x_ener.at[others], e_out.at[my_tm], own_sems.at[1 + FAST_CHUNKS]).start()

    def own_a():
        stage_a(others)
        pltpu.make_async_copy(a_send.at[others], a_out.at[my_tm], own_sems.at[0]).start()

    tasks = [functools.partial(lax.fori_loop, u, u + 1, a_one, 0) for u in range(others)]
    tasks.append(own_a)
    few = 4
    for i in range(0, peers, few):
        tasks.append(functools.partial(lax.fori_loop, i, min(i + few, peers), send_ener, 0))
    tasks.append(keep_ener)

    def spare():
        if tasks:
            tasks.pop(0)()

    last = len(Z_CAPS) - 1
    sent_ener = False
    send_y(0)
    send_y(1)
    fill(0)
    send_z(0, 0)
    send_y(2)
    fill(1)
    send_z(1, 0)
    send_y(3)
    spare()
    for first in range(0, FAST_CHUNKS, 2):
        second = first + 1
        more = first + 2 < FAST_CHUNKS
        for r in range(last):
            take_z(first, r)
            send_z(first, r + 1)
            spare()
            take_z(second, r)
            send_z(second, r + 1)
            spare()
            if first + 4 + r < FAST_CHUNKS and r < 2:
                send_y(first + 4 + r)
        if more:
            fill(first + 2)
            send_z(first + 2, 0)
        take_z(first, last)
        send_x(first)
        if more:
            fill(first + 3)
            send_z(first + 3, 0)
        take_z(second, last)
        send_x(second)
        if not tasks and not sent_ener:
            sent_ener = True
            send_x_ener()
    assert sent_ener

    wait_bytes(y_send, y_ssem)
    wait_bytes(z_send, z_ssem)
    wait_bytes(e_send.at[pl.ds(0, CAP * peers)], pair_send)
    pltpu.make_async_copy(a_send.at[others], a_out.at[my_tm], own_sems.at[0]).wait()
    for side in range(2):
        wait_bytes(a_send.at[pl.ds(0, others)], a_sems.at[side])
        wait_bytes(x_ener.at[pl.ds(0, others)], e_sems.at[side])
        for c in range(FAST_CHUNKS):
            wait_bytes(x_send.at[pl.ds(0, others), :, spans[c]], g_sems.at[side, c])
    for c in range(FAST_CHUNKS):
        part = spans[c]
        pltpu.make_async_copy(x_send.at[others, :, part], g_out.at[my_tm, :, part], own_sems.at[1 + c]).wait()
    pltpu.make_async_copy(x_ener.at[others], e_out.at[my_tm], own_sems.at[1 + FAST_CHUNKS]).wait()


def half_way(n_z, z_key):
    half = n_z // 2
    node = np.arange(n_z)
    gap = (node[:, None] - node[None, :]) % n_z
    count = jnp.sum((z_key[:, :, None] == node).astype(jnp.bfloat16), axis=1)
    masks = []
    for way in range(2):
        trip = gap if way == 0 else (-gap) % n_z
        from_start = trip
        passes = (trip[:, :, None] < half) & (from_start.T[None, :, :] < trip[:, :, None])
        masks.append(passes.reshape(n_z * n_z, n_z))
    opposite = (gap == half).reshape(n_z * n_z, 1) & (np.arange(n_z * n_z)[:, None] % n_z == node[None, :])
    masks.append(opposite)
    mask = jnp.asarray(np.concatenate(masks, axis=1), jnp.bfloat16)
    sums = jnp.dot(count.reshape(N_Y, n_z * n_z), mask, preferred_element_type=jnp.float32).astype(jnp.int32)
    up, down, there = sums[:, :n_z], sums[:, n_z : 2 * n_z], sums[:, 2 * n_z :]
    most = lambda v, by: functools.reduce(jnp.maximum, [jnp.roll(v, by * h, axis=1) for h in range(half)])
    busy = (most(up, -1), most(down, 1))
    even = ((np.arange(N_Y)[:, None] + node[None, :]) % 2 == 0).astype(np.int32)
    return jnp.clip((there * 32 + 8 * (busy[1] - busy[0]) + 32 * even) // 64, 0, there)


def routes(n_pair, blocks, my_pair, live, source, held, rank):
    listed = live.shape[1]
    n_z = n_pair // N_Y
    n = n_z * listed
    my_y, my_z = my_pair // n_z, my_pair % n_z
    rows = jnp.arange(n_pair, dtype=jnp.int32)
    mine = source == my_pair
    per_row = jnp.sum(mine.astype(jnp.int32), axis=1)
    same = (rows[:, None] // n_z == rows[None, :] // n_z) & (rows[None, :] < rows[:, None])
    first = jnp.sum(jnp.where(same, per_row[None, :], 0), axis=1)
    place = jnp.where(mine, first[:, None] + rank, -1).reshape(N_Y, 1, n)
    want = jnp.arange(Y_CAP, dtype=jnp.int32)[None, :, None]
    y_tab = jnp.sum(jnp.where(place == want, held.reshape(N_Y, 1, n), 0), axis=2)
    y_tab = lax.dynamic_slice_in_dim(jnp.concatenate([y_tab, y_tab]), my_y + 1, N_Y - 1)
    ring_source = source.reshape(N_Y, n)
    ids = jnp.arange(n, dtype=jnp.int32)
    earlier = ids[:, None] < ids[None, :]
    y_same = (ring_source[:, :, None] == ring_source[:, None, :]) & earlier[None]
    y_rank = jnp.sum(y_same.astype(jnp.int32), axis=1)
    off_ring = live.reshape(N_Y, n) & (ring_source // n_z != jnp.arange(N_Y)[:, None])
    y_over = jnp.where(off_ring, y_rank, 0) - (Y_CAP - 1)

    pos_in = jnp.arange(listed, dtype=jnp.int32)
    z_key = jnp.where(live, source % n_z, -1)
    z_same = (z_key[:, :, None] == z_key[:, None, :]) & (pos_in[:, None] < pos_in[None, :])[None]
    z_rank = jnp.sum(z_same.astype(jnp.int32), axis=1).reshape(N_Y, n)
    zd = ids // listed
    zs = ring_source % n_z
    delta = (zd[None, :] - zs) % n_z
    half = n_z // 2
    share = half_way(n_z, z_key)
    mine_share = jnp.sum(jnp.where(zs[None] == jnp.arange(n_z)[:, None, None], share.T[:, :, None], 0), axis=0)
    plus = (delta < half) | ((delta == half) & (z_rank < mine_share))
    way = jnp.where(plus, 0, 1)
    rem = jnp.where(live.reshape(N_Y, n), jnp.where(plus, delta, n_z - delta), 0)
    pos = zs

    ring = lambda v: lax.dynamic_index_in_dim(v, my_y, 0, keepdims=False)
    src, my_way = ring(ring_source), ring(way)
    step_y = (my_y - src // n_z) % N_Y
    loc = jnp.where(step_y == 0, ring(held.reshape(N_Y, n)), blocks + (step_y - 1) * Y_CAP + ring(y_rank))
    loc = jnp.where(src >= 0, loc, 0)
    total = sum(Z_CAPS)
    tables, begun = [], 0
    slots = jnp.arange(Z_CAPS[0], dtype=jnp.int32)
    for cap in Z_CAPS:
        group = jnp.where(rem > 0, pos * 2 + way, -1)
        key = rem * n - ids[None, :]
        ahead = (group[:, :, None] == group[:, None, :]) & (key[:, :, None] > key[:, None, :])
        order = jnp.sum(ahead.astype(jnp.int32), axis=1)
        moved = (rem > 0) & (order < cap)
        my_order, my_moved, my_group = ring(order), ring(moved), ring(group)
        for w in range(2):
            here = jnp.where(my_moved & (my_group == my_z * 2 + w), my_order, -1)
            tables.append(jnp.sum(jnp.where(here[None, :] == slots[:, None], loc[None, :], 0), axis=1))
        loc = jnp.where(my_moved, blocks + (N_Y - 1) * Y_CAP + my_way * total + begun + my_order, loc)
        pos = jnp.where(moved, (pos + jnp.where(plus, 1, n_z - 1)) % n_z, pos)
        rem = rem - moved.astype(jnp.int32)
        begun += cap
    final = lax.dynamic_slice_in_dim(loc, my_z * listed, listed)
    fits = jnp.maximum(jnp.max(rem), jnp.max(y_over)) <= 0
    return fits, y_tab.reshape(-1), jnp.concatenate(tables), final


def entry_kernel(own, n_time, a_ref, g_ref, e_ref, tile_ref, cos_ref, tau_ref, live_ref, w_ref, c_ref, x_ref, y_ref, s_ref):
    e = pl.program_id(0)
    slices, _, size, width = a_ref.shape
    live = live_ref[e]
    lines = lambda v: jnp.concatenate([v[i : i + 1] for i in range(v.shape[0])], axis=1)
    for m in range(slices):
        span = pl.ds(m * width, width)
        x_ref[:, span] = a_ref[m, 0]
        rate = lines(e_ref[m, e] + e_ref[m, own + e])
        g = g_ref[m, 0].astype(jnp.float32)
        for t in range(n_time):
            decay = jnp.exp(-tau_ref[t] * rate)
            s_ref[pl.ds(t, 1), span] = decay
            y_ref[t, :, span] = (g * decay).astype(jnp.bfloat16)
    chi = []
    for t in range(n_time):
        chi.append(live * lax.dot_general(
            x_ref[...], y_ref[t], (((1,), (1,)), ((), ())), preferred_element_type=jnp.float32
        ))
    wfreq = []
    for w in range(n_time):
        chiw = sum(cos_ref[w, t] * chi[t] for t in range(n_time)).astype(jnp.bfloat16)
        prod = jnp.dot(chiw, tile_ref[0], preferred_element_type=jnp.float32)
        prod_b = prod.astype(jnp.bfloat16)
        wfreq.append(
            prod + jnp.dot(prod_b, prod_b, preferred_element_type=jnp.float32) * (1.0 / math.sqrt(size))
        )
    for t in range(n_time):
        w_ref[0, t] = (sum(cos_ref[w, t] * wfreq[w] for w in range(n_time)) * (1.0 / n_time)).astype(jnp.bfloat16)
    screened = w_ref[0].reshape(n_time * size, size)
    for m in range(slices):
        span = pl.ds(m * width, width)
        wy = jnp.dot(screened, g_ref[m, 0], preferred_element_type=jnp.float32)
        a = a_ref[m, 0].astype(jnp.float32)
        total = jnp.zeros((1, width), jnp.float32)
        for t in range(n_time):
            part = jnp.sum(a * wy[t * size : (t + 1) * size], axis=0, keepdims=True)
            total = total + s_ref[pl.ds(t, 1), span] * part
        c_ref[0, pl.ds(m, 1), :] = total * (1.0 / n_time)


def return_kernel(
    n_tm, n_pair, own,
    back_ref, contrib_ref, owning_ref,
    out_ref,
    c_send, c_recv, p_send, p_recv, tm_sems, pair_sems,
):
    my_tm, my_pair = lax.axis_index("tm"), lax.axis_index("pair")
    peers, others = n_pair - 1, n_tm - 1
    width = out_ref.shape[1]
    c_send[...] = jnp.zeros_like(c_send)
    greet(n_tm, n_pair, my_tm, my_pair)

    def stage_c(u):
        owner = lax.rem(my_tm + u + 1, n_tm)
        for e in range(own):
            c_send[u, pl.ds(e, 1), :] = contrib_ref[e, pl.ds(owner, 1), :]
        return owner

    def tm_one(u, carry):
        owner = stage_c(u)
        pltpu.make_async_remote_copy(
            src_ref=c_send.at[u], dst_ref=c_recv.at[u],
            send_sem=tm_sems.at[0], recv_sem=tm_sems.at[1],
            device_id=(owner, my_pair), device_id_type=MESH,
        ).start()
        return carry

    lax.fori_loop(0, others, tm_one, 0)
    stage_c(others)
    wait_bytes(c_recv.at[pl.ds(0, others)], tm_sems.at[1])
    c_recv[others] = c_send[others]

    def stage_p(i):
        for j in range(CAP):
            at = back_ref[CAP * i + j]
            keep = jnp.where(at >= 0, 1.0, 0.0)
            at = jnp.maximum(at, 0)
            line = c_recv[at // own, pl.ds(lax.rem(at, own), 1), :] * keep
            for h in range(width // LINE):
                p_send[CAP * i + j, pl.ds(h, 1), :] = line[:, h * LINE : (h + 1) * LINE]

    def pair_one(i, carry):
        stage_p(i)
        target = lax.rem(my_pair + n_pair - 1 - i, n_pair)
        pltpu.make_async_remote_copy(
            src_ref=p_send.at[pl.ds(CAP * i, CAP)], dst_ref=p_recv.at[pl.ds(CAP * i, CAP)],
            send_sem=pair_sems.at[0], recv_sem=pair_sems.at[1],
            device_id=(my_tm, target), device_id_type=MESH,
        ).start()
        return carry

    lax.fori_loop(0, peers, pair_one, 0)
    stage_p(peers)
    wait_bytes(p_recv.at[pl.ds(0, CAP * peers)], pair_sems.at[1])
    for j in range(CAP * peers, CAP * n_pair):
        p_recv[j] = p_send[j]
    for h in range(width // LINE):
        out_ref[:, pl.ds(h * LINE, LINE)] = jnp.dot(
            owning_ref[...], p_recv[:, h, :], precision=lax.Precision.HIGHEST, preferred_element_type=jnp.float32
        )
    wait_bytes(c_send.at[pl.ds(0, others)], tm_sems.at[0])
    wait_bytes(p_send.at[pl.ds(0, CAP * peers)], pair_sems.at[0])


def body(n_tm, n_pair, coefs, energies, coulomb, tau_grid, freq_grid, pairs):
    blocks, size, width = coefs.shape
    n_time = tau_grid.shape[0]
    listed = pairs.shape[1]
    own = listed // n_tm
    my_tm, my_pair = lax.axis_index("tm"), lax.axis_index("pair")
    remote, local = pairs[:, :, 0], pairs[:, :, 1]
    live = remote >= 0
    source = jnp.where(live, remote // blocks, -1)
    held = remote % blocks
    pos = jnp.arange(listed, dtype=jnp.int32)
    before = (source[:, :, None] == source[:, None, :]) & (pos[:, None] < pos[None, :])[None]
    rank = jnp.sum(before.astype(jnp.int32), axis=1)
    slots = jnp.arange(CAP, dtype=jnp.int32)
    hit = (source == my_pair)[:, None, :] & (rank[:, None, :] == slots[None, :, None])
    pick = jnp.sum(jnp.where(hit, held[:, None, :], 0), axis=2)
    used = jnp.sum(hit.astype(jnp.int32), axis=2)
    turn = lambda v: lax.dynamic_slice_in_dim(jnp.concatenate([v, v]), my_pair + 1, n_pair)
    pick, used = turn(pick), turn(used)
    row = lambda v: lax.dynamic_index_in_dim(v, my_pair, 0, keepdims=False)
    my_live, my_source, my_rank = row(live), row(source), row(rank)
    my_local = jnp.where(my_live, row(local), 0)
    offset = (my_pair - my_source + n_pair - 1) % n_pair
    slot = jnp.where(my_live, offset * CAP + my_rank, 0)
    lane = jnp.arange(n_pair * CAP, dtype=jnp.int32)
    match = (slot[None, :] == lane[:, None]) & my_live[None, :]
    back = jnp.sum(jnp.where(match, pos[None, :], 0), axis=1)
    back = ((my_tm - back // own + n_tm - 1) % n_tm) * own + back % own
    back = jnp.where(jnp.any(match, axis=1), back, -1)
    given = jnp.where(used > 0, pick, -1).reshape(1, -1)
    owning = (jnp.arange(blocks, dtype=jnp.int32)[:, None] == given).astype(jnp.float32)
    my_owned = lax.dynamic_slice_in_dim(my_live, my_tm * own, own).astype(jnp.float32)
    cosine = jnp.cos(freq_grid[:, None] * tau_grid[None, :])
    lined = energies.astype(jnp.float32).reshape(blocks, width // LINE, LINE)

    smem = pl.BlockSpec(memory_space=pltpu.SMEM)
    vmem = pl.BlockSpec(memory_space=pltpu.VMEM)
    hbm = pl.BlockSpec(memory_space=pl.ANY)
    bf16 = jnp.bfloat16
    DMA = pltpu.SemaphoreType.DMA
    step = size // CHUNKS
    thin = size // FAST_CHUNKS
    gathered = (
        jax.ShapeDtypeStruct((n_tm, own, size, width), bf16),
        jax.ShapeDtypeStruct((n_tm, own, size, width), bf16),
        jax.ShapeDtypeStruct((n_tm, 2 * own, width // LINE, LINE), jnp.float32),
    )
    fits, y_tab, z_tab, final = routes(n_pair, blocks, my_pair, live, source, held, rank)
    table = jnp.concatenate([slot, my_local, pick.reshape(-1), final, y_tab, z_tab]).astype(jnp.int32)

    def pooled(table, coefs, lined):
        total = sum(Z_CAPS)
        depth = blocks + (N_Y - 1) * Y_CAP + 2 * total
        return pl.pallas_call(
            functools.partial(fast_kernel, n_tm, n_pair, own, size),
            out_shape=gathered,
            in_specs=[smem, hbm, vmem],
            out_specs=(hbm, hbm, hbm),
            scratch_shapes=[pltpu.VMEM((blocks, size, width), bf16)]
            + [pltpu.VMEM((N_Y - 1, Y_CAP * size, width), bf16)] * 2
            + [pltpu.VMEM((2, total * size, width), bf16)] * 2
            + [
                pltpu.VMEM((CAP * n_pair, width // LINE, LINE), jnp.float32),
                pltpu.VMEM((CAP * n_pair, width // LINE, LINE), jnp.float32),
                pltpu.VMEM((n_tm, own, size, width), bf16),
                pltpu.VMEM((n_tm, own, size, width), bf16),
                pltpu.VMEM((n_tm, 2 * own, width // LINE, LINE), jnp.float32),
            ]
            + [pltpu.VMEM((depth, max(PARTS), width), bf16)] * POOLS
            + [
                DMA,
                DMA((FAST_CHUNKS,)),
                DMA,
                DMA((FAST_CHUNKS, len(Z_CAPS), 2)),
                DMA,
                DMA,
                DMA((2,)),
                DMA((2, FAST_CHUNKS)),
                DMA((2,)),
                DMA((3 + FAST_CHUNKS,)),
            ],
            compiler_params=pltpu.CompilerParams(
                collective_id=2, has_side_effects=True, vmem_limit_bytes=62 * 1024 * 1024
            ),
        )(table, coefs, lined)

    def direct(table, coefs, lined):
        return pl.pallas_call(
            functools.partial(gather_kernel, n_tm, n_pair, own, size),
            out_shape=gathered,
            in_specs=[smem] + [vmem] * 2,
            out_specs=(hbm, hbm, hbm),
            scratch_shapes=[pltpu.VMEM((CAP * n_pair, step, width), bf16)] * (2 * CHUNKS)
            + [
                pltpu.VMEM((CAP * n_pair, width // LINE, LINE), jnp.float32),
                pltpu.VMEM((CAP * n_pair, width // LINE, LINE), jnp.float32),
                pltpu.VMEM((n_tm, own, size, width), bf16),
                pltpu.VMEM((CHUNKS, n_tm, own, step, width), bf16),
                pltpu.VMEM((n_tm, 2 * own, width // LINE, LINE), jnp.float32),
                DMA((CHUNKS + 1,)),
                DMA((CHUNKS + 1,)),
                DMA((2,)),
                DMA((2, CHUNKS)),
                DMA((2,)),
                DMA((2 + CHUNKS,)),
            ],
            compiler_params=pltpu.CompilerParams(
                collective_id=0, has_side_effects=True, vmem_limit_bytes=56 * 1024 * 1024
            ),
        )(table, coefs, lined)

    a_all, g_all, e_all = lax.cond(
        fits, pooled, direct, table, coefs, lined
    )

    screened, contrib = pl.pallas_call(
        functools.partial(entry_kernel, own, n_time),
        grid=(own,),
        out_shape=(
            jax.ShapeDtypeStruct((own, n_time, size, size), bf16),
            jax.ShapeDtypeStruct((own, n_tm, width), jnp.float32),
        ),
        in_specs=[
            pl.BlockSpec((n_tm, 1, size, width), lambda e: (0, e, 0, 0)),
            pl.BlockSpec((n_tm, 1, size, width), lambda e: (0, e, 0, 0)),
            pl.BlockSpec((n_tm, 2 * own, width // LINE, LINE), lambda e: (0, 0, 0, 0)),
            pl.BlockSpec((1, size, size), lambda e: (e, 0, 0)),
            smem, smem, smem,
        ],
        out_specs=(
            pl.BlockSpec((1, n_time, size, size), lambda e: (e, 0, 0, 0)),
            pl.BlockSpec((1, n_tm, width), lambda e: (e, 0, 0)),
        ),
        scratch_shapes=[
            pltpu.VMEM((size, n_tm * width), bf16),
            pltpu.VMEM((n_time, size, n_tm * width), bf16),
            pltpu.VMEM((8, n_tm * width), jnp.float32),
        ],
        compiler_params=pltpu.CompilerParams(vmem_limit_bytes=48 * 1024 * 1024),
    )(a_all, g_all, e_all, coulomb[0], cosine, tau_grid, my_owned)

    self_energy = pl.pallas_call(
        functools.partial(return_kernel, n_tm, n_pair, own),
        out_shape=jax.ShapeDtypeStruct((blocks, width), jnp.float32),
        in_specs=[smem, vmem, vmem],
        out_specs=vmem,
        scratch_shapes=[
            pltpu.VMEM((n_tm, 8, width), jnp.float32),
            pltpu.VMEM((n_tm, 8, width), jnp.float32),
            pltpu.VMEM((CAP * n_pair, width // LINE, LINE), jnp.float32),
            pltpu.VMEM((CAP * n_pair, width // LINE, LINE), jnp.float32),
            DMA((2,)),
            DMA((2,)),
        ],
        compiler_params=pltpu.CompilerParams(collective_id=1, has_side_effects=True),
    )(back, contrib, owning)
    return (screened[None], self_energy)


def solution(mesh):
    return jax.shard_map(
        functools.partial(body, mesh.shape["tm"], mesh.shape["pair"]),
        mesh=mesh,
        in_specs=(
            P("pair", None, "tm"),
            P("pair", "tm"),
            P("pair", "tm", None, None),
            P(),
            P(),
            P(),
        ),
        out_specs=(P("pair", "tm", None, None, None), P("pair", "tm")),
        check_vma=False,
    )
```

```python
import functools
import math

import jax
import jax.numpy as jnp
import numpy as np
from jax import lax
from jax.experimental import pallas as pl
from jax.experimental.pallas import tpu as pltpu
from jax.sharding import PartitionSpec as P

CAP = 2
CHUNKS = 4
PARTS = (16, 16, 32, 32, 32, 32, 32, 32, 16, 16)
FAST_CHUNKS = len(PARTS)
Y_CAP = 15
Z_CAPS = (10, 10, 9, 8)
LINE = 128
N_Y = 4
POOLS = 3
MESH = pl.DeviceIdType.MESH


def greet(n_tm, n_pair, my_tm, my_pair):
    barrier = pltpu.get_barrier_semaphore()

    def pair_peer(i, c):
        other = lax.rem(my_pair + i, n_pair)
        pl.semaphore_signal(barrier, inc=1, device_id=(my_tm, other), device_id_type=MESH)
        return c

    def tm_peer(i, c):
        other = lax.rem(my_tm + i, n_tm)
        pl.semaphore_signal(barrier, inc=1, device_id=(other, my_pair), device_id_type=MESH)
        return c

    lax.fori_loop(1, n_pair, pair_peer, 0)
    lax.fori_loop(1, n_tm, tm_peer, 0)
    return lambda: pl.semaphore_wait(barrier, n_pair + n_tm - 2)


class View:
    def __init__(self, ref, at):
        self.ref, self.at = ref, at

    def __getitem__(self, i):
        return self.ref[self.at + i]


def views(table, listed, n_pair):
    sizes = (listed, listed, CAP * n_pair, listed, (N_Y - 1) * Y_CAP)
    at = [sum(sizes[:i]) for i in range(len(sizes) + 1)]
    return [View(table, i) for i in at]


def spread(flat_ref, tile_ref):
    flat = flat_ref[...].astype(jnp.float32)
    for h in range(flat.shape[1] // LINE):
        tile_ref[:, h, :] = flat[:, h * LINE : (h + 1) * LINE]


def wait_bytes(ref, sem):
    pltpu.make_async_copy(ref, ref, sem).wait()


def gather_kernel(
    n_tm, n_pair, own, rows,
    table_ref, coef_ref, ener_in,
    a_out, g_out, e_out,
    *scratch,
):
    slot_ref, local_ref, pick_ref = views(table_ref, n_tm * own, n_pair)[:3]
    my_tm, my_pair = lax.axis_index("tm"), lax.axis_index("pair")
    sends, recvs = scratch[:CHUNKS], scratch[CHUNKS : 2 * CHUNKS]
    (e_send, e_recv, a_send, g_send, x_ener,
     pair_send, pair_recv, a_sems, g_sems, e_sems, own_sems, ener_ref) = scratch[2 * CHUNKS :]
    peers, others = n_pair - 1, n_tm - 1
    step = rows // CHUNKS
    spread(ener_in, ener_ref)
    greet(n_tm, n_pair, my_tm, my_pair)()

    def pair_copy(i, c):
        target = lax.rem(my_pair + i + 1, n_pair)
        return pltpu.make_async_remote_copy(
            src_ref=sends[c].at[pl.ds(CAP * i, CAP)],
            dst_ref=recvs[c].at[pl.ds(CAP * i, CAP)],
            send_sem=pair_send.at[c], recv_sem=pair_recv.at[c],
            device_id=(my_tm, target), device_id_type=MESH,
        )

    def ener_copy(i):
        target = lax.rem(my_pair + i + 1, n_pair)
        return pltpu.make_async_remote_copy(
            src_ref=e_send.at[pl.ds(CAP * i, CAP)], dst_ref=e_recv.at[pl.ds(CAP * i, CAP)],
            send_sem=pair_send.at[CHUNKS], recv_sem=pair_recv.at[CHUNKS],
            device_id=(my_tm, target), device_id_type=MESH,
        )


    def stage_a(u):
        owner = lax.rem(my_tm + u + 1, n_tm)
        for e in range(own):
            a_send[u, e] = coef_ref[local_ref[owner * own + e]]
        return owner

    def send_pair(c):
        def one(i, carry):
            for j in range(CAP):
                sends[c][CAP * i + j] = coef_ref[pick_ref[CAP * i + j], pl.ds(c * step, step), :]
            pair_copy(i, c).start()
            return carry

        lax.fori_loop(0, peers, one, 0)
        for j in range(CAP):
            recvs[c][CAP * peers + j] = coef_ref[pick_ref[CAP * peers + j], pl.ds(c * step, step), :]

    def send_ener(i, carry):
        for j in range(CAP):
            e_send[CAP * i + j] = ener_ref[pick_ref[CAP * i + j]]
        ener_copy(i).start()
        return carry

    def keep_ener():
        for j in range(CAP * peers, CAP * n_pair):
            e_recv[j] = ener_ref[pick_ref[j]]

    def a_one(u, carry):
        owner = stage_a(u)
        pltpu.make_async_remote_copy(
            src_ref=a_send.at[u], dst_ref=a_out.at[my_tm],
            send_sem=a_sems.at[0], recv_sem=a_sems.at[1],
            device_id=(owner, my_pair), device_id_type=MESH,
        ).start()
        return carry

    send_pair(0)
    lax.fori_loop(0, others, a_one, 0)
    stage_a(others)
    own_a = pltpu.make_async_copy(a_send.at[others], a_out.at[my_tm], own_sems.at[0])
    own_a.start()
    lax.fori_loop(0, peers, send_ener, 0)
    keep_ener()
    for c in range(1, CHUNKS):
        send_pair(c)

    owned_g = []
    for c in range(CHUNKS):
        wait_bytes(recvs[c].at[pl.ds(0, CAP * peers)], pair_recv.at[c])

        def stage_g(u):
            owner = lax.rem(my_tm + u + 1, n_tm)
            for e in range(own):
                g_send[c, u, e] = recvs[c][slot_ref[owner * own + e]]
            return owner

        def g_one(u, carry):
            owner = stage_g(u)
            pltpu.make_async_remote_copy(
                src_ref=g_send.at[c, u], dst_ref=g_out.at[my_tm, :, pl.ds(c * step, step)],
                send_sem=g_sems.at[0, c], recv_sem=g_sems.at[1, c],
                device_id=(owner, my_pair), device_id_type=MESH,
            ).start()
            return carry

        lax.fori_loop(0, others, g_one, 0)
        stage_g(others)
        copy = pltpu.make_async_copy(g_send.at[c, others], g_out.at[my_tm, :, pl.ds(c * step, step)], own_sems.at[1 + c])
        copy.start()
        owned_g.append(copy)
        if c == 0:
            wait_bytes(e_recv.at[pl.ds(0, CAP * peers)], pair_recv.at[CHUNKS])

            def stage_x(u):
                owner = lax.rem(my_tm + u + 1, n_tm)
                for e in range(own):
                    x_ener[u, e] = e_recv[slot_ref[owner * own + e]]
                    x_ener[u, own + e] = ener_ref[local_ref[owner * own + e]]
                return owner

            def x_one(u, carry):
                owner = stage_x(u)
                pltpu.make_async_remote_copy(
                    src_ref=x_ener.at[u], dst_ref=e_out.at[my_tm],
                    send_sem=e_sems.at[0], recv_sem=e_sems.at[1],
                    device_id=(owner, my_pair), device_id_type=MESH,
                ).start()
                return carry

            lax.fori_loop(0, others, x_one, 0)
            stage_x(others)
            own_e = pltpu.make_async_copy(x_ener.at[others], e_out.at[my_tm], own_sems.at[1 + CHUNKS])
            own_e.start()

    for c in range(CHUNKS):
        wait_bytes(sends[c].at[pl.ds(0, CAP * peers)], pair_send.at[c])
    wait_bytes(e_send.at[pl.ds(0, CAP * peers)], pair_send.at[CHUNKS])
    for side in range(2):
        wait_bytes(a_send.at[pl.ds(0, others)], a_sems.at[side])
        wait_bytes(x_ener.at[pl.ds(0, others)], e_sems.at[side])
        for c in range(CHUNKS):
            wait_bytes(g_send.at[c, pl.ds(0, others)], g_sems.at[side, c])
    own_a.wait()
    own_e.wait()
    for copy in owned_g:
        copy.wait()


def fast_kernel(
    n_tm, n_pair, own, rows,
    table_ref, coef_hbm, ener_in,
    a_out, g_out, e_out,
    coef_ref, ener_ref, y_send, y_recv, z_send, z_recv, e_send, e_recv, a_send, x_send, x_ener, *rest,
):
    slot_ref, local_ref, pick_ref, final_ref, y_ref, z_ref = views(table_ref, n_tm * own, n_pair)
    pools = rest[:POOLS]
    (y_ssem, y_rsem, z_ssem, z_rsem, pair_send, pair_recv, a_sems, g_sems, e_sems, own_sems) = rest[POOLS:]
    my_tm, my_pair = lax.axis_index("tm"), lax.axis_index("pair")
    peers, others = n_pair - 1, n_tm - 1
    n_z = n_pair // N_Y
    my_y, my_z = my_pair // n_z, lax.rem(my_pair, n_z)
    assert sum(PARTS) == rows
    begin = [sum(PARTS[:c]) for c in range(FAST_CHUNKS)]
    spans = [pl.ds(begin[c], PARTS[c]) for c in range(FAST_CHUNKS)]
    y_rows = [pl.ds(Y_CAP * begin[c], Y_CAP * PARTS[c]) for c in range(FAST_CHUNKS)]
    blocks, _, width = coef_ref.shape
    y_slots = (N_Y - 1) * Y_CAP
    ahead = (my_y * n_z + lax.rem(my_z + 1, n_z), my_y * n_z + lax.rem(my_z + n_z - 1, n_z))
    firsts = [sum(Z_CAPS[:r]) for r in range(len(Z_CAPS) + 1)]
    load = pltpu.make_async_copy(coef_hbm, coef_ref, own_sems.at[2 + FAST_CHUNKS])
    load.start()
    met = greet(n_tm, n_pair, my_tm, my_pair)
    spread(ener_in, ener_ref)
    load.wait()

    def ener_copy(i):
        target = lax.rem(my_pair + i + 1, n_pair)
        return pltpu.make_async_remote_copy(
            src_ref=e_send.at[pl.ds(CAP * i, CAP)], dst_ref=e_recv.at[pl.ds(CAP * i, CAP)],
            send_sem=pair_send, recv_sem=pair_recv,
            device_id=(my_tm, target), device_id_type=MESH,
        )

    def send_ener(i, carry):
        for j in range(CAP):
            e_send[CAP * i + j] = ener_ref[pick_ref[CAP * i + j]]
        ener_copy(i).start()
        return carry

    def keep_ener():
        for j in range(CAP * peers, CAP * n_pair):
            e_recv[j] = ener_ref[pick_ref[j]]

    def stage_y(c):
        for i in range(N_Y - 1):
            def one(j, carry):
                y_send[i, pl.ds(pl.multiple_of(Y_CAP * begin[c] + j * PARTS[c], 16), PARTS[c]), :] = coef_ref[y_ref[i * Y_CAP + j], spans[c], :]
                return carry

            lax.fori_loop(0, Y_CAP, one, 0)

    def start_y(c):
        for i in range(N_Y - 1):
            target = lax.rem(my_y + i + 1, N_Y) * n_z + my_z
            pltpu.make_async_remote_copy(
                src_ref=y_send.at[i, y_rows[c]], dst_ref=y_recv.at[i, y_rows[c]],
                send_sem=y_ssem, recv_sem=y_rsem.at[c],
                device_id=(my_tm, target), device_id_type=MESH,
            ).start()

    def send_y(c):
        stage_y(c)
        start_y(c)

    def fill(c):
        pool = pools[c % POOLS]
        held = pl.ds(0, PARTS[c])
        pool[pl.ds(0, blocks), held] = coef_ref[:, spans[c], :]
        wait_bytes(y_recv.at[:, y_rows[c]], y_rsem.at[c])
        for i in range(N_Y - 1):
            pool[pl.ds(blocks + i * Y_CAP, Y_CAP), held] = y_recv[i, y_rows[c]].reshape(Y_CAP, PARTS[c], width)

    def span(c, r, way):
        return (way, pl.ds(firsts[-1] * begin[c] + firsts[r] * PARTS[c], Z_CAPS[r] * PARTS[c]))

    def send_z(c, r):
        pool = pools[c % POOLS]
        for way in range(2):
            base = (2 * r + way) * Z_CAPS[0]

            def one(j, carry):
                at = firsts[-1] * begin[c] + (firsts[r] + j) * PARTS[c]
                z_send[way, pl.ds(pl.multiple_of(at, 16), PARTS[c]), :] = pool[z_ref[base + j], pl.ds(0, PARTS[c])]
                return carry

            lax.fori_loop(0, Z_CAPS[r], one, 0)
            pltpu.make_async_remote_copy(
                src_ref=z_send.at[span(c, r, way)], dst_ref=z_recv.at[span(c, r, way)],
                send_sem=z_ssem, recv_sem=z_rsem.at[c, r, way],
                device_id=(my_tm, ahead[way]), device_id_type=MESH,
            ).start()

    def take_z(c, r):
        pool = pools[c % POOLS]
        for way in range(2):
            wait_bytes(z_recv.at[span(c, r, way)], z_rsem.at[c, r, way])
            at = blocks + y_slots + way * firsts[-1] + firsts[r]
            pool[pl.ds(at, Z_CAPS[r]), pl.ds(0, PARTS[c])] = z_recv[span(c, r, way)].reshape(Z_CAPS[r], PARTS[c], width)

    def stage_a(u):
        owner = lax.rem(my_tm + u + 1, n_tm)
        for e in range(own):
            a_send[u, e] = coef_ref[local_ref[owner * own + e]]
        return owner

    def a_one(u, carry):
        owner = stage_a(u)
        pltpu.make_async_remote_copy(
            src_ref=a_send.at[u], dst_ref=a_out.at[my_tm],
            send_sem=a_sems.at[0], recv_sem=a_sems.at[1],
            device_id=(owner, my_pair), device_id_type=MESH,
        ).start()
        return carry

    def send_x(c):
        pool = pools[c % POOLS]
        part = spans[c]

        def stage_g(u):
            owner = lax.rem(my_tm + u + 1, n_tm)
            for e in range(own):
                x_send[u, e, part] = pool[final_ref[owner * own + e], pl.ds(0, PARTS[c])]
            return owner

        def g_one(u, carry):
            owner = stage_g(u)
            pltpu.make_async_remote_copy(
                src_ref=x_send.at[u, :, part], dst_ref=g_out.at[my_tm, :, part],
                send_sem=g_sems.at[0, c], recv_sem=g_sems.at[1, c],
                device_id=(owner, my_pair), device_id_type=MESH,
            ).start()
            return carry

        lax.fori_loop(0, others, g_one, 0)
        stage_g(others)
        pltpu.make_async_copy(x_send.at[others, :, part], g_out.at[my_tm, :, part], own_sems.at[1 + c]).start()

    def send_x_ener():
        wait_bytes(e_recv.at[pl.ds(0, CAP * peers)], pair_recv)

        def stage_x(u):
            owner = lax.rem(my_tm + u + 1, n_tm)
            for e in range(own):
                x_ener[u, e] = e_recv[slot_ref[owner * own + e]]
                x_ener[u, own + e] = ener_ref[local_ref[owner * own + e]]
            return owner

        def x_one(u, carry):
            owner = stage_x(u)
            pltpu.make_async_remote_copy(
                src_ref=x_ener.at[u], dst_ref=e_out.at[my_tm],
                send_sem=e_sems.at[0], recv_sem=e_sems.at[1],
                device_id=(owner, my_pair), device_id_type=MESH,
            ).start()
            return carry

        lax.fori_loop(0, others, x_one, 0)
        stage_x(others)
        pltpu.make_async_copy(x_ener.at[others], e_out.at[my_tm], own_sems.at[1 + FAST_CHUNKS]).start()

    def own_a():
        stage_a(others)
        pltpu.make_async_copy(a_send.at[others], a_out.at[my_tm], own_sems.at[0]).start()

    tasks = [functools.partial(lax.fori_loop, u, u + 1, a_one, 0) for u in range(others)]
    tasks.append(own_a)
    few = 4
    for i in range(0, peers, few):
        tasks.append(functools.partial(lax.fori_loop, i, min(i + few, peers), send_ener, 0))
    tasks.append(keep_ener)

    def spare():
        if tasks:
            tasks.pop(0)()

    last = len(Z_CAPS) - 1
    sent_ener = False
    stage_y(0)
    met()
    start_y(0)
    send_y(1)
    fill(0)
    send_z(0, 0)
    send_y(2)
    fill(1)
    send_z(1, 0)
    send_y(3)
    spare()
    for first in range(0, FAST_CHUNKS, 2):
        second = first + 1
        more = first + 2 < FAST_CHUNKS
        for r in range(last):
            take_z(first, r)
            send_z(first, r + 1)
            spare()
            take_z(second, r)
            send_z(second, r + 1)
            spare()
            if first + 4 + r < FAST_CHUNKS and r < 2:
                send_y(first + 4 + r)
        if more:
            fill(first + 2)
            send_z(first + 2, 0)
        take_z(first, last)
        send_x(first)
        if more:
            fill(first + 3)
            send_z(first + 3, 0)
        take_z(second, last)
        send_x(second)
        if not tasks and not sent_ener:
            sent_ener = True
            send_x_ener()
    assert sent_ener

    wait_bytes(y_send, y_ssem)
    wait_bytes(z_send, z_ssem)
    wait_bytes(e_send.at[pl.ds(0, CAP * peers)], pair_send)
    pltpu.make_async_copy(a_send.at[others], a_out.at[my_tm], own_sems.at[0]).wait()
    for side in range(2):
        wait_bytes(a_send.at[pl.ds(0, others)], a_sems.at[side])
        wait_bytes(x_ener.at[pl.ds(0, others)], e_sems.at[side])
        for c in range(FAST_CHUNKS):
            wait_bytes(x_send.at[pl.ds(0, others), :, spans[c]], g_sems.at[side, c])
    for c in range(FAST_CHUNKS):
        part = spans[c]
        pltpu.make_async_copy(x_send.at[others, :, part], g_out.at[my_tm, :, part], own_sems.at[1 + c]).wait()
    pltpu.make_async_copy(x_ener.at[others], e_out.at[my_tm], own_sems.at[1 + FAST_CHUNKS]).wait()


def half_way(n_z, z_key):
    half = n_z // 2
    node = np.arange(n_z)
    gap = (node[:, None] - node[None, :]) % n_z
    count = jnp.sum((z_key[:, :, None] == node).astype(jnp.bfloat16), axis=1)
    masks = []
    for way in range(2):
        trip = gap if way == 0 else (-gap) % n_z
        from_start = trip
        passes = (trip[:, :, None] < half) & (from_start.T[None, :, :] < trip[:, :, None])
        masks.append(passes.reshape(n_z * n_z, n_z))
    opposite = (gap == half).reshape(n_z * n_z, 1) & (np.arange(n_z * n_z)[:, None] % n_z == node[None, :])
    masks.append(opposite)
    mask = jnp.asarray(np.concatenate(masks, axis=1), jnp.bfloat16)
    sums = jnp.dot(count.reshape(N_Y, n_z * n_z), mask, preferred_element_type=jnp.float32).astype(jnp.int32)
    up, down, there = sums[:, :n_z], sums[:, n_z : 2 * n_z], sums[:, 2 * n_z :]
    most = lambda v, by: functools.reduce(jnp.maximum, [jnp.roll(v, by * h, axis=1) for h in range(half)])
    busy = (most(up, -1), most(down, 1))
    even = ((np.arange(N_Y)[:, None] + node[None, :]) % 2 == 0).astype(np.int32)
    return jnp.clip((there * 32 + 8 * (busy[1] - busy[0]) + 32 * even) // 64, 0, there)


def routes(n_pair, blocks, my_pair, live, source, held, rank):
    listed = live.shape[1]
    n_z = n_pair // N_Y
    n = n_z * listed
    my_y, my_z = my_pair // n_z, my_pair % n_z
    rows = jnp.arange(n_pair, dtype=jnp.int32)
    mine = source == my_pair
    per_row = jnp.sum(mine.astype(jnp.int32), axis=1)
    same = (rows[:, None] // n_z == rows[None, :] // n_z) & (rows[None, :] < rows[:, None])
    first = jnp.sum(jnp.where(same, per_row[None, :], 0), axis=1)
    place = jnp.where(mine, first[:, None] + rank, -1).reshape(N_Y, 1, n)
    want = jnp.arange(Y_CAP, dtype=jnp.int32)[None, :, None]
    y_tab = jnp.sum(jnp.where(place == want, held.reshape(N_Y, 1, n), 0), axis=2)
    y_tab = lax.dynamic_slice_in_dim(jnp.concatenate([y_tab, y_tab]), my_y + 1, N_Y - 1)
    ring_source = source.reshape(N_Y, n)
    ids = jnp.arange(n, dtype=jnp.int32)
    earlier = ids[:, None] < ids[None, :]
    y_same = (ring_source[:, :, None] == ring_source[:, None, :]) & earlier[None]
    y_rank = jnp.sum(y_same.astype(jnp.int32), axis=1)
    off_ring = live.reshape(N_Y, n) & (ring_source // n_z != jnp.arange(N_Y)[:, None])
    y_over = jnp.where(off_ring, y_rank, 0) - (Y_CAP - 1)

    pos_in = jnp.arange(listed, dtype=jnp.int32)
    z_key = jnp.where(live, source % n_z, -1)
    z_same = (z_key[:, :, None] == z_key[:, None, :]) & (pos_in[:, None] < pos_in[None, :])[None]
    z_rank = jnp.sum(z_same.astype(jnp.int32), axis=1).reshape(N_Y, n)
    zd = ids // listed
    zs = ring_source % n_z
    delta = (zd[None, :] - zs) % n_z
    half = n_z // 2
    share = half_way(n_z, z_key)
    mine_share = jnp.sum(jnp.where(zs[None] == jnp.arange(n_z)[:, None, None], share.T[:, :, None], 0), axis=0)
    plus = (delta < half) | ((delta == half) & (z_rank < mine_share))
    way = jnp.where(plus, 0, 1)
    rem = jnp.where(live.reshape(N_Y, n), jnp.where(plus, delta, n_z - delta), 0)
    pos = zs

    ring = lambda v: lax.dynamic_index_in_dim(v, my_y, 0, keepdims=False)
    src, my_way = ring(ring_source), ring(way)
    step_y = (my_y - src // n_z) % N_Y
    loc = jnp.where(step_y == 0, ring(held.reshape(N_Y, n)), blocks + (step_y - 1) * Y_CAP + ring(y_rank))
    loc = jnp.where(src >= 0, loc, 0)
    total = sum(Z_CAPS)
    tables, begun = [], 0
    slots = jnp.arange(Z_CAPS[0], dtype=jnp.int32)
    for cap in Z_CAPS:
        group = jnp.where(rem > 0, pos * 2 + way, -1)
        key = rem * n - ids[None, :]
        ahead = (group[:, :, None] == group[:, None, :]) & (key[:, :, None] > key[:, None, :])
        order = jnp.sum(ahead.astype(jnp.int32), axis=1)
        moved = (rem > 0) & (order < cap)
        my_order, my_moved, my_group = ring(order), ring(moved), ring(group)
        for w in range(2):
            here = jnp.where(my_moved & (my_group == my_z * 2 + w), my_order, -1)
            tables.append(jnp.sum(jnp.where(here[None, :] == slots[:, None], loc[None, :], 0), axis=1))
        loc = jnp.where(my_moved, blocks + (N_Y - 1) * Y_CAP + my_way * total + begun + my_order, loc)
        pos = jnp.where(moved, (pos + jnp.where(plus, 1, n_z - 1)) % n_z, pos)
        rem = rem - moved.astype(jnp.int32)
        begun += cap
    final = lax.dynamic_slice_in_dim(loc, my_z * listed, listed)
    fits = jnp.maximum(jnp.max(rem), jnp.max(y_over)) <= 0
    return fits, y_tab.reshape(-1), jnp.concatenate(tables), final


def entry_kernel(own, n_time, a_ref, g_ref, e_ref, tile_ref, cos_ref, tau_ref, live_ref, w_ref, c_ref, x_ref, y_ref, s_ref):
    e = pl.program_id(0)
    slices, _, size, width = a_ref.shape
    live = live_ref[e]
    lines = lambda v: jnp.concatenate([v[i : i + 1] for i in range(v.shape[0])], axis=1)
    for m in range(slices):
        span = pl.ds(m * width, width)
        x_ref[:, span] = a_ref[m, 0]
        rate = lines(e_ref[m, e] + e_ref[m, own + e])
        g = g_ref[m, 0].astype(jnp.float32)
        for t in range(n_time):
            decay = jnp.exp(-tau_ref[t] * rate)
            s_ref[pl.ds(t, 1), span] = decay
            y_ref[t, :, span] = (g * decay).astype(jnp.bfloat16)
    chi = []
    for t in range(n_time):
        chi.append(live * lax.dot_general(
            x_ref[...], y_ref[t], (((1,), (1,)), ((), ())), preferred_element_type=jnp.float32
        ))
    wfreq = []
    for w in range(n_time):
        chiw = sum(cos_ref[w, t] * chi[t] for t in range(n_time)).astype(jnp.bfloat16)
        prod = jnp.dot(chiw, tile_ref[0], preferred_element_type=jnp.float32)
        prod_b = prod.astype(jnp.bfloat16)
        wfreq.append(
            prod + jnp.dot(prod_b, prod_b, preferred_element_type=jnp.float32) * (1.0 / math.sqrt(size))
        )
    for t in range(n_time):
        w_ref[0, t] = (sum(cos_ref[w, t] * wfreq[w] for w in range(n_time)) * (1.0 / n_time)).astype(jnp.bfloat16)
    screened = w_ref[0].reshape(n_time * size, size)
    for m in range(slices):
        span = pl.ds(m * width, width)
        wy = jnp.dot(screened, g_ref[m, 0], preferred_element_type=jnp.float32)
        a = a_ref[m, 0].astype(jnp.float32)
        total = jnp.zeros((1, width), jnp.float32)
        for t in range(n_time):
            part = jnp.sum(a * wy[t * size : (t + 1) * size], axis=0, keepdims=True)
            total = total + s_ref[pl.ds(t, 1), span] * part
        c_ref[0, pl.ds(m, 1), :] = total * (1.0 / n_time)


def return_kernel(
    n_tm, n_pair, own,
    back_ref, contrib_ref, given_ref,
    out_ref,
    c_send, c_recv, p_send, p_recv, tm_sems, pair_sems,
):
    my_tm, my_pair = lax.axis_index("tm"), lax.axis_index("pair")
    peers, others = n_pair - 1, n_tm - 1
    width = out_ref.shape[1]
    met = greet(n_tm, n_pair, my_tm, my_pair)
    c_send[...] = jnp.zeros_like(c_send)

    def stage_c(u):
        owner = lax.rem(my_tm + u + 1, n_tm)
        for e in range(own):
            c_send[u, pl.ds(e, 1), :] = contrib_ref[e, pl.ds(owner, 1), :]
        return owner

    def tm_one(u, carry):
        owner = lax.rem(my_tm + u + 1, n_tm)
        pltpu.make_async_remote_copy(
            src_ref=c_send.at[u], dst_ref=c_recv.at[u],
            send_sem=tm_sems.at[0], recv_sem=tm_sems.at[1],
            device_id=(owner, my_pair), device_id_type=MESH,
        ).start()
        return carry

    for u in range(n_tm):
        stage_c(u)
    met()
    lax.fori_loop(0, others, tm_one, 0)
    block_id = lax.broadcasted_iota(jnp.int32, (out_ref.shape[0], CAP * n_pair), 0)
    owning = (block_id == given_ref[...]).astype(jnp.float32)
    wait_bytes(c_recv.at[pl.ds(0, others)], tm_sems.at[1])
    c_recv[others] = c_send[others]

    def stage_p(i):
        for j in range(CAP):
            at = back_ref[CAP * i + j]
            keep = jnp.where(at >= 0, 1.0, 0.0)
            at = jnp.maximum(at, 0)
            line = c_recv[at // own, pl.ds(lax.rem(at, own), 1), :] * keep
            for h in range(width // LINE):
                p_send[CAP * i + j, pl.ds(h, 1), :] = line[:, h * LINE : (h + 1) * LINE]

    def pair_one(i, carry):
        stage_p(i)
        target = lax.rem(my_pair + n_pair - 1 - i, n_pair)
        pltpu.make_async_remote_copy(
            src_ref=p_send.at[pl.ds(CAP * i, CAP)], dst_ref=p_recv.at[pl.ds(CAP * i, CAP)],
            send_sem=pair_sems.at[0], recv_sem=pair_sems.at[1],
            device_id=(my_tm, target), device_id_type=MESH,
        ).start()
        return carry

    lax.fori_loop(0, peers, pair_one, 0)
    stage_p(peers)
    wait_bytes(p_recv.at[pl.ds(0, CAP * peers)], pair_sems.at[1])
    for j in range(CAP * peers, CAP * n_pair):
        p_recv[j] = p_send[j]
    for h in range(width // LINE):
        out_ref[:, pl.ds(h * LINE, LINE)] = jnp.dot(
            owning, p_recv[:, h, :], precision=lax.Precision.HIGHEST, preferred_element_type=jnp.float32
        )
    wait_bytes(c_send.at[pl.ds(0, others)], tm_sems.at[0])
    wait_bytes(p_send.at[pl.ds(0, CAP * peers)], pair_sems.at[0])


def body(n_tm, n_pair, coefs, energies, coulomb, tau_grid, freq_grid, pairs):
    blocks, size, width = coefs.shape
    n_time = tau_grid.shape[0]
    listed = pairs.shape[1]
    own = listed // n_tm
    my_tm, my_pair = lax.axis_index("tm"), lax.axis_index("pair")
    remote, local = pairs[:, :, 0], pairs[:, :, 1]
    live = remote >= 0
    source = jnp.where(live, remote // blocks, -1)
    held = remote % blocks
    pos = jnp.arange(listed, dtype=jnp.int32)
    before = (source[:, :, None] == source[:, None, :]) & (pos[:, None] < pos[None, :])[None]
    rank = jnp.sum(before.astype(jnp.int32), axis=1)
    slots = jnp.arange(CAP, dtype=jnp.int32)
    hit = (source == my_pair)[:, None, :] & (rank[:, None, :] == slots[None, :, None])
    pick = jnp.sum(jnp.where(hit, held[:, None, :], 0), axis=2)
    used = jnp.sum(hit.astype(jnp.int32), axis=2)
    turn = lambda v: lax.dynamic_slice_in_dim(jnp.concatenate([v, v]), my_pair + 1, n_pair)
    pick, used = turn(pick), turn(used)
    row = lambda v: lax.dynamic_index_in_dim(v, my_pair, 0, keepdims=False)
    my_live, my_source, my_rank = row(live), row(source), row(rank)
    my_local = jnp.where(my_live, row(local), 0)
    offset = (my_pair - my_source + n_pair - 1) % n_pair
    slot = jnp.where(my_live, offset * CAP + my_rank, 0)
    lane = jnp.arange(n_pair * CAP, dtype=jnp.int32)
    match = (slot[None, :] == lane[:, None]) & my_live[None, :]
    back = jnp.sum(jnp.where(match, pos[None, :], 0), axis=1)
    back = ((my_tm - back // own + n_tm - 1) % n_tm) * own + back % own
    back = jnp.where(jnp.any(match, axis=1), back, -1)
    given = jnp.where(used > 0, pick, -1).reshape(1, -1)
    my_owned = lax.dynamic_slice_in_dim(my_live, my_tm * own, own).astype(jnp.float32)
    cosine = jnp.cos(freq_grid[:, None] * tau_grid[None, :])

    smem = pl.BlockSpec(memory_space=pltpu.SMEM)
    vmem = pl.BlockSpec(memory_space=pltpu.VMEM)
    hbm = pl.BlockSpec(memory_space=pl.ANY)
    bf16 = jnp.bfloat16
    DMA = pltpu.SemaphoreType.DMA
    step = size // CHUNKS
    thin = size // FAST_CHUNKS
    gathered = (
        jax.ShapeDtypeStruct((n_tm, own, size, width), bf16),
        jax.ShapeDtypeStruct((n_tm, own, size, width), bf16),
        jax.ShapeDtypeStruct((n_tm, 2 * own, width // LINE, LINE), jnp.float32),
    )
    fits, y_tab, z_tab, final = routes(n_pair, blocks, my_pair, live, source, held, rank)
    table = jnp.concatenate([slot, my_local, pick.reshape(-1), final, y_tab, z_tab]).astype(jnp.int32)

    def pooled(table, coefs, energies):
        total = sum(Z_CAPS)
        depth = blocks + (N_Y - 1) * Y_CAP + 2 * total
        return pl.pallas_call(
            functools.partial(fast_kernel, n_tm, n_pair, own, size),
            out_shape=gathered,
            in_specs=[smem, hbm, vmem],
            out_specs=(hbm, hbm, hbm),
            scratch_shapes=[
                pltpu.VMEM((blocks, size, width), bf16),
                pltpu.VMEM((blocks, width // LINE, LINE), jnp.float32),
            ]
            + [pltpu.VMEM((N_Y - 1, Y_CAP * size, width), bf16)] * 2
            + [pltpu.VMEM((2, total * size, width), bf16)] * 2
            + [
                pltpu.VMEM((CAP * n_pair, width // LINE, LINE), jnp.float32),
                pltpu.VMEM((CAP * n_pair, width // LINE, LINE), jnp.float32),
                pltpu.VMEM((n_tm, own, size, width), bf16),
                pltpu.VMEM((n_tm, own, size, width), bf16),
                pltpu.VMEM((n_tm, 2 * own, width // LINE, LINE), jnp.float32),
            ]
            + [pltpu.VMEM((depth, max(PARTS), width), bf16)] * POOLS
            + [
                DMA,
                DMA((FAST_CHUNKS,)),
                DMA,
                DMA((FAST_CHUNKS, len(Z_CAPS), 2)),
                DMA,
                DMA,
                DMA((2,)),
                DMA((2, FAST_CHUNKS)),
                DMA((2,)),
                DMA((3 + FAST_CHUNKS,)),
            ],
            compiler_params=pltpu.CompilerParams(
                collective_id=2, has_side_effects=True, vmem_limit_bytes=62 * 1024 * 1024
            ),
        )(table, coefs, energies)

    def direct(table, coefs, energies):
        return pl.pallas_call(
            functools.partial(gather_kernel, n_tm, n_pair, own, size),
            out_shape=gathered,
            in_specs=[smem] + [vmem] * 2,
            out_specs=(hbm, hbm, hbm),
            scratch_shapes=[pltpu.VMEM((CAP * n_pair, step, width), bf16)] * (2 * CHUNKS)
            + [
                pltpu.VMEM((CAP * n_pair, width // LINE, LINE), jnp.float32),
                pltpu.VMEM((CAP * n_pair, width // LINE, LINE), jnp.float32),
                pltpu.VMEM((n_tm, own, size, width), bf16),
                pltpu.VMEM((CHUNKS, n_tm, own, step, width), bf16),
                pltpu.VMEM((n_tm, 2 * own, width // LINE, LINE), jnp.float32),
                DMA((CHUNKS + 1,)),
                DMA((CHUNKS + 1,)),
                DMA((2,)),
                DMA((2, CHUNKS)),
                DMA((2,)),
                DMA((2 + CHUNKS,)),
                pltpu.VMEM((blocks, width // LINE, LINE), jnp.float32),
            ],
            compiler_params=pltpu.CompilerParams(
                collective_id=0, has_side_effects=True, vmem_limit_bytes=56 * 1024 * 1024
            ),
        )(table, coefs, energies)

    a_all, g_all, e_all = lax.cond(
        fits, pooled, direct, table, coefs, energies
    )

    screened, contrib = pl.pallas_call(
        functools.partial(entry_kernel, own, n_time),
        grid=(own,),
        out_shape=(
            jax.ShapeDtypeStruct((own, n_time, size, size), bf16),
            jax.ShapeDtypeStruct((own, n_tm, width), jnp.float32),
        ),
        in_specs=[
            pl.BlockSpec((n_tm, 1, size, width), lambda e: (0, e, 0, 0)),
            pl.BlockSpec((n_tm, 1, size, width), lambda e: (0, e, 0, 0)),
            pl.BlockSpec((n_tm, 2 * own, width // LINE, LINE), lambda e: (0, 0, 0, 0)),
            pl.BlockSpec((1, size, size), lambda e: (e, 0, 0)),
            smem, smem, smem,
        ],
        out_specs=(
            pl.BlockSpec((1, n_time, size, size), lambda e: (e, 0, 0, 0)),
            pl.BlockSpec((1, n_tm, width), lambda e: (e, 0, 0)),
        ),
        scratch_shapes=[
            pltpu.VMEM((size, n_tm * width), bf16),
            pltpu.VMEM((n_time, size, n_tm * width), bf16),
            pltpu.VMEM((8, n_tm * width), jnp.float32),
        ],
        compiler_params=pltpu.CompilerParams(vmem_limit_bytes=48 * 1024 * 1024),
    )(a_all, g_all, e_all, coulomb[0], cosine, tau_grid, my_owned)

    self_energy = pl.pallas_call(
        functools.partial(return_kernel, n_tm, n_pair, own),
        out_shape=jax.ShapeDtypeStruct((blocks, width), jnp.float32),
        in_specs=[smem, vmem, vmem],
        out_specs=vmem,
        scratch_shapes=[
            pltpu.VMEM((n_tm, 8, width), jnp.float32),
            pltpu.VMEM((n_tm, 8, width), jnp.float32),
            pltpu.VMEM((CAP * n_pair, width // LINE, LINE), jnp.float32),
            pltpu.VMEM((CAP * n_pair, width // LINE, LINE), jnp.float32),
            DMA((2,)),
            DMA((2,)),
        ],
        compiler_params=pltpu.CompilerParams(collective_id=1, has_side_effects=True),
    )(back, contrib, given)
    return (screened[None], self_energy)


def solution(mesh):
    return jax.shard_map(
        functools.partial(body, mesh.shape["tm"], mesh.shape["pair"]),
        mesh=mesh,
        in_specs=(
            P("pair", None, "tm"),
            P("pair", "tm"),
            P("pair", "tm", None, None),
            P(),
            P(),
            P(),
        ),
        out_specs=(P("pair", "tm", None, None, None), P("pair", "tm")),
        check_vma=False,
    )
```

```python
import functools
import math

import jax
import jax.numpy as jnp
import numpy as np
from jax import lax
from jax.experimental import pallas as pl
from jax.experimental.pallas import tpu as pltpu
from jax.sharding import PartitionSpec as P

CAP = 2
CHUNKS = 4
PARTS = (32,) * 8
FAST_CHUNKS = len(PARTS)
Y_CAP = 15
Z_CAPS = (10, 9, 9, 8)
LINE = 128
N_Y = 4
POOLS = 3
MESH = pl.DeviceIdType.MESH


def greet(n_tm, n_pair, my_tm, my_pair):
    barrier = pltpu.get_barrier_semaphore()

    def pair_peer(i, c):
        other = lax.rem(my_pair + i, n_pair)
        pl.semaphore_signal(barrier, inc=1, device_id=(my_tm, other), device_id_type=MESH)
        return c

    def tm_peer(i, c):
        other = lax.rem(my_tm + i, n_tm)
        pl.semaphore_signal(barrier, inc=1, device_id=(other, my_pair), device_id_type=MESH)
        return c

    lax.fori_loop(1, n_pair, pair_peer, 0)
    lax.fori_loop(1, n_tm, tm_peer, 0)
    return lambda: pl.semaphore_wait(barrier, n_pair + n_tm - 2)


class View:
    def __init__(self, ref, at):
        self.ref, self.at = ref, at

    def __getitem__(self, i):
        return self.ref[self.at + i]


def views(table, listed, n_pair):
    sizes = (listed, listed, CAP * n_pair, listed, (N_Y - 1) * Y_CAP)
    at = [sum(sizes[:i]) for i in range(len(sizes) + 1)]
    return [View(table, i) for i in at]


def spread(flat_ref, tile_ref):
    flat = flat_ref[...].astype(jnp.float32)
    for h in range(flat.shape[1] // LINE):
        tile_ref[:, h, :] = flat[:, h * LINE : (h + 1) * LINE]


def wait_bytes(ref, sem):
    pltpu.make_async_copy(ref, ref, sem).wait()


def gather_kernel(
    n_tm, n_pair, own, rows,
    table_ref, coef_ref, ener_in,
    a_out, g_out, e_out,
    *scratch,
):
    slot_ref, local_ref, pick_ref = views(table_ref, n_tm * own, n_pair)[:3]
    my_tm, my_pair = lax.axis_index("tm"), lax.axis_index("pair")
    sends, recvs = scratch[:CHUNKS], scratch[CHUNKS : 2 * CHUNKS]
    (e_send, e_recv, a_send, g_send, x_ener,
     pair_send, pair_recv, a_sems, g_sems, e_sems, own_sems, ener_ref) = scratch[2 * CHUNKS :]
    peers, others = n_pair - 1, n_tm - 1
    step = rows // CHUNKS
    spread(ener_in, ener_ref)
    greet(n_tm, n_pair, my_tm, my_pair)()

    def pair_copy(i, c):
        target = lax.rem(my_pair + i + 1, n_pair)
        return pltpu.make_async_remote_copy(
            src_ref=sends[c].at[pl.ds(CAP * i, CAP)],
            dst_ref=recvs[c].at[pl.ds(CAP * i, CAP)],
            send_sem=pair_send.at[c], recv_sem=pair_recv.at[c],
            device_id=(my_tm, target), device_id_type=MESH,
        )

    def ener_copy(i):
        target = lax.rem(my_pair + i + 1, n_pair)
        return pltpu.make_async_remote_copy(
            src_ref=e_send.at[pl.ds(CAP * i, CAP)], dst_ref=e_recv.at[pl.ds(CAP * i, CAP)],
            send_sem=pair_send.at[CHUNKS], recv_sem=pair_recv.at[CHUNKS],
            device_id=(my_tm, target), device_id_type=MESH,
        )


    def stage_a(u):
        owner = lax.rem(my_tm + u + 1, n_tm)
        for e in range(own):
            a_send[u, e] = coef_ref[local_ref[owner * own + e]]
        return owner

    def send_pair(c):
        def one(i, carry):
            for j in range(CAP):
                sends[c][CAP * i + j] = coef_ref[pick_ref[CAP * i + j], pl.ds(c * step, step), :]
            pair_copy(i, c).start()
            return carry

        lax.fori_loop(0, peers, one, 0)
        for j in range(CAP):
            recvs[c][CAP * peers + j] = coef_ref[pick_ref[CAP * peers + j], pl.ds(c * step, step), :]

    def send_ener(i, carry):
        for j in range(CAP):
            e_send[CAP * i + j] = ener_ref[pick_ref[CAP * i + j]]
        ener_copy(i).start()
        return carry

    def keep_ener():
        for j in range(CAP * peers, CAP * n_pair):
            e_recv[j] = ener_ref[pick_ref[j]]

    def a_one(u, carry):
        owner = stage_a(u)
        pltpu.make_async_remote_copy(
            src_ref=a_send.at[u], dst_ref=a_out.at[my_tm],
            send_sem=a_sems.at[0], recv_sem=a_sems.at[1],
            device_id=(owner, my_pair), device_id_type=MESH,
        ).start()
        return carry

    send_pair(0)
    lax.fori_loop(0, others, a_one, 0)
    stage_a(others)
    own_a = pltpu.make_async_copy(a_send.at[others], a_out.at[my_tm], own_sems.at[0])
    own_a.start()
    lax.fori_loop(0, peers, send_ener, 0)
    keep_ener()
    for c in range(1, CHUNKS):
        send_pair(c)

    owned_g = []
    for c in range(CHUNKS):
        wait_bytes(recvs[c].at[pl.ds(0, CAP * peers)], pair_recv.at[c])

        def stage_g(u):
            owner = lax.rem(my_tm + u + 1, n_tm)
            for e in range(own):
                g_send[c, u, e] = recvs[c][slot_ref[owner * own + e]]
            return owner

        def g_one(u, carry):
            owner = stage_g(u)
            pltpu.make_async_remote_copy(
                src_ref=g_send.at[c, u], dst_ref=g_out.at[my_tm, :, pl.ds(c * step, step)],
                send_sem=g_sems.at[0, c], recv_sem=g_sems.at[1, c],
                device_id=(owner, my_pair), device_id_type=MESH,
            ).start()
            return carry

        lax.fori_loop(0, others, g_one, 0)
        stage_g(others)
        copy = pltpu.make_async_copy(g_send.at[c, others], g_out.at[my_tm, :, pl.ds(c * step, step)], own_sems.at[1 + c])
        copy.start()
        owned_g.append(copy)
        if c == 0:
            wait_bytes(e_recv.at[pl.ds(0, CAP * peers)], pair_recv.at[CHUNKS])

            def stage_x(u):
                owner = lax.rem(my_tm + u + 1, n_tm)
                for e in range(own):
                    x_ener[u, e] = e_recv[slot_ref[owner * own + e]]
                    x_ener[u, own + e] = ener_ref[local_ref[owner * own + e]]
                return owner

            def x_one(u, carry):
                owner = stage_x(u)
                pltpu.make_async_remote_copy(
                    src_ref=x_ener.at[u], dst_ref=e_out.at[my_tm],
                    send_sem=e_sems.at[0], recv_sem=e_sems.at[1],
                    device_id=(owner, my_pair), device_id_type=MESH,
                ).start()
                return carry

            lax.fori_loop(0, others, x_one, 0)
            stage_x(others)
            own_e = pltpu.make_async_copy(x_ener.at[others], e_out.at[my_tm], own_sems.at[1 + CHUNKS])
            own_e.start()

    for c in range(CHUNKS):
        wait_bytes(sends[c].at[pl.ds(0, CAP * peers)], pair_send.at[c])
    wait_bytes(e_send.at[pl.ds(0, CAP * peers)], pair_send.at[CHUNKS])
    for side in range(2):
        wait_bytes(a_send.at[pl.ds(0, others)], a_sems.at[side])
        wait_bytes(x_ener.at[pl.ds(0, others)], e_sems.at[side])
        for c in range(CHUNKS):
            wait_bytes(g_send.at[c, pl.ds(0, others)], g_sems.at[side, c])
    own_a.wait()
    own_e.wait()
    for copy in owned_g:
        copy.wait()


def fast_kernel(
    n_tm, n_pair, own, rows,
    table_ref, coef_hbm, ener_in,
    a_out, g_out, e_out,
    coef_ref, ener_ref, y_send, y_recv, z_send, z_recv, e_send, e_recv, a_send, x_send, x_ener, *rest,
):
    slot_ref, local_ref, pick_ref, final_ref, y_ref, z_ref = views(table_ref, n_tm * own, n_pair)
    pools = rest[:POOLS]
    (y_ssem, y_rsem, z_ssem, z_rsem, pair_send, pair_recv, a_sems, g_sems, e_sems, own_sems) = rest[POOLS:]
    my_tm, my_pair = lax.axis_index("tm"), lax.axis_index("pair")
    peers, others = n_pair - 1, n_tm - 1
    n_z = n_pair // N_Y
    my_y, my_z = my_pair // n_z, lax.rem(my_pair, n_z)
    assert sum(PARTS) == rows
    begin = [sum(PARTS[:c]) for c in range(FAST_CHUNKS)]
    spans = [pl.ds(begin[c], PARTS[c]) for c in range(FAST_CHUNKS)]
    y_rows = [pl.ds(Y_CAP * begin[c], Y_CAP * PARTS[c]) for c in range(FAST_CHUNKS)]
    blocks, _, width = coef_ref.shape
    y_slots = (N_Y - 1) * Y_CAP
    ahead = (my_y * n_z + lax.rem(my_z + 1, n_z), my_y * n_z + lax.rem(my_z + n_z - 1, n_z))
    firsts = [sum(Z_CAPS[:r]) for r in range(len(Z_CAPS) + 1)]
    load = pltpu.make_async_copy(coef_hbm, coef_ref, own_sems.at[2 + FAST_CHUNKS])
    load.start()
    met = greet(n_tm, n_pair, my_tm, my_pair)
    spread(ener_in, ener_ref)
    load.wait()

    def ener_copy(i):
        target = lax.rem(my_pair + i + 1, n_pair)
        return pltpu.make_async_remote_copy(
            src_ref=e_send.at[pl.ds(CAP * i, CAP)], dst_ref=e_recv.at[pl.ds(CAP * i, CAP)],
            send_sem=pair_send, recv_sem=pair_recv,
            device_id=(my_tm, target), device_id_type=MESH,
        )

    def send_ener(i, carry):
        for j in range(CAP):
            e_send[CAP * i + j] = ener_ref[pick_ref[CAP * i + j]]
        ener_copy(i).start()
        return carry

    def keep_ener():
        for j in range(CAP * peers, CAP * n_pair):
            e_recv[j] = ener_ref[pick_ref[j]]

    def stage_y(c):
        for i in range(N_Y - 1):
            def one(j, carry):
                y_send[i, pl.ds(pl.multiple_of(Y_CAP * begin[c] + j * PARTS[c], 16), PARTS[c]), :] = coef_ref[y_ref[i * Y_CAP + j], spans[c], :]
                return carry

            lax.fori_loop(0, Y_CAP, one, 0)

    def start_y(c):
        for i in range(N_Y - 1):
            target = lax.rem(my_y + i + 1, N_Y) * n_z + my_z
            pltpu.make_async_remote_copy(
                src_ref=y_send.at[i, y_rows[c]], dst_ref=y_recv.at[i, y_rows[c]],
                send_sem=y_ssem, recv_sem=y_rsem.at[c],
                device_id=(my_tm, target), device_id_type=MESH,
            ).start()

    def send_y(c):
        stage_y(c)
        start_y(c)

    def fill(c):
        pool = pools[c % POOLS]
        held = pl.ds(0, PARTS[c])
        pool[pl.ds(0, blocks), held] = coef_ref[:, spans[c], :]
        wait_bytes(y_recv.at[:, y_rows[c]], y_rsem.at[c])
        for i in range(N_Y - 1):
            pool[pl.ds(blocks + i * Y_CAP, Y_CAP), held] = y_recv[i, y_rows[c]].reshape(Y_CAP, PARTS[c], width)

    def span(c, r, way):
        return (way, pl.ds(firsts[-1] * begin[c] + firsts[r] * PARTS[c], Z_CAPS[r] * PARTS[c]))

    def send_z(c, r):
        pool = pools[c % POOLS]
        for way in range(2):
            base = (2 * r + way) * Z_CAPS[0]

            def one(j, carry):
                at = firsts[-1] * begin[c] + (firsts[r] + j) * PARTS[c]
                z_send[way, pl.ds(pl.multiple_of(at, 16), PARTS[c]), :] = pool[z_ref[base + j], pl.ds(0, PARTS[c])]
                return carry

            lax.fori_loop(0, Z_CAPS[r], one, 0)
            pltpu.make_async_remote_copy(
                src_ref=z_send.at[span(c, r, way)], dst_ref=z_recv.at[span(c, r, way)],
                send_sem=z_ssem, recv_sem=z_rsem.at[c, r, way],
                device_id=(my_tm, ahead[way]), device_id_type=MESH,
            ).start()

    def take_z(c, r):
        pool = pools[c % POOLS]
        for way in range(2):
            wait_bytes(z_recv.at[span(c, r, way)], z_rsem.at[c, r, way])
            at = blocks + y_slots + way * firsts[-1] + firsts[r]
            pool[pl.ds(at, Z_CAPS[r]), pl.ds(0, PARTS[c])] = z_recv[span(c, r, way)].reshape(Z_CAPS[r], PARTS[c], width)

    def stage_a(u):
        owner = lax.rem(my_tm + u + 1, n_tm)
        for e in range(own):
            a_send[u, e] = coef_ref[local_ref[owner * own + e]]
        return owner

    def a_one(u, carry):
        owner = stage_a(u)
        pltpu.make_async_remote_copy(
            src_ref=a_send.at[u], dst_ref=a_out.at[my_tm],
            send_sem=a_sems.at[0], recv_sem=a_sems.at[1],
            device_id=(owner, my_pair), device_id_type=MESH,
        ).start()
        return carry

    def send_x(c):
        pool = pools[c % POOLS]
        part = spans[c]

        def stage_g(u):
            owner = lax.rem(my_tm + u + 1, n_tm)
            for e in range(own):
                x_send[u, e, part] = pool[final_ref[owner * own + e], pl.ds(0, PARTS[c])]
            return owner

        def g_one(u, carry):
            owner = stage_g(u)
            pltpu.make_async_remote_copy(
                src_ref=x_send.at[u, :, part], dst_ref=g_out.at[my_tm, :, part],
                send_sem=g_sems.at[0, c], recv_sem=g_sems.at[1, c],
                device_id=(owner, my_pair), device_id_type=MESH,
            ).start()
            return carry

        lax.fori_loop(0, others, g_one, 0)
        stage_g(others)
        pltpu.make_async_copy(x_send.at[others, :, part], g_out.at[my_tm, :, part], own_sems.at[1 + c]).start()

    def send_x_ener():
        wait_bytes(e_recv.at[pl.ds(0, CAP * peers)], pair_recv)

        def stage_x(u):
            owner = lax.rem(my_tm + u + 1, n_tm)
            for e in range(own):
                x_ener[u, e] = e_recv[slot_ref[owner * own + e]]
                x_ener[u, own + e] = ener_ref[local_ref[owner * own + e]]
            return owner

        def x_one(u, carry):
            owner = stage_x(u)
            pltpu.make_async_remote_copy(
                src_ref=x_ener.at[u], dst_ref=e_out.at[my_tm],
                send_sem=e_sems.at[0], recv_sem=e_sems.at[1],
                device_id=(owner, my_pair), device_id_type=MESH,
            ).start()
            return carry

        lax.fori_loop(0, others, x_one, 0)
        stage_x(others)
        pltpu.make_async_copy(x_ener.at[others], e_out.at[my_tm], own_sems.at[1 + FAST_CHUNKS]).start()

    def own_a():
        stage_a(others)
        pltpu.make_async_copy(a_send.at[others], a_out.at[my_tm], own_sems.at[0]).start()

    tasks = [functools.partial(lax.fori_loop, u, u + 1, a_one, 0) for u in range(others)]
    tasks.append(own_a)
    few = 4
    for i in range(0, peers, few):
        tasks.append(functools.partial(lax.fori_loop, i, min(i + few, peers), send_ener, 0))
    tasks.append(keep_ener)

    def spare():
        if tasks:
            tasks.pop(0)()

    last = len(Z_CAPS) - 1
    sent_ener = False
    stage_y(0)
    met()
    start_y(0)
    send_y(1)
    fill(0)
    send_z(0, 0)
    send_y(2)
    fill(1)
    send_z(1, 0)
    send_y(3)
    spare()
    for first in range(0, FAST_CHUNKS, 2):
        second = first + 1
        more = first + 2 < FAST_CHUNKS
        for r in range(last):
            take_z(first, r)
            send_z(first, r + 1)
            spare()
            take_z(second, r)
            send_z(second, r + 1)
            spare()
            if first + 4 + r < FAST_CHUNKS and r < 2:
                send_y(first + 4 + r)
        if more:
            fill(first + 2)
            send_z(first + 2, 0)
        take_z(first, last)
        send_x(first)
        if more:
            fill(first + 3)
            send_z(first + 3, 0)
        take_z(second, last)
        send_x(second)
        if not tasks and not sent_ener:
            sent_ener = True
            send_x_ener()
    assert sent_ener

    wait_bytes(y_send, y_ssem)
    wait_bytes(z_send, z_ssem)
    wait_bytes(e_send.at[pl.ds(0, CAP * peers)], pair_send)
    pltpu.make_async_copy(a_send.at[others], a_out.at[my_tm], own_sems.at[0]).wait()
    for side in range(2):
        wait_bytes(a_send.at[pl.ds(0, others)], a_sems.at[side])
        wait_bytes(x_ener.at[pl.ds(0, others)], e_sems.at[side])
        for c in range(FAST_CHUNKS):
            wait_bytes(x_send.at[pl.ds(0, others), :, spans[c]], g_sems.at[side, c])
    for c in range(FAST_CHUNKS):
        part = spans[c]
        pltpu.make_async_copy(x_send.at[others, :, part], g_out.at[my_tm, :, part], own_sems.at[1 + c]).wait()
    pltpu.make_async_copy(x_ener.at[others], e_out.at[my_tm], own_sems.at[1 + FAST_CHUNKS]).wait()


def half_way(n_z, z_key):
    half = n_z // 2
    node = np.arange(n_z)
    gap = (node[:, None] - node[None, :]) % n_z
    count = jnp.sum((z_key[:, :, None] == node).astype(jnp.bfloat16), axis=1)
    masks = []
    for way in range(2):
        trip = gap if way == 0 else (-gap) % n_z
        from_start = trip
        passes = (trip[:, :, None] < half) & (from_start.T[None, :, :] < trip[:, :, None])
        masks.append(passes.reshape(n_z * n_z, n_z))
    opposite = (gap == half).reshape(n_z * n_z, 1) & (np.arange(n_z * n_z)[:, None] % n_z == node[None, :])
    masks.append(opposite)
    mask = jnp.asarray(np.concatenate(masks, axis=1), jnp.bfloat16)
    sums = jnp.dot(count.reshape(N_Y, n_z * n_z), mask, preferred_element_type=jnp.float32).astype(jnp.int32)
    up, down, there = sums[:, :n_z], sums[:, n_z : 2 * n_z], sums[:, 2 * n_z :]
    most = lambda v, by: functools.reduce(jnp.maximum, [jnp.roll(v, by * h, axis=1) for h in range(half)])
    busy = (most(up, -1), most(down, 1))
    even = ((np.arange(N_Y)[:, None] + node[None, :]) % 2 == 0).astype(np.int32)
    return jnp.clip((there * 32 + 8 * (busy[1] - busy[0]) + 32 * even) // 64, 0, there)


def routes(n_pair, blocks, my_pair, live, source, held, rank):
    listed = live.shape[1]
    n_z = n_pair // N_Y
    n = n_z * listed
    my_y, my_z = my_pair // n_z, my_pair % n_z
    rows = jnp.arange(n_pair, dtype=jnp.int32)
    mine = source == my_pair
    per_row = jnp.sum(mine.astype(jnp.int32), axis=1)
    same = (rows[:, None] // n_z == rows[None, :] // n_z) & (rows[None, :] < rows[:, None])
    first = jnp.sum(jnp.where(same, per_row[None, :], 0), axis=1)
    place = jnp.where(mine, first[:, None] + rank, -1).reshape(N_Y, 1, n)
    want = jnp.arange(Y_CAP, dtype=jnp.int32)[None, :, None]
    y_tab = jnp.sum(jnp.where(place == want, held.reshape(N_Y, 1, n), 0), axis=2)
    y_tab = lax.dynamic_slice_in_dim(jnp.concatenate([y_tab, y_tab]), my_y + 1, N_Y - 1)
    ring_source = source.reshape(N_Y, n)
    ids = jnp.arange(n, dtype=jnp.int32)
    earlier = ids[:, None] < ids[None, :]
    y_same = (ring_source[:, :, None] == ring_source[:, None, :]) & earlier[None]
    y_rank = jnp.sum(y_same.astype(jnp.int32), axis=1)
    off_ring = live.reshape(N_Y, n) & (ring_source // n_z != jnp.arange(N_Y)[:, None])
    y_over = jnp.where(off_ring, y_rank, 0) - (Y_CAP - 1)

    pos_in = jnp.arange(listed, dtype=jnp.int32)
    z_key = jnp.where(live, source % n_z, -1)
    z_same = (z_key[:, :, None] == z_key[:, None, :]) & (pos_in[:, None] < pos_in[None, :])[None]
    z_rank = jnp.sum(z_same.astype(jnp.int32), axis=1).reshape(N_Y, n)
    zd = ids // listed
    zs = ring_source % n_z
    delta = (zd[None, :] - zs) % n_z
    half = n_z // 2
    share = half_way(n_z, z_key)
    mine_share = jnp.sum(jnp.where(zs[None] == jnp.arange(n_z)[:, None, None], share.T[:, :, None], 0), axis=0)
    plus = (delta < half) | ((delta == half) & (z_rank < mine_share))
    way = jnp.where(plus, 0, 1)
    rem = jnp.where(live.reshape(N_Y, n), jnp.where(plus, delta, n_z - delta), 0)
    pos = zs

    ring = lambda v: lax.dynamic_index_in_dim(v, my_y, 0, keepdims=False)
    src, my_way = ring(ring_source), ring(way)
    step_y = (my_y - src // n_z) % N_Y
    loc = jnp.where(step_y == 0, ring(held.reshape(N_Y, n)), blocks + (step_y - 1) * Y_CAP + ring(y_rank))
    loc = jnp.where(src >= 0, loc, 0)
    total = sum(Z_CAPS)
    tables, begun = [], 0
    slots = jnp.arange(Z_CAPS[0], dtype=jnp.int32)
    for cap in Z_CAPS:
        group = jnp.where(rem > 0, pos * 2 + way, -1)
        key = rem * n - ids[None, :]
        ahead = (group[:, :, None] == group[:, None, :]) & (key[:, :, None] > key[:, None, :])
        order = jnp.sum(ahead.astype(jnp.int32), axis=1)
        moved = (rem > 0) & (order < cap)
        my_order, my_moved, my_group = ring(order), ring(moved), ring(group)
        for w in range(2):
            here = jnp.where(my_moved & (my_group == my_z * 2 + w), my_order, -1)
            tables.append(jnp.sum(jnp.where(here[None, :] == slots[:, None], loc[None, :], 0), axis=1))
        loc = jnp.where(my_moved, blocks + (N_Y - 1) * Y_CAP + my_way * total + begun + my_order, loc)
        pos = jnp.where(moved, (pos + jnp.where(plus, 1, n_z - 1)) % n_z, pos)
        rem = rem - moved.astype(jnp.int32)
        begun += cap
    final = lax.dynamic_slice_in_dim(loc, my_z * listed, listed)
    fits = jnp.maximum(jnp.max(rem), jnp.max(y_over)) <= 0
    return fits, y_tab.reshape(-1), jnp.concatenate(tables), final


def entry_kernel(own, n_time, a_ref, g_ref, e_ref, tile_ref, cos_ref, tau_ref, live_ref, w_ref, c_ref, x_ref, y_ref, s_ref):
    e = pl.program_id(0)
    slices, _, size, width = a_ref.shape
    live = live_ref[e]
    lines = lambda v: jnp.concatenate([v[i : i + 1] for i in range(v.shape[0])], axis=1)
    for m in range(slices):
        span = pl.ds(m * width, width)
        x_ref[:, span] = a_ref[m, 0]
        rate = lines(e_ref[m, e] + e_ref[m, own + e])
        g = g_ref[m, 0].astype(jnp.float32)
        for t in range(n_time):
            decay = jnp.exp(-tau_ref[t] * rate)
            s_ref[pl.ds(t, 1), span] = decay
            y_ref[t, :, span] = (g * decay).astype(jnp.bfloat16)
    chi = []
    for t in range(n_time):
        chi.append(live * lax.dot_general(
            x_ref[...], y_ref[t], (((1,), (1,)), ((), ())), preferred_element_type=jnp.float32
        ))
    wfreq = []
    for w in range(n_time):
        chiw = sum(cos_ref[w, t] * chi[t] for t in range(n_time)).astype(jnp.bfloat16)
        prod = jnp.dot(chiw, tile_ref[0], preferred_element_type=jnp.float32)
        prod_b = prod.astype(jnp.bfloat16)
        wfreq.append(
            prod + jnp.dot(prod_b, prod_b, preferred_element_type=jnp.float32) * (1.0 / math.sqrt(size))
        )
    for t in range(n_time):
        w_ref[0, t] = (sum(cos_ref[w, t] * wfreq[w] for w in range(n_time)) * (1.0 / n_time)).astype(jnp.bfloat16)
    screened = w_ref[0].reshape(n_time * size, size)
    for m in range(slices):
        span = pl.ds(m * width, width)
        wy = jnp.dot(screened, g_ref[m, 0], preferred_element_type=jnp.float32)
        a = a_ref[m, 0].astype(jnp.float32)
        total = jnp.zeros((1, width), jnp.float32)
        for t in range(n_time):
            part = jnp.sum(a * wy[t * size : (t + 1) * size], axis=0, keepdims=True)
            total = total + s_ref[pl.ds(t, 1), span] * part
        c_ref[0, pl.ds(m, 1), :] = total * (1.0 / n_time)


def return_kernel(
    n_tm, n_pair, own,
    back_ref, contrib_ref, given_ref,
    out_ref,
    c_send, c_recv, p_send, p_recv, tm_sems, pair_sems,
):
    my_tm, my_pair = lax.axis_index("tm"), lax.axis_index("pair")
    peers, others = n_pair - 1, n_tm - 1
    width = out_ref.shape[1]
    met = greet(n_tm, n_pair, my_tm, my_pair)
    c_send[...] = jnp.zeros_like(c_send)

    def stage_c(u):
        owner = lax.rem(my_tm + u + 1, n_tm)
        for e in range(own):
            c_send[u, pl.ds(e, 1), :] = contrib_ref[e, pl.ds(owner, 1), :]
        return owner

    def tm_one(u, carry):
        owner = lax.rem(my_tm + u + 1, n_tm)
        pltpu.make_async_remote_copy(
            src_ref=c_send.at[u], dst_ref=c_recv.at[u],
            send_sem=tm_sems.at[0], recv_sem=tm_sems.at[1],
            device_id=(owner, my_pair), device_id_type=MESH,
        ).start()
        return carry

    for u in range(n_tm):
        stage_c(u)
    met()
    lax.fori_loop(0, others, tm_one, 0)
    block_id = lax.broadcasted_iota(jnp.int32, (out_ref.shape[0], CAP * n_pair), 0)
    owning = (block_id == given_ref[...]).astype(jnp.float32)
    wait_bytes(c_recv.at[pl.ds(0, others)], tm_sems.at[1])
    c_recv[others] = c_send[others]

    def stage_p(i):
        for j in range(CAP):
            at = back_ref[CAP * i + j]
            keep = jnp.where(at >= 0, 1.0, 0.0)
            at = jnp.maximum(at, 0)
            line = c_recv[at // own, pl.ds(lax.rem(at, own), 1), :] * keep
            for h in range(width // LINE):
                p_send[CAP * i + j, pl.ds(h, 1), :] = line[:, h * LINE : (h + 1) * LINE]

    def pair_one(i, carry):
        stage_p(i)
        target = lax.rem(my_pair + n_pair - 1 - i, n_pair)
        pltpu.make_async_remote_copy(
            src_ref=p_send.at[pl.ds(CAP * i, CAP)], dst_ref=p_recv.at[pl.ds(CAP * i, CAP)],
            send_sem=pair_sems.at[0], recv_sem=pair_sems.at[1],
            device_id=(my_tm, target), device_id_type=MESH,
        ).start()
        return carry

    lax.fori_loop(0, peers, pair_one, 0)
    stage_p(peers)
    wait_bytes(p_recv.at[pl.ds(0, CAP * peers)], pair_sems.at[1])
    for j in range(CAP * peers, CAP * n_pair):
        p_recv[j] = p_send[j]
    for h in range(width // LINE):
        out_ref[:, pl.ds(h * LINE, LINE)] = jnp.dot(
            owning, p_recv[:, h, :], precision=lax.Precision.HIGHEST, preferred_element_type=jnp.float32
        )
    wait_bytes(c_send.at[pl.ds(0, others)], tm_sems.at[0])
    wait_bytes(p_send.at[pl.ds(0, CAP * peers)], pair_sems.at[0])


def body(n_tm, n_pair, coefs, energies, coulomb, tau_grid, freq_grid, pairs):
    blocks, size, width = coefs.shape
    n_time = tau_grid.shape[0]
    listed = pairs.shape[1]
    own = listed // n_tm
    my_tm, my_pair = lax.axis_index("tm"), lax.axis_index("pair")
    remote, local = pairs[:, :, 0], pairs[:, :, 1]
    live = remote >= 0
    source = jnp.where(live, remote // blocks, -1)
    held = remote % blocks
    pos = jnp.arange(listed, dtype=jnp.int32)
    before = (source[:, :, None] == source[:, None, :]) & (pos[:, None] < pos[None, :])[None]
    rank = jnp.sum(before.astype(jnp.int32), axis=1)
    slots = jnp.arange(CAP, dtype=jnp.int32)
    hit = (source == my_pair)[:, None, :] & (rank[:, None, :] == slots[None, :, None])
    pick = jnp.sum(jnp.where(hit, held[:, None, :], 0), axis=2)
    used = jnp.sum(hit.astype(jnp.int32), axis=2)
    turn = lambda v: lax.dynamic_slice_in_dim(jnp.concatenate([v, v]), my_pair + 1, n_pair)
    pick, used = turn(pick), turn(used)
    row = lambda v: lax.dynamic_index_in_dim(v, my_pair, 0, keepdims=False)
    my_live, my_source, my_rank = row(live), row(source), row(rank)
    my_local = jnp.where(my_live, row(local), 0)
    offset = (my_pair - my_source + n_pair - 1) % n_pair
    slot = jnp.where(my_live, offset * CAP + my_rank, 0)
    lane = jnp.arange(n_pair * CAP, dtype=jnp.int32)
    match = (slot[None, :] == lane[:, None]) & my_live[None, :]
    back = jnp.sum(jnp.where(match, pos[None, :], 0), axis=1)
    back = ((my_tm - back // own + n_tm - 1) % n_tm) * own + back % own
    back = jnp.where(jnp.any(match, axis=1), back, -1)
    given = jnp.where(used > 0, pick, -1).reshape(1, -1)
    my_owned = lax.dynamic_slice_in_dim(my_live, my_tm * own, own).astype(jnp.float32)
    cosine = jnp.cos(freq_grid[:, None] * tau_grid[None, :])

    smem = pl.BlockSpec(memory_space=pltpu.SMEM)
    vmem = pl.BlockSpec(memory_space=pltpu.VMEM)
    hbm = pl.BlockSpec(memory_space=pl.ANY)
    bf16 = jnp.bfloat16
    DMA = pltpu.SemaphoreType.DMA
    step = size // CHUNKS
    thin = size // FAST_CHUNKS
    gathered = (
        jax.ShapeDtypeStruct((n_tm, own, size, width), bf16),
        jax.ShapeDtypeStruct((n_tm, own, size, width), bf16),
        jax.ShapeDtypeStruct((n_tm, 2 * own, width // LINE, LINE), jnp.float32),
    )
    fits, y_tab, z_tab, final = routes(n_pair, blocks, my_pair, live, source, held, rank)
    table = jnp.concatenate([slot, my_local, pick.reshape(-1), final, y_tab, z_tab]).astype(jnp.int32)

    def pooled(table, coefs, energies):
        total = sum(Z_CAPS)
        depth = blocks + (N_Y - 1) * Y_CAP + 2 * total
        return pl.pallas_call(
            functools.partial(fast_kernel, n_tm, n_pair, own, size),
            out_shape=gathered,
            in_specs=[smem, hbm, vmem],
            out_specs=(hbm, hbm, hbm),
            scratch_shapes=[
                pltpu.VMEM((blocks, size, width), bf16),
                pltpu.VMEM((blocks, width // LINE, LINE), jnp.float32),
            ]
            + [pltpu.VMEM((N_Y - 1, Y_CAP * size, width), bf16)] * 2
            + [pltpu.VMEM((2, total * size, width), bf16)] * 2
            + [
                pltpu.VMEM((CAP * n_pair, width // LINE, LINE), jnp.float32),
                pltpu.VMEM((CAP * n_pair, width // LINE, LINE), jnp.float32),
                pltpu.VMEM((n_tm, own, size, width), bf16),
                pltpu.VMEM((n_tm, own, size, width), bf16),
                pltpu.VMEM((n_tm, 2 * own, width // LINE, LINE), jnp.float32),
            ]
            + [pltpu.VMEM((depth, max(PARTS), width), bf16)] * POOLS
            + [
                DMA,
                DMA((FAST_CHUNKS,)),
                DMA,
                DMA((FAST_CHUNKS, len(Z_CAPS), 2)),
                DMA,
                DMA,
                DMA((2,)),
                DMA((2, FAST_CHUNKS)),
                DMA((2,)),
                DMA((3 + FAST_CHUNKS,)),
            ],
            compiler_params=pltpu.CompilerParams(
                collective_id=2, has_side_effects=True, vmem_limit_bytes=62 * 1024 * 1024
            ),
        )(table, coefs, energies)

    def direct(table, coefs, energies):
        return pl.pallas_call(
            functools.partial(gather_kernel, n_tm, n_pair, own, size),
            out_shape=gathered,
            in_specs=[smem] + [vmem] * 2,
            out_specs=(hbm, hbm, hbm),
            scratch_shapes=[pltpu.VMEM((CAP * n_pair, step, width), bf16)] * (2 * CHUNKS)
            + [
                pltpu.VMEM((CAP * n_pair, width // LINE, LINE), jnp.float32),
                pltpu.VMEM((CAP * n_pair, width // LINE, LINE), jnp.float32),
                pltpu.VMEM((n_tm, own, size, width), bf16),
                pltpu.VMEM((CHUNKS, n_tm, own, step, width), bf16),
                pltpu.VMEM((n_tm, 2 * own, width // LINE, LINE), jnp.float32),
                DMA((CHUNKS + 1,)),
                DMA((CHUNKS + 1,)),
                DMA((2,)),
                DMA((2, CHUNKS)),
                DMA((2,)),
                DMA((2 + CHUNKS,)),
                pltpu.VMEM((blocks, width // LINE, LINE), jnp.float32),
            ],
            compiler_params=pltpu.CompilerParams(
                collective_id=0, has_side_effects=True, vmem_limit_bytes=56 * 1024 * 1024
            ),
        )(table, coefs, energies)

    a_all, g_all, e_all = lax.cond(
        fits, pooled, direct, table, coefs, energies
    )

    screened, contrib = pl.pallas_call(
        functools.partial(entry_kernel, own, n_time),
        grid=(own,),
        out_shape=(
            jax.ShapeDtypeStruct((own, n_time, size, size), bf16),
            jax.ShapeDtypeStruct((own, n_tm, width), jnp.float32),
        ),
        in_specs=[
            pl.BlockSpec((n_tm, 1, size, width), lambda e: (0, e, 0, 0)),
            pl.BlockSpec((n_tm, 1, size, width), lambda e: (0, e, 0, 0)),
            pl.BlockSpec((n_tm, 2 * own, width // LINE, LINE), lambda e: (0, 0, 0, 0)),
            pl.BlockSpec((1, size, size), lambda e: (e, 0, 0)),
            smem, smem, smem,
        ],
        out_specs=(
            pl.BlockSpec((1, n_time, size, size), lambda e: (e, 0, 0, 0)),
            pl.BlockSpec((1, n_tm, width), lambda e: (e, 0, 0)),
        ),
        scratch_shapes=[
            pltpu.VMEM((size, n_tm * width), bf16),
            pltpu.VMEM((n_time, size, n_tm * width), bf16),
            pltpu.VMEM((8, n_tm * width), jnp.float32),
        ],
        compiler_params=pltpu.CompilerParams(vmem_limit_bytes=48 * 1024 * 1024),
    )(a_all, g_all, e_all, coulomb[0], cosine, tau_grid, my_owned)

    self_energy = pl.pallas_call(
        functools.partial(return_kernel, n_tm, n_pair, own),
        out_shape=jax.ShapeDtypeStruct((blocks, width), jnp.float32),
        in_specs=[smem, vmem, vmem],
        out_specs=vmem,
        scratch_shapes=[
            pltpu.VMEM((n_tm, 8, width), jnp.float32),
            pltpu.VMEM((n_tm, 8, width), jnp.float32),
            pltpu.VMEM((CAP * n_pair, width // LINE, LINE), jnp.float32),
            pltpu.VMEM((CAP * n_pair, width // LINE, LINE), jnp.float32),
            DMA((2,)),
            DMA((2,)),
        ],
        compiler_params=pltpu.CompilerParams(collective_id=1, has_side_effects=True),
    )(back, contrib, given)
    return (screened[None], self_energy)


def solution(mesh):
    return jax.shard_map(
        functools.partial(body, mesh.shape["tm"], mesh.shape["pair"]),
        mesh=mesh,
        in_specs=(
            P("pair", None, "tm"),
            P("pair", "tm"),
            P("pair", "tm", None, None),
            P(),
            P(),
            P(),
        ),
        out_specs=(P("pair", "tm", None, None, None), P("pair", "tm")),
        check_vma=False,
    )
```
